32 devices in a mesh: dp: 32 (over z, y, x, core).
Axes of the slice: x: 2, y: 2, z: 4, core: 2. Of those that a mesh axis runs over, the one named last changes fastest.
Arguments:
- layer_in: bfloat16 [4096, 1024], P('dp'), may hold values from -6 to 6
- cotangent: bfloat16 [4096, 1024], P('dp'), may hold values from -6 to 6
- doc_positions: int32 [4096], P('dp'), may hold values from 0 to 2047, as said below
- norm_gain: bfloat16 [1024], P('dp'), may hold values from 0.5 to 1.5
- in_proj: bfloat16 [1024, 3352], P('dp'), may hold values from -0.1875 to 0.1875
- w_query: bfloat16 [1024, 512], P('dp'), may hold values from -0.1875 to 0.1875
- w_key: bfloat16 [1024, 128], P('dp'), may hold values from -0.1875 to 0.1875
- w_value: bfloat16 [1024, 128], P('dp'), may hold values from -0.1875 to 0.1875
- out_proj: bfloat16 [1536, 1024], P(None, 'dp'), may hold values from -0.15625 to 0.15625
- w_attn_out: bfloat16 [512, 1024], P(None, 'dp'), may hold values from -0.75 to 0.75
- ffn_gain: bfloat16 [1024], P('dp'), may hold values from 0.5 to 1.5
- w_gate: bfloat16 [1024, 2048], P('dp'), may hold values from -0.1875 to 0.1875
- w_up: bfloat16 [1024, 2048], P('dp'), may hold values from -0.1875 to 0.1875
- w_down: bfloat16 [2048, 1024], P(None, 'dp'), may hold values from -0.125 to 0.125
- conv_weight: float32 [4, 1792], replicated, may hold values from -3 to 3
- conv_bias: float32 [1792], replicated, may hold values from -3 to 3
- a_log: float32 [24], replicated, may hold values from -7 to 1
- dt_bias: float32 [24], replicated, may hold values from -5 to -2
- d_skip: float32 [24], replicated, may hold values from 0.5 to 1.5
Outputs:
- layer_out: bfloat16 [4096, 1024], P('dp')
- grad_in: float32 [4096, 1024], P('dp')
- grad_norm_gain: float32 [1024], P('dp')
- grad_in_proj: float32 [1024, 3352], P('dp')
- grad_query: float32 [1024, 512], P('dp')
- grad_key: float32 [1024, 128], P('dp')
- grad_value: float32 [1024, 128], P('dp')
- grad_out_proj: float32 [1536, 1024], P(None, 'dp')
- grad_attn_out: float32 [512, 1024], P(None, 'dp')
- grad_ffn_gain: float32 [1024], P('dp')
- grad_gate: float32 [1024, 2048], P('dp')
- grad_up: float32 [1024, 2048], P('dp')
- grad_down: float32 [2048, 1024], P(None, 'dp')
- grad_conv_weight: float32 [4, 1792], replicated
- grad_conv_bias: float32 [1792], replicated
- grad_a_log: float32 [24], replicated
- grad_dt_bias: float32 [24], replicated
- grad_d_skip: float32 [24], replicated
The draws below stay inside these ranges and needn't reach their ends.
Inputs may be any that keep to these rules, and one draw needn't show every extreme that they name: `doc_positions`: positions count 0, 1, 2, ... along each document. Documents never cross a boundary of the aligned spans of 2048 tokens, and each such span holds one or two documents of 256 to 2048 tokens; in every draw some span is a single document of 2048 tokens.
All inputs are finite; a program needn't handle non-finite values.
Results may differ from the reference program's by a relative error of at most 0.017.
Values may be sent and summed in bfloat16 or wider, within the bound.
No kernel may reach another device: no remote copies, remote signals or barrier semaphores. Data moves between devices by JAX's collectives and lax.ppermute only.
A program may use at most 256 MiB of HBM per device.

```python
import jax
import jax.numpy as jnp
from jax import lax

D = 1024
MH = 24
HD = 64
NST = 128
KCONV = 4
AH = 8
KVH = 2
FF = 2048
SCAN_BLOCK = 128
DI = 1536
CONVCH = 1792
PROJ = 3352
SEQ = 2048
TOKENS = 4096


def draw_doc_positions(key, part):
    key = jax.random.fold_in(key, 11)
    cut_key, whole_key = jax.random.split(key)
    seq_count = TOKENS // SEQ
    cuts = jax.random.randint(cut_key, (seq_count,), SEQ // 8, SEQ - SEQ // 8 + 1)
    whole_one = jax.random.randint(whole_key, (), 0, seq_count)
    cuts = jnp.where(jnp.arange(seq_count) == whole_one, SEQ, cuts)
    within = jnp.arange(SEQ)[None, :]
    positions = jnp.where(within < cuts[:, None], within, within - cuts[:, None])
    return positions.reshape(-1).astype(jnp.int32)


def block_scale(rng, dims, cuts, low, largest):
    factor_of = 1.0
    for position, blocks in cuts:
        draws = jax.random.uniform(jax.random.fold_in(jax.random.fold_in(rng, 6), position), (blocks,), jnp.float32, low / len(cuts), largest / len(cuts))
        factor_of = factor_of * jnp.repeat(jnp.exp(draws), dims[position] // blocks).reshape((-1,) + (1,) * (len(dims) - 1 - position))
    return factor_of


def gaussian(stream_key, dims, scale, reach, shards=(), kind=jnp.bfloat16):
    level = block_scale(stream_key, dims, shards, -0.22, 0.18) if shards else 1.0
    values = jax.random.normal(stream_key, dims, jnp.float32) * scale * level
    return jnp.minimum(jnp.maximum(values, -reach), reach).astype(kind)


def setup_inputs(seed: int = 0) -> dict:
    key_of = jax.random.split(jax.random.key(seed), 20)
    return {
        "layer_in": gaussian(key_of[0], (TOKENS, D), 1.0, 6.0, ((0, 32),)),
        "cotangent": gaussian(key_of[1], (TOKENS, D), 1.0, 6.0, ((0, 32),)),
        "doc_positions": draw_doc_positions(jax.random.fold_in(key_of[19], 71), 0),
        "norm_gain": jnp.clip(1.0 + 0.1 * jax.random.normal(key_of[3], (D,), jnp.float32), 0.5, 1.5).astype(jnp.bfloat16),
        "in_proj": gaussian(key_of[4], (D, PROJ), D ** -0.5, 0.1875, ((0, 32),)),
        "w_query": gaussian(key_of[5], (D, AH * HD), D ** -0.5, 0.1875, ((0, 32),)),
        "w_key": gaussian(key_of[6], (D, KVH * HD), D ** -0.5, 0.1875, ((0, 32),)),
        "w_value": gaussian(key_of[7], (D, KVH * HD), D ** -0.5, 0.1875, ((0, 32),)),
        "out_proj": gaussian(key_of[8], (DI, D), DI ** -0.5, 0.15625, ((1, 32),)),
        "w_attn_out": gaussian(key_of[9], (AH * HD, D), (AH * HD // 8) ** -0.5, 0.75, ((1, 32),)),
        "ffn_gain": jnp.clip(1.0 + 0.1 * jax.random.normal(key_of[10], (D,), jnp.float32), 0.5, 1.5).astype(jnp.bfloat16),
        "w_gate": gaussian(key_of[11], (D, FF), D ** -0.5, 0.1875, ((0, 32),)),
        "w_up": gaussian(key_of[12], (D, FF), D ** -0.5, 0.1875, ((0, 32),)),
        "w_down": gaussian(key_of[13], (FF, D), FF ** -0.5, 0.125, ((1, 32),)),
        "conv_weight": gaussian(key_of[14], (KCONV, CONVCH), KCONV ** -0.5, 3.0, (), jnp.float32),
        "conv_bias": gaussian(key_of[15], (CONVCH,), 0.5, 3.0, (), jnp.float32),
        "a_log": jnp.clip(jax.random.uniform(key_of[16], (MH,), jnp.float32, -7.0, 1.0), -7.0, 1.0),
        "dt_bias": jnp.clip(jax.random.uniform(key_of[17], (MH,), jnp.float32, -5.0, -2.0), -5.0, -2.0),
        "d_skip": jnp.clip(jax.random.uniform(key_of[18], (MH,), jnp.float32, 0.5, 1.5), 0.5, 1.5),
    }


@jax.custom_vjp
def low(v):
    return lax.optimization_barrier(v.astype(jnp.bfloat16)).astype(jnp.float32)

@jax.custom_vjp
def low_back(v):
    return v

def low_keep(v):
    return (low(v), None)

def low_pass(kept, grad):
    return (grad,)

def back_keep(v):
    return (v, None)

def back_low(kept, grad):
    return (low(grad),)
low.defvjp(low_keep, low_pass)
low_back.defvjp(back_keep, back_low)
EPS = 1e-05
ROPE_BASE = 10000.0

def matmul_high(first_arg, second_arg):
    return jnp.dot(first_arg, second_arg, precision=lax.Precision.HIGHEST, preferred_element_type=jnp.float32)

def rms_scale(values, gain_vec):
    return values * lax.rsqrt(lax.optimization_barrier(jnp.mean(values * values, axis=-1, keepdims=True)) + EPS) * gain_vec

def rotate(values, positions):
    half_dim = values.shape[-1] // 2
    frequency = ROPE_BASE ** (-jnp.arange(half_dim, dtype=jnp.float32) / half_dim)
    angles = positions.astype(jnp.float32)[:, None] * frequency[None, :]
    cosine = jnp.cos(angles)[:, None, :]
    sine_vals = jnp.sin(angles)[:, None, :]
    first_half = values[..., :half_dim]
    second_half = values[..., half_dim:]
    return jnp.concatenate([first_half * cosine - second_half * sine_vals, second_half * cosine + first_half * sine_vals], axis=-1)

def causal_conv(padded, conv_weight, conv_bias, positions):
    token_count = padded.shape[0] - (KCONV - 1)
    conv_sum = jnp.zeros((token_count, padded.shape[1]), jnp.float32) + conv_bias[None, :]
    for tap_index in range(KCONV):
        lag_rows = KCONV - 1 - tap_index
        shifted = padded[tap_index:tap_index + token_count] * conv_weight[tap_index][None, :]
        conv_sum = conv_sum + jnp.where((positions >= lag_rows)[:, None], shifted, 0.0)
    return jax.nn.silu(conv_sum)

def scan_blocks(inputs, b_rows, c_rows, step_sizes, log_decay, positions, state_in):
    token_count = inputs.shape[0]
    block_count = token_count // SCAN_BLOCK
    highest = lax.Precision.HIGHEST

    def one_block(state_carry, pieces):
        in_rows, b_part, c_part, step_part, decay_part, pos_part = pieces
        cumulative = jnp.cumsum(decay_part, axis=0)
        row_index = jnp.arange(SCAN_BLOCK)
        doc_start = row_index - pos_part
        inside = (row_index[None, :] <= row_index[:, None]) & (row_index[None, :] >= doc_start[:, None])
        log_gap = jnp.where(inside[None], cumulative.T[:, :, None] - cumulative.T[:, None, :], -1e+30)
        inner_sums = matmul_high(c_part, b_part.T)
        mixed = jnp.exp(log_gap) * inner_sums[None] * step_part.T[:, None, :]
        local_out = jnp.einsum('hij,jhp->ihp', mixed, in_rows, precision=highest)
        carried = jnp.where((pos_part > row_index)[:, None], jnp.exp(cumulative), 0.0)
        before = jnp.einsum('in,hpn->ihp', c_part, state_carry, precision=highest) * carried[:, :, None]
        last_row = SCAN_BLOCK - 1
        tail_mask = jnp.where(row_index >= last_row - pos_part[last_row], 1.0, 0.0)
        fade_weights = jnp.exp(cumulative[last_row][None, :] - cumulative) * tail_mask[:, None] * step_part
        fresh_state = jnp.einsum('jh,jhp,jn->hpn', fade_weights, in_rows, b_part, precision=highest)
        keep_rate = jnp.where(pos_part[last_row] > last_row, jnp.exp(cumulative[last_row]), 0.0)
        return (keep_rate[:, None, None] * state_carry + fresh_state, local_out + before)
    pieces = (inputs.reshape(block_count, SCAN_BLOCK, MH, HD), b_rows.reshape(block_count, SCAN_BLOCK, NST), c_rows.reshape(block_count, SCAN_BLOCK, NST), step_sizes.reshape(block_count, SCAN_BLOCK, MH), log_decay.reshape(block_count, SCAN_BLOCK, MH), positions.reshape(block_count, SCAN_BLOCK))
    final_state, outputs = lax.scan(jax.checkpoint(one_block), state_in, pieces)
    return (outputs.reshape(token_count, MH, HD), final_state)

def attend_sequence(pieces):
    query, key_rows, value_rows, positions = pieces
    length = query.shape[0]
    group_size = AH // KVH
    grouped = query.reshape(length, KVH, group_size, HD)
    scores = jnp.einsum('sgjd,tgd->gjst', grouped, key_rows, precision=lax.Precision.HIGHEST) * HD ** (-0.5)
    scores = low_back(scores)
    row_index = jnp.arange(length)
    visible = (row_index[None, :] <= row_index[:, None]) & (row_index[None, :] >= (row_index - positions)[:, None])
    scores = jnp.where(visible, scores, -1e+30)
    totals = jax.nn.logsumexp(scores, axis=-1, keepdims=True)
    probabilities = low(jnp.exp(scores - totals))
    attended = jnp.einsum('gjst,tgd->sgjd', probabilities, value_rows, precision=lax.Precision.HIGHEST)
    return attended.reshape(length, AH * HD)

def layer(residual_in, norm_gain, in_proj, w_query, w_key, w_value, out_proj, w_attn_out, ffn_gain, w_gate, w_up, w_down, conv_weight, conv_bias, a_log, dt_bias, d_skip, positions):
    token_count = residual_in.shape[0]
    normed = low(rms_scale(residual_in, norm_gain))
    projected = low_back(matmul_high(normed, in_proj))
    gate_z = projected[:, :DI]
    conv_in = low(projected[:, DI:DI + CONVCH])
    dt_raw = projected[:, DI + CONVCH:]
    padded = jnp.concatenate([jnp.zeros((KCONV - 1, CONVCH), jnp.float32), conv_in], axis=0)
    conv_out = causal_conv(padded, conv_weight, conv_bias, positions)
    inputs = conv_out[:, :DI].reshape(token_count, MH, HD)
    b_rows = conv_out[:, DI:DI + NST]
    c_rows = conv_out[:, DI + NST:]
    step_sizes = jax.nn.softplus(dt_raw + dt_bias)
    log_decay = -step_sizes * jnp.exp(a_log)
    scanned, _ = scan_blocks(inputs, b_rows, c_rows, step_sizes, log_decay, positions, jnp.zeros((MH, HD, NST), jnp.float32))
    ssm_out = scanned + d_skip[None, :, None] * inputs
    gated = low(ssm_out.reshape(token_count, DI) * jax.nn.silu(gate_z))
    mamba_branch = low_back(matmul_high(gated, out_proj))
    query = low(rotate(low_back(matmul_high(normed, w_query)).reshape(token_count, AH, HD), positions))
    keys = low(rotate(low_back(matmul_high(normed, w_key)).reshape(token_count, KVH, HD), positions))
    values = low(low_back(matmul_high(normed, w_value))).reshape(token_count, KVH, HD)
    seq_count = token_count // SEQ
    attended = lax.map(jax.checkpoint(attend_sequence), (query.reshape(seq_count, SEQ, AH, HD), keys.reshape(seq_count, SEQ, KVH, HD), values.reshape(seq_count, SEQ, KVH, HD), positions.reshape(seq_count, SEQ)))
    attended = low(low_back(attended.reshape(token_count, AH * HD)))
    attn_branch = low_back(matmul_high(attended, w_attn_out))
    middle = residual_in + mamba_branch + attn_branch
    normed_two = low(rms_scale(middle, ffn_gain))
    gate_value = low_back(matmul_high(normed_two, w_gate))
    up_value = low_back(matmul_high(normed_two, w_up))
    hidden = low(jax.nn.silu(gate_value) * up_value)
    return middle + low_back(matmul_high(hidden, w_down))

def reference(layer_in, cotangent, doc_positions, norm_gain, in_proj, w_query, w_key, w_value, out_proj, w_attn_out, ffn_gain, w_gate, w_up, w_down, conv_weight, conv_bias, a_log, dt_bias, d_skip):
    floats = tuple((item.astype(jnp.float32) for item in (layer_in, norm_gain, in_proj, w_query, w_key, w_value, out_proj, w_attn_out, ffn_gain, w_gate, w_up, w_down)))

    def forward(*params):
        return layer(*params, doc_positions)
    result, pullback = jax.vjp(forward, *floats, conv_weight, conv_bias, a_log, dt_bias, d_skip)
    grads = pullback(cotangent.astype(jnp.float32))
    return (result.astype(jnp.bfloat16), grads[0], grads[1], grads[2], grads[3], grads[4], grads[5], grads[6], grads[7], grads[8], grads[9], grads[10], grads[11], grads[12], grads[13], grads[14], grads[15], grads[16])
```

```python
import jax
import jax.numpy as jnp
from jax import lax
from jax.sharding import PartitionSpec as P

D = 1024
MH = 24
HD = 64
NST = 128
KCONV = 4
AH = 8
KVH = 2
FF = 2048
CHUNK = 128
DI = 1536
CONVCH = 1792
SEQ = 2048

EPS = 1e-05
ROPE_BASE = 10000.0

TEAM = 4
BITS = TEAM.bit_length() - 1
HEADS = MH // TEAM
CX = HEADS * HD
QH = AH // TEAM
CQ = QH * HD
CF = FF // TEAM
SHARE = TEAM // KVH
CB = 2 * NST // TEAM

F32 = jnp.float32
BF16 = jnp.bfloat16


def product(first_arg, second_arg):
    return jnp.dot(first_arg, second_arg, preferred_element_type=F32)


def times_transposed(first_arg, second_arg):
    return lax.dot_general(
        first_arg, second_arg, (((1,), (1,)), ((), ())), preferred_element_type=F32
    )


def transposed_times(first_arg, second_arg):
    return lax.dot_general(
        first_arg, second_arg, (((0,), (0,)), ((), ())), preferred_element_type=F32
    )


def device_index():
    return lax.axis_index("dp")


def member():
    return device_index() % TEAM


def member_bit(bit):
    return (device_index() >> bit) & 1


def peer(value, distance):
    count = lax.axis_size("dp")
    return lax.ppermute(value, "dp", [(i, i ^ distance) for i in range(count)])


def shift_teams(value, steps):
    count = lax.axis_size("dp")
    offset = steps * TEAM
    first, last = (max(0, -offset), min(count, count - offset))
    return lax.ppermute(value, "dp", [(i, i + offset) for i in range(first, last)])


def team_gather(value):
    blocks = value[None]
    for bit in reversed(range(BITS)):
        other = peer(blocks, 1 << bit)
        blocks = jnp.where(
            member_bit(bit) == 0,
            jnp.stack([blocks, other], axis=1),
            jnp.stack([other, blocks], axis=1),
        )
        blocks = blocks.reshape((-1,) + value.shape)
    return blocks.reshape((-1,) + value.shape[1:])


def team_scatter(partial):
    blocks = partial.reshape((TEAM, -1) + partial.shape[1:])
    for bit in range(BITS):
        mine = member_bit(bit)
        halves = blocks.reshape((-1, 2) + blocks.shape[1:])
        kept = lax.dynamic_index_in_dim(halves, mine, 1, False)
        sent = lax.dynamic_index_in_dim(halves, 1 - mine, 1, False)
        blocks = kept.astype(F32) + peer(sent.astype(BF16), 1 << bit).astype(F32)
    return blocks[0]


def member_order(pieces):
    for bit in range(BITS):
        split = pieces.reshape((TEAM >> (bit + 1), 2, 1 << bit) + pieces.shape[1:])
        flipped = jnp.concatenate([split[:, 1:], split[:, :1]], axis=1)
        pieces = jnp.where(member_bit(bit) == 0, split, flipped).reshape(pieces.shape)
    return pieces


def team_exchange(pieces):
    relative = member_order(pieces)
    arrived = [relative[0]] + [peer(relative[k], k) for k in range(1, TEAM)]
    return member_order(jnp.stack(arrived))


def across_groups():
    count = lax.axis_size("dp")
    return [list(range(first, count, TEAM)) for first in range(TEAM)]


def gather_rows(pieces):
    rows = team_exchange(pieces)
    rows = rows.reshape((-1, rows.shape[-1]))
    return lax.all_gather(rows, "dp", axis=0, tiled=True, axis_index_groups=across_groups())


def scatter_rows(matrix):
    summed = lax.psum_scatter(
        matrix, "dp", scatter_dimension=0, tiled=True, axis_index_groups=across_groups()
    )
    return team_exchange(summed.reshape(TEAM, -1, summed.shape[-1]))


def sum_across_teams(vector):
    count = lax.axis_size("dp")
    distance = TEAM
    while distance < count:
        vector = vector + peer(vector, distance)
        distance *= 2
    return vector


def columns_of(matrix, index, width):
    return lax.slice_in_dim(matrix, index * width, (index + 1) * width, axis=1)


def my_slice(array, width, axis=-1):
    axis = axis % array.ndim
    return lax.dynamic_slice_in_dim(array, member() * width, width, axis)


def rotate(values, cosine, sine_vals):
    half_dim = HD // 2
    rows = values.shape[0]
    heads = values.reshape(rows, -1, HD)
    first_half = heads[..., :half_dim]
    second_half = heads[..., half_dim:]
    cosine = cosine[:, None, :]
    sine_vals = sine_vals[:, None, :]
    return jnp.concatenate(
        [
            first_half * cosine - second_half * sine_vals,
            second_half * cosine + first_half * sine_vals,
        ],
        axis=-1,
    ).reshape(values.shape)


def causal_conv(padded, conv_weight, conv_bias, positions):
    token_count = padded.shape[0] - (KCONV - 1)
    conv_sum = jnp.zeros((token_count, padded.shape[1]), F32) + conv_bias[None, :]
    for tap_index in range(KCONV):
        lag_rows = KCONV - 1 - tap_index
        shifted = padded[tap_index : tap_index + token_count] * conv_weight[tap_index][None, :]
        conv_sum = conv_sum + jnp.where((positions >= lag_rows)[:, None], shifted, 0.0)
    return jax.nn.silu(conv_sum)


def ssm_core(inputs, b_rows, c_rows, step_sizes, log_decay, state_in, positions):
    token_count = inputs.shape[0]
    blocks = token_count // CHUNK
    high = lax.Precision.HIGH
    in_rows = inputs.reshape(blocks, CHUNK, HEADS, HD)
    b_part = b_rows.reshape(blocks, CHUNK, NST)
    c_part = c_rows.reshape(blocks, CHUNK, NST)
    step_part = step_sizes.reshape(blocks, CHUNK, HEADS)
    pos_part = positions.reshape(blocks, CHUNK)
    cumulative = jnp.cumsum(log_decay.reshape(blocks, CHUNK, HEADS), axis=1)
    row_index = jnp.arange(CHUNK)
    doc_start = row_index[None, :] - pos_part
    inside = (row_index[None, None, :] <= row_index[None, :, None]) & (
        row_index[None, None, :] >= doc_start[:, :, None]
    )
    by_head = cumulative.transpose(0, 2, 1)
    log_gap = jnp.where(inside[:, None], by_head[:, :, :, None] - by_head[:, :, None, :], -1e30)
    inner_sums = jnp.einsum("cin,cjn->cij", c_part, b_part, precision=high)
    mixed = jnp.exp(log_gap) * inner_sums[:, None] * step_part.transpose(0, 2, 1)[:, :, None, :]
    local_out = jnp.einsum("chij,cjhp->cihp", mixed, in_rows, precision=high)
    last_row = CHUNK - 1
    tail_mask = jnp.where(row_index[None, :] >= last_row - pos_part[:, last_row:], 1.0, 0.0)
    fade_weights = (
        jnp.exp(cumulative[:, last_row:] - cumulative) * tail_mask[:, :, None] * step_part
    )
    fresh = jnp.einsum(
        "cjhp,cjn->chpn", in_rows * fade_weights[..., None], b_part, precision=high
    )
    keep_rate = jnp.where(
        pos_part[:, last_row:] > last_row, jnp.exp(cumulative[:, last_row]), 0.0
    )
    entering = []
    state = state_in
    for block in range(blocks):
        entering.append(state)
        state = keep_rate[block][:, None, None] * state + fresh[block]
    carried = jnp.where(
        (pos_part > row_index[None, :])[:, :, None], jnp.exp(cumulative), 0.0
    )
    before = jnp.einsum("cin,chpn->cihp", c_part, jnp.stack(entering), precision=high)
    outputs = local_out + before * carried[..., None]
    return outputs.reshape(token_count, CX), state


def combine_states(own, rate, steps, reach):
    flat = jnp.concatenate([own.reshape(-1, NST), jnp.broadcast_to(rate[0], (8, NST)),
                            jnp.broadcast_to(rate[1], (8, NST))], axis=0).astype(BF16)
    total = None
    through = None
    for distance in range(1, reach + 1):
        arrived = shift_teams(flat, steps * distance).astype(F32)
        state = arrived[:CX].reshape(HEADS, HD, NST)
        their_rate = (arrived[CX, :HEADS] + arrived[CX + 8, :HEADS])[:, None, None]
        if total is None:
            total, through = state, their_rate
        else:
            total = total + through * state
            through = through * their_rate
    return total


def packed_rate(rate):
    wide = jnp.zeros((NST,), F32).at[:HEADS].set(rate)
    coarse = wide.astype(BF16).astype(F32)
    return coarse, wide - coarse


def masked_scores(query_low, key_low, positions):
    row_count = query_low.shape[0]
    span_rows = key_low.shape[0]
    grouped = query_low.reshape(row_count, QH, HD)
    scores = jnp.einsum("sjd,td->jst", grouped, key_low, preferred_element_type=F32) * HD ** (-0.5)
    q_index = span_rows - row_count + jnp.arange(row_count)
    k_index = jnp.arange(span_rows)
    visible = (k_index[None, :] <= q_index[:, None]) & (
        k_index[None, :] >= (q_index - positions)[:, None]
    )
    return jnp.where(visible, scores, -1e30), grouped


def attend_forward(query_low, key_low, value_low, positions):
    scores, _ = masked_scores(query_low, key_low, positions)
    totals = jax.nn.logsumexp(scores, axis=-1, keepdims=True)
    weights_low = jnp.exp(scores - totals).astype(BF16)
    attended = jnp.einsum("jst,td->sjd", weights_low, value_low, preferred_element_type=F32)
    return attended.reshape(query_low.shape[0], CQ), totals


def attend_backward(query_low, key_low, value_low, positions, totals, grad_attended_low):
    scores, grouped = masked_scores(query_low, key_low, positions)
    row_count = query_low.shape[0]
    weights_full = jnp.exp(scores - totals)
    weights_low = weights_full.astype(BF16)
    grad_grouped = grad_attended_low.reshape(row_count, QH, HD)
    grad_weights = jnp.einsum(
        "sjd,td->jst", grad_grouped, value_low, preferred_element_type=F32
    )
    row_sums = jnp.sum(weights_full * grad_weights, axis=-1, keepdims=True)
    grad_scores = (weights_full * (grad_weights - row_sums)).astype(BF16)
    scale = HD ** (-0.5)
    grad_query = jnp.einsum("jst,td->sjd", grad_scores, key_low, preferred_element_type=F32) * scale
    grad_keys = jnp.einsum("jst,sjd->td", grad_scores, grouped, preferred_element_type=F32) * scale
    grad_values = jnp.einsum("jst,sjd->td", weights_low, grad_grouped, preferred_element_type=F32)
    return grad_query.reshape(row_count, CQ), jnp.concatenate([grad_keys, grad_values], axis=1)


def silu_slope(value):
    chance = jax.nn.sigmoid(value)
    return chance * (1.0 + value * (1.0 - chance))


def body(
    layer_in,
    cotangent,
    doc_positions,
    norm_gain,
    in_proj,
    w_query,
    w_key,
    w_value,
    out_proj,
    w_attn_out,
    ffn_gain,
    w_gate,
    w_up,
    w_down,
    conv_weight,
    conv_bias,
    a_log,
    dt_bias,
    d_skip,
):
    me = member()
    kv_mine = me // SHARE
    bc_cols = in_proj[:, 2 * DI : 2 * DI + 2 * NST]
    dt_cols = in_proj[:, DI + CONVCH :]
    first_pieces = jnp.stack(
        [
            jnp.concatenate(
                [
                    columns_of(in_proj[:, :DI], r, CX),
                    columns_of(in_proj[:, DI : 2 * DI], r, CX),
                    bc_cols,
                    columns_of(w_query, r, CQ),
                    columns_of(w_key, r // SHARE, HD),
                    columns_of(w_value, r // SHARE, HD),
                    columns_of(dt_cols, r, HEADS),
                    norm_gain[:, None],
                ],
                axis=1,
            )
            for r in range(TEAM)
        ]
    )
    out_rows = out_proj.T
    attn_rows = w_attn_out.T
    down_rows = w_down.T
    second_pieces = jnp.stack(
        [
            jnp.concatenate(
                [
                    columns_of(out_rows, r, CX),
                    columns_of(attn_rows, r, CQ),
                    columns_of(w_gate, r, CF),
                    columns_of(w_up, r, CF),
                    columns_of(down_rows, r, CF),
                    ffn_gain[:, None],
                ],
                axis=1,
            )
            for r in range(TEAM)
        ]
    )
    rows_one = gather_rows(first_pieces)
    rows_two = gather_rows(second_pieces)
    team_in = team_gather(layer_in)
    positions = team_gather(doc_positions)
    team_top = team_gather(cotangent)

    z_end = CX
    x_end = 2 * CX
    bc_end = x_end + 2 * NST
    q_end = bc_end + CQ
    kv_end = q_end + 2 * HD
    dt_end = kv_end + HEADS
    main_one = rows_one[:, :dt_end]
    gain_one = rows_one[:, dt_end].astype(F32)
    mix_weights = rows_two[:, : CX + CQ]
    ffn_weights = rows_two[:, CX + CQ : CX + CQ + 2 * CF]
    down_weights = rows_two[:, CX + CQ + 2 * CF : CX + CQ + 3 * CF]
    gain_two = rows_two[:, CX + CQ + 3 * CF].astype(F32)

    tokens = team_in.shape[0]
    row_count = layer_in.shape[0]
    reach = SEQ // tokens - 1
    last = tokens - 1

    wide_in = team_in.astype(F32)
    scaled_in = wide_in * lax.rsqrt(jnp.mean(wide_in * wide_in, axis=-1, keepdims=True) + EPS)
    normed_low = (scaled_in * gain_one).astype(BF16)
    projected = product(normed_low, main_one)

    half_dim = HD // 2
    frequency = ROPE_BASE ** (-jnp.arange(half_dim, dtype=F32) / half_dim)
    angles = positions.astype(F32)[:, None] * frequency[None, :]
    cosine = jnp.cos(angles)
    sine_vals = jnp.sin(angles)

    gate_z = projected[:, :z_end]
    conv_low = projected[:, z_end:bc_end].astype(BF16)
    rim_rows = shift_teams(conv_low[tokens - (KCONV - 1) :], 1)
    query_low = rotate(projected[:, bc_end:q_end], cosine, sine_vals).astype(BF16)
    key_low = rotate(projected[:, q_end : q_end + HD], cosine, sine_vals).astype(BF16)
    value_low = projected[:, q_end + HD : kv_end].astype(BF16)
    dt_raw = projected[:, kv_end:dt_end]
    own_window = jnp.concatenate([key_low, value_low], axis=1)
    window = jnp.concatenate(
        [shift_teams(own_window, steps) for steps in range(reach, 0, -1)] + [own_window], axis=0
    )
    key_window = window[:, :HD]
    value_window = window[:, HD:]

    taps_x = my_slice(conv_weight[:, :DI], CX)
    bias_x = my_slice(conv_bias[:DI], CX)
    taps = jnp.concatenate([taps_x, conv_weight[:, DI:]], axis=1)
    bias = jnp.concatenate([bias_x, conv_bias[DI:]], axis=0)
    my_log_rates = my_slice(a_log, HEADS)
    my_dt_bias = my_slice(dt_bias, HEADS)
    my_skip = my_slice(d_skip, HEADS)
    skip_wide = jnp.repeat(my_skip, HD)

    padded = jnp.concatenate([rim_rows, conv_low], axis=0).astype(F32)
    conv_out = causal_conv(padded, taps, bias, positions)
    inputs = conv_out[:, :CX]
    b_rows = conv_out[:, CX : CX + NST]
    c_rows = conv_out[:, CX + NST :]

    def decays(raw_steps, step_bias, log_rates):
        step_sizes = jax.nn.softplus(raw_steps + step_bias)
        return step_sizes, -step_sizes * jnp.exp(log_rates)

    (step_sizes, log_decay), decays_back = jax.vjp(decays, dt_raw, my_dt_bias, my_log_rates)
    cumulative = jnp.cumsum(log_decay, axis=0)
    row_index = jnp.arange(tokens)
    tail_mask = jnp.where(row_index >= last - positions[last], 1.0, 0.0)
    fade_weights = jnp.exp(cumulative[last][None, :] - cumulative) * tail_mask[:, None] * step_sizes
    local_state = transposed_times(inputs * jnp.repeat(fade_weights, HD, axis=1), b_rows)
    through = jnp.where(positions[last] > last, jnp.exp(cumulative[last]), 0.0)
    rates = packed_rate(through)
    state_in = combine_states(local_state.reshape(HEADS, HD, NST), rates, 1, reach)

    attended, totals = attend_forward(query_low, key_window, value_window, positions)
    attended_low = attended.astype(BF16)

    def core(in_rows, b_part, c_part, step_part, decay_part):
        return ssm_core(in_rows, b_part, c_part, step_part, decay_part, state_in, positions)

    (scanned, _), core_back = jax.vjp(core, inputs, b_rows, c_rows, step_sizes, log_decay)
    ssm_out = scanned + skip_wide * inputs
    silu_z = jax.nn.silu(gate_z)
    gated_low = (ssm_out * silu_z).astype(BF16)
    mixed_low = jnp.concatenate([gated_low, attended_low], axis=1)
    branches = team_scatter(times_transposed(mixed_low, mix_weights))
    middle = layer_in.astype(F32) + branches
    inverse_two = lax.rsqrt(jnp.mean(middle * middle, axis=-1, keepdims=True) + EPS)
    scaled_two = middle * inverse_two
    normed_two = team_gather((scaled_two * gain_two).astype(BF16))
    gate_up = product(normed_two, ffn_weights)
    gate_value = gate_up[:, :CF]
    up_value = gate_up[:, CF:]
    silu_gate = jax.nn.silu(gate_value)
    hidden_low = (silu_gate * up_value).astype(BF16)
    layer_out = (middle + team_scatter(times_transposed(hidden_low, down_weights))).astype(BF16)

    grad_hidden = product(team_top, down_weights)
    grad_gate_up = jnp.concatenate(
        [grad_hidden * up_value * silu_slope(gate_value), grad_hidden * silu_gate], axis=1
    ).astype(BF16)
    grad_normed_two = team_scatter(times_transposed(grad_gate_up, ffn_weights))
    ffn_sums = jnp.concatenate(
        [transposed_times(normed_two, grad_gate_up), transposed_times(team_top, hidden_low)], axis=1
    ).astype(BF16)
    ffn_grads = scatter_rows(ffn_sums)
    grad_gain_two = jnp.sum(grad_normed_two * scaled_two, axis=0)
    pulled = grad_normed_two * gain_two
    grad_middle = cotangent.astype(F32) + inverse_two * (
        pulled - scaled_two * jnp.mean(pulled * scaled_two, axis=-1, keepdims=True)
    )
    grad_branch = team_gather(grad_middle.astype(BF16))
    grad_mixed = product(grad_branch, mix_weights)
    grad_gated = grad_mixed[:, :CX]
    grad_attended_low = grad_mixed[:, CX:].astype(BF16)
    grad_ssm = grad_gated * silu_z
    grad_z_low = (grad_gated * ssm_out * silu_slope(gate_z)).astype(BF16)

    entry_weights = jnp.where((positions > row_index)[:, None], jnp.exp(cumulative), 0.0)
    local_adjoint = transposed_times(grad_ssm * jnp.repeat(entry_weights, HD, axis=1), c_rows)
    grad_state = combine_states(local_adjoint.reshape(HEADS, HD, NST), rates, -1, reach)

    grad_query_rot, grad_window = attend_backward(
        query_low, key_window, value_window, positions, totals, grad_attended_low
    )
    own_grad = grad_window[reach * tokens :]
    for steps in range(1, reach + 1):
        part = grad_window[(reach - steps) * tokens : (reach - steps + 1) * tokens]
        own_grad = own_grad + shift_teams(part.astype(BF16), -steps).astype(F32)
    distance = 1
    while distance < SHARE:
        own_grad = own_grad + peer(own_grad, distance)
        distance *= 2
    grad_query_low = rotate(grad_query_rot, cosine, -sine_vals).astype(BF16)
    grad_key_low = rotate(own_grad[:, :HD], cosine, -sine_vals).astype(BF16)
    grad_value_low = own_grad[:, HD:].astype(BF16)

    grad_core = core_back((grad_ssm, grad_state))
    grad_inputs, grad_b, grad_c, grad_steps, grad_decay = grad_core
    grad_inputs = grad_inputs + skip_wide * grad_ssm
    grad_skip = jnp.sum((grad_ssm * inputs).reshape(tokens, HEADS, HD), axis=(0, 2))
    grad_bc = jnp.concatenate([grad_b, grad_c], axis=1).reshape(tokens, TEAM, CB)
    grad_bc = team_scatter(grad_bc.transpose(1, 0, 2).reshape(TEAM * tokens, CB))
    grad_dt_raw, grad_step_bias, grad_log_rates = decays_back((grad_steps, grad_decay))

    conv_padded = jnp.concatenate([padded[:, :CX], my_slice(padded[:, CX:], CB)], axis=1)
    conv_taps = jnp.concatenate([taps[:, :CX], my_slice(taps[:, CX:], CB)], axis=1)
    conv_shift = jnp.concatenate([bias[:CX], my_slice(bias[CX:], CB)], axis=0)
    _, conv_back = jax.vjp(
        lambda rows, weights, offset: causal_conv(rows, weights, offset, positions),
        conv_padded, conv_taps, conv_shift,
    )
    grad_padded, grad_taps, grad_shift = conv_back(
        jnp.concatenate([grad_inputs, grad_bc], axis=1)
    )
    returned_rim = shift_teams(grad_padded[: KCONV - 1], -1)
    grad_conv = grad_padded[KCONV - 1 :]
    grad_conv = jnp.concatenate(
        [grad_conv[: tokens - (KCONV - 1)], grad_conv[tokens - (KCONV - 1) :] + returned_rim],
        axis=0,
    )
    grad_conv_low = grad_conv.astype(BF16)
    grad_dt_low = grad_dt_raw.astype(BF16)

    early_low = jnp.concatenate([grad_z_low, grad_query_low, grad_key_low, grad_value_low], axis=1)
    mix_sums = jnp.concatenate(
        [
            transposed_times(grad_branch, mixed_low),
            transposed_times(normed_low, early_low),
            grad_gain_two[:, None],
        ],
        axis=1,
    ).astype(BF16)
    mix_grads = scatter_rows(mix_sums)

    shared = 1.0 / SHARE
    late_low = jnp.concatenate([grad_conv_low, grad_dt_low], axis=1)
    all_low = jnp.concatenate(
        [
            grad_z_low,
            grad_conv_low,
            grad_query_low,
            grad_key_low * BF16(shared),
            grad_value_low * BF16(shared),
            grad_dt_low,
        ],
        axis=1,
    )
    back_weights = jnp.concatenate(
        [main_one[:, :x_end], my_slice(main_one[:, x_end:bc_end], CB), main_one[:, bc_end:]], axis=1
    )
    grad_normed_part = times_transposed(all_low, back_weights)
    gain_sums = jnp.sum(grad_normed_part * scaled_in, axis=0)
    late_sums = jnp.concatenate(
        [transposed_times(normed_low, late_low), gain_sums[:, None]], axis=1
    ).astype(BF16)
    late_grads = scatter_rows(late_sums)
    grad_normed = team_scatter(grad_normed_part)
    own_in = layer_in.astype(F32)
    inverse_one = lax.rsqrt(jnp.mean(own_in * own_in, axis=-1, keepdims=True) + EPS)
    own_scaled = own_in * inverse_one
    pulled_one = grad_normed * gain_one
    grad_in = grad_middle + inverse_one * (
        pulled_one - own_scaled * jnp.mean(pulled_one * own_scaled, axis=-1, keepdims=True)
    )

    small = jnp.concatenate(
        [grad_taps.reshape(-1), grad_shift, grad_log_rates, grad_step_bias, grad_skip]
    )
    small = team_gather(sum_across_teams(small)[None])
    width = CX + CB
    taps_all = small[:, : KCONV * width].reshape(TEAM, KCONV, width)
    shift_all = small[:, KCONV * width : (KCONV + 1) * width]
    rest = small[:, (KCONV + 1) * width :].reshape(TEAM, 3, HEADS)
    grad_conv_weight = jnp.concatenate(
        [
            taps_all[:, :, :CX].transpose(1, 0, 2).reshape(KCONV, DI),
            taps_all[:, :, CX:].transpose(1, 0, 2).reshape(KCONV, 2 * NST),
        ],
        axis=1,
    )
    grad_conv_bias = jnp.concatenate([shift_all[:, :CX].reshape(-1), shift_all[:, CX:].reshape(-1)])
    grad_a_log = rest[:, 0].reshape(-1)
    grad_dt_bias = rest[:, 1].reshape(-1)
    grad_d_skip = rest[:, 2].reshape(-1)

    def joined(pieces, first, stop, members=range(TEAM)):
        return jnp.concatenate([pieces[r, :, first:stop] for r in members], axis=1).astype(F32)

    grad_gate = joined(ffn_grads, 0, CF)
    grad_up = joined(ffn_grads, CF, 2 * CF)
    grad_down = joined(ffn_grads, 2 * CF, 3 * CF).T
    grad_out_proj = joined(mix_grads, 0, CX).T
    grad_attn_out = joined(mix_grads, CX, CX + CQ).T
    base = CX + CQ
    owners = range(0, TEAM, SHARE)
    grad_query = joined(mix_grads, base + CX, base + CX + CQ)
    grad_key = joined(mix_grads, base + CX + CQ, base + CX + CQ + HD, owners)
    grad_value = joined(mix_grads, base + CX + CQ + HD, base + CX + CQ + 2 * HD, owners)
    grad_ffn_gain = jnp.sum(mix_grads[:, :, base + CX + CQ + 2 * HD].astype(F32), axis=0)
    grad_in_proj = jnp.concatenate(
        [
            joined(mix_grads, base, base + CX),
            joined(late_grads, 0, CX),
            joined(late_grads, CX, CX + CB),
            joined(late_grads, CX + CB, CX + CB + HEADS),
        ],
        axis=1,
    )
    grad_norm_gain = jnp.sum(late_grads[:, :, CX + CB + HEADS].astype(F32), axis=0)
    return (
        layer_out,
        grad_in,
        grad_norm_gain,
        grad_in_proj,
        grad_query,
        grad_key,
        grad_value,
        grad_out_proj,
        grad_attn_out,
        grad_ffn_gain,
        grad_gate,
        grad_up,
        grad_down,
        grad_conv_weight,
        grad_conv_bias,
        grad_a_log,
        grad_dt_bias,
        grad_d_skip,
    )


def solution(mesh):
    rows = P("dp", None)
    columns = P(None, "dp")
    in_specs = (
        (rows, rows, P("dp"), P("dp"), rows, rows, rows, rows, columns, columns)
        + (P("dp"), rows, rows, columns)
        + (P(),) * 5
    )
    out_specs = (
        (rows, rows, P("dp"), rows, rows, rows, rows, columns, columns)
        + (P("dp"), rows, rows, columns)
        + (P(),) * 5
    )
    return jax.shard_map(body, mesh=mesh, in_specs=in_specs, out_specs=out_specs, check_vma=False)
```

```python
import functools

import jax
import jax.numpy as jnp
from jax import lax
from jax.experimental import pallas as pl
from jax.experimental.pallas import tpu as pltpu
from jax.sharding import PartitionSpec as P

D = 1024
MH = 24
HD = 64
NST = 128
KCONV = 4
AH = 8
KVH = 2
FF = 2048
CHUNK = 128
DI = 1536
CONVCH = 1792
SEQ = 2048

EPS = 1e-05
ROPE_BASE = 10000.0

TEAM = 4
BITS = TEAM.bit_length() - 1
HEADS = MH // TEAM
CX = HEADS * HD
QH = AH // TEAM
CQ = QH * HD
CF = FF // TEAM
SHARE = TEAM // KVH
CB = 2 * NST // TEAM

F32 = jnp.float32
BF16 = jnp.bfloat16


def product(first_arg, second_arg):
    return jnp.dot(first_arg, second_arg, preferred_element_type=F32)


def times_transposed(first_arg, second_arg):
    return lax.dot_general(
        first_arg, second_arg, (((1,), (1,)), ((), ())), preferred_element_type=F32
    )


def transposed_times(first_arg, second_arg):
    return lax.dot_general(
        first_arg, second_arg, (((0,), (0,)), ((), ())), preferred_element_type=F32
    )


def device_index():
    return lax.axis_index("dp")


def member():
    return device_index() % TEAM


def member_bit(bit):
    return (device_index() >> bit) & 1


def peer(value, distance):
    count = lax.axis_size("dp")
    return lax.ppermute(value, "dp", [(i, i ^ distance) for i in range(count)])


def shift_teams(value, steps):
    count = lax.axis_size("dp")
    offset = steps * TEAM
    first, last = (max(0, -offset), min(count, count - offset))
    return lax.ppermute(value, "dp", [(i, i + offset) for i in range(first, last)])


def team_gather(value):
    for bit in reversed(range(BITS)):
        value = jnp.concatenate([value, peer(value, 1 << bit)], axis=0)
    return value


def team_scatter(partial):
    for bit in range(BITS):
        half = partial.shape[0] // 2
        arrived = peer(partial[half:].astype(BF16), 1 << bit)
        partial = partial[:half] + arrived.astype(F32)
    return partial


def reversed_bits(value):
    result = 0
    for bit in range(BITS):
        result = result | (((value >> bit) & 1) << (BITS - 1 - bit))
    return result


def copy_kernel(index_ref, from_ref, to_ref):
    to_ref[...] = from_ref[...]


def reorder(value, to_seq):
    rows = value.shape[0] // TEAM

    def source(block, index_ref):
        if to_seq:
            return (reversed_bits(block ^ index_ref[0]), 0)
        return (reversed_bits(block) ^ index_ref[0], 0)

    return pl.pallas_call(
        copy_kernel,
        grid_spec=pltpu.PrefetchScalarGridSpec(
            num_scalar_prefetch=1,
            grid=(TEAM,),
            in_specs=[pl.BlockSpec((rows, value.shape[1]), source)],
            out_specs=pl.BlockSpec((rows, value.shape[1]), lambda block, index_ref: (block, 0)),
        ),
        out_shape=jax.ShapeDtypeStruct(value.shape, value.dtype),
    )(member()[None].astype(jnp.int32), value)


def member_order(pieces):
    for bit in range(BITS):
        split = pieces.reshape((TEAM >> (bit + 1), 2, 1 << bit) + pieces.shape[1:])
        flipped = jnp.concatenate([split[:, 1:], split[:, :1]], axis=1)
        pieces = jnp.where(member_bit(bit) == 0, split, flipped).reshape(pieces.shape)
    return pieces


def reorder_rows(rows):
    order = [0]
    for bit in reversed(range(BITS)):
        order = order + [k | (1 << bit) for k in order]
    return member_order(jnp.stack([rows[order.index(k)] for k in range(TEAM)]))


def team_exchange(pieces):
    relative = member_order(pieces)
    arrived = [relative[0]] + [peer(relative[k], k) for k in range(1, TEAM)]
    return member_order(jnp.stack(arrived))


def across_groups():
    count = lax.axis_size("dp")
    return [list(range(first, count, TEAM)) for first in range(TEAM)]


def gather_rows(pieces):
    rows = team_exchange(pieces)
    rows = rows.reshape((-1, rows.shape[-1]))
    return lax.all_gather(rows, "dp", axis=0, tiled=True, axis_index_groups=across_groups())


def first_level():
    rows = D // (lax.axis_size("dp") // TEAM)
    return max(0, (CHUNK // rows).bit_length() - 1)


def later_levels():
    levels = (lax.axis_size("dp") // TEAM).bit_length() - 1
    first = first_level()
    return list(range(levels - 1, first, -1)) + list(range(first - 1, -1, -1))


def sums_kernel(index_ref, left_ref, right_ref, sent_ref, kept_ref):
    half = pl.num_programs(0) // 2
    part = transposed_times(left_ref[...], right_ref[...]).astype(BF16)

    @pl.when(pl.program_id(0) < half)
    def _():
        sent_ref[...] = part

    @pl.when(pl.program_id(0) >= half)
    def _():
        kept_ref[...] = part


def split_sums(left, right):
    blocks = (lax.axis_size("dp") // TEAM) >> first_level()
    half = blocks // 2
    tokens, width = right.shape
    rows = left.shape[1] // blocks

    def source(block, index_ref):
        mine = index_ref[0]
        return (0, 2 * (block % half) + jnp.where(block < half, 1 - mine, mine))

    return pl.pallas_call(
        sums_kernel,
        grid_spec=pltpu.PrefetchScalarGridSpec(
            num_scalar_prefetch=1,
            grid=(blocks,),
            in_specs=[
                pl.BlockSpec((tokens, rows), source),
                pl.BlockSpec((tokens, width), lambda block, index_ref: (0, 0)),
            ],
            out_specs=[
                pl.BlockSpec((rows, width), lambda block, index_ref: (jnp.minimum(block, half - 1), 0)),
                pl.BlockSpec((rows, width), lambda block, index_ref: (jnp.maximum(block - half, 0), 0)),
            ],
        ),
        out_shape=[jax.ShapeDtypeStruct((half * rows, width), BF16)] * 2,
    )(member_bit(BITS + first_level())[None].astype(jnp.int32), left, right)


def sum_rows(matrix):
    return lax.psum_scatter(
        matrix, "dp", scatter_dimension=0, tiled=True, axis_index_groups=across_groups()
    )


def scatter_step(blocks, level):
    half = blocks.shape[0] // 2
    mine = member_bit(BITS + level)
    kept = lax.dynamic_slice_in_dim(blocks, mine * half, half, 0)
    sent = lax.dynamic_slice_in_dim(blocks, (1 - mine) * half, half, 0)
    arrived = peer(sent, TEAM << level)
    return (kept.astype(F32) + arrived.astype(F32)).astype(BF16)


def tied(first, second):
    return lax.optimization_barrier((first, second))


def hand_out(summed):
    rows = summed.shape[0] // TEAM
    arrived = []
    for k in range(TEAM):
        piece = lax.dynamic_slice_in_dim(summed, (member() ^ k) * rows, rows, 0)
        arrived.append(piece if k == 0 else peer(piece, k))
    return arrived


def place_kernel(plan, index_ref, *refs):
    outs = refs[len(refs) - plan["outs"] :]
    me = index_ref[0]
    for k in range(TEAM):
        for source in range(TEAM):

            @pl.when((me ^ k) == source)
            def _():
                for group, first, stop, out, column in plan["moves"]:
                    piece = refs[group * TEAM + k]
                    share = plan["share"][out]
                    if source % share == 0:
                        at = column + (source // share) * (stop - first)
                        outs[out][:, at : at + stop - first] = piece[:, first:stop].astype(F32)


def place(groups, moves, widths, share):
    plan = {"moves": moves, "outs": len(widths), "share": share}
    rows = groups[0][0].shape[0]
    operands = [piece for group in groups for piece in group]
    return pl.pallas_call(
        functools.partial(place_kernel, plan),
        out_shape=[jax.ShapeDtypeStruct((rows, width), F32) for width in widths],
        in_specs=[pl.BlockSpec(memory_space=pltpu.SMEM)]
        + [pl.BlockSpec(memory_space=pltpu.VMEM)] * len(operands),
        out_specs=[pl.BlockSpec(memory_space=pltpu.VMEM)] * len(widths),
    )(member()[None].astype(jnp.int32), *operands)


def sum_across_teams(vector):
    count = lax.axis_size("dp")
    distance = TEAM
    while distance < count:
        vector = vector + peer(vector, distance)
        distance *= 2
    return vector


def columns_of(matrix, index, width):
    return lax.slice_in_dim(matrix, index * width, (index + 1) * width, axis=1)


def my_slice(array, width, axis=-1):
    axis = axis % array.ndim
    return lax.dynamic_slice_in_dim(array, member() * width, width, axis)


def rotate(values, cosine, sine_vals):
    half_dim = HD // 2
    rows = values.shape[0]
    heads = values.reshape(rows, -1, HD)
    first_half = heads[..., :half_dim]
    second_half = heads[..., half_dim:]
    cosine = cosine[:, None, :]
    sine_vals = sine_vals[:, None, :]
    return jnp.concatenate(
        [
            first_half * cosine - second_half * sine_vals,
            second_half * cosine + first_half * sine_vals,
        ],
        axis=-1,
    ).reshape(values.shape)


def causal_conv(padded, conv_weight, conv_bias, positions):
    token_count = padded.shape[0] - (KCONV - 1)
    conv_sum = jnp.zeros((token_count, padded.shape[1]), F32) + conv_bias[None, :]
    for tap_index in range(KCONV):
        lag_rows = KCONV - 1 - tap_index
        shifted = padded[tap_index : tap_index + token_count] * conv_weight[tap_index][None, :]
        conv_sum = conv_sum + jnp.where((positions >= lag_rows)[:, None], shifted, 0.0)
    return jax.nn.silu(conv_sum)


def head_spread():
    head = lax.broadcasted_iota(jnp.int32, (HEADS, CX), 0)
    channel = lax.broadcasted_iota(jnp.int32, (HEADS, CX), 1)
    return jnp.where(channel // HD == head, 1.0, 0.0).astype(F32)


def exact(first_arg, second_arg, dims=((1,), (0,))):
    return lax.dot_general(
        first_arg,
        second_arg,
        (dims, ((), ())),
        precision=lax.Precision.HIGHEST,
        preferred_element_type=F32,
    )


def chunk_terms(decay, step, positions):
    row = lax.broadcasted_iota(jnp.int32, (CHUNK, CHUNK), 0)
    col = lax.broadcasted_iota(jnp.int32, (CHUNK, CHUNK), 1)
    inside = (col <= row) & (col >= row - positions)
    lower = jnp.where(col <= row, 1.0, 0.0).astype(F32)
    cumulative = exact(lower, decay)
    cumulative_rows = exact(decay, lower, ((0,), (1,)))
    spread = head_spread()
    wide = exact(cumulative, spread)
    step_wide = exact(step, spread)
    index = lax.broadcasted_iota(jnp.int32, (CHUNK, 1), 0)
    final = CHUNK - 1
    final_position = positions[final:, :]
    final_sum = wide[final:, :]
    carried = jnp.where(positions > index, jnp.exp(wide), 0.0)
    fade = jnp.where(index >= final - final_position, jnp.exp(final_sum - wide), 0.0)
    keep = jnp.where(final_position > final, jnp.exp(final_sum), 0.0)
    return inside, lower, cumulative, cumulative_rows, spread, step_wide, carried, fade, keep


def head_decay(inside, cumulative, cumulative_rows, head):
    gap = cumulative[:, head : head + 1] - cumulative_rows[head : head + 1, :]
    return jnp.exp(jnp.where(inside, gap, -1e30))


def scan_forward_kernel(
    x_ref, b_ref, c_ref, step_ref, decay_ref, pos_ref, start_ref, y_ref, enter_ref, state_ref
):
    @pl.when(pl.program_id(0) == 0)
    def _():
        state_ref[...] = start_ref[...]

    terms = chunk_terms(decay_ref[...], step_ref[...], pos_ref[...])
    inside, _, cumulative, cumulative_rows, _, step_wide, carried, fade, keep = terms
    scaled = x_ref[...] * step_wide
    scaled_low = scaled.astype(BF16)
    b_low = b_ref[...].astype(BF16)
    c_low = c_ref[...].astype(BF16)
    inner = times_transposed(c_low, b_low)
    state = state_ref[...]
    enter_ref[0] = state
    far = product(c_low, state.astype(BF16)) * carried
    first_half = lax.broadcasted_iota(jnp.int32, (CHUNK, 2 * HD), 1) < HD
    for pair in range(HEADS // 2):
        lanes = slice(pair * 2 * HD, (pair + 1) * 2 * HD)
        near = [
            product(
                (head_decay(inside, cumulative, cumulative_rows, head) * inner).astype(BF16),
                scaled_low[:, lanes],
            )
            for head in (2 * pair, 2 * pair + 1)
        ]
        y_ref[:, lanes] = jnp.where(first_half, near[0], near[1]) + far[:, lanes]
    state_ref[...] = state * keep + transposed_times(b_low, (scaled * fade).astype(BF16))


def scan_specs(blocks, reverse):
    def at(block):
        return blocks - 1 - block if reverse else block

    def rows(width):
        return pl.BlockSpec((CHUNK, width), lambda block: (at(block), 0))

    whole = pl.BlockSpec((NST, CX), lambda block: (0, 0))
    entering = pl.BlockSpec((1, NST, CX), lambda block: (at(block), 0, 0))
    return rows, whole, entering


def scan_forward(inputs, b_rows, c_rows, step_sizes, log_decay, positions, state_in):
    tokens = inputs.shape[0]
    blocks = tokens // CHUNK
    rows, whole, entering = scan_specs(blocks, False)
    return pl.pallas_call(
        scan_forward_kernel,
        grid=(blocks,),
        in_specs=[rows(CX), rows(NST), rows(NST), rows(HEADS), rows(HEADS), rows(1), whole],
        out_specs=[rows(CX), entering],
        out_shape=[
            jax.ShapeDtypeStruct((tokens, CX), F32),
            jax.ShapeDtypeStruct((blocks, NST, CX), F32),
        ],
        scratch_shapes=[pltpu.VMEM((NST, CX), F32)],
        cost_estimate=pl.CostEstimate(flops=300000000, bytes_accessed=4000000, transcendentals=500000),
    )(inputs, b_rows, c_rows, step_sizes, log_decay, positions, state_in)


def scan_backward_kernel(
    x_ref, b_ref, c_ref, step_ref, decay_ref, pos_ref, slope_ref, rate_ref, skip_ref, enter_ref,
    grad_ref, end_ref, gx_ref, gb_ref, gc_ref, gdt_ref, gsums_ref, gskip_ref, adjoint_ref,
):
    @pl.when(pl.program_id(0) == 0)
    def _():
        adjoint_ref[...] = end_ref[...]
        gsums_ref[...] = jnp.zeros_like(gsums_ref)
        gskip_ref[...] = jnp.zeros_like(gskip_ref)

    step = step_ref[...]
    decay = decay_ref[...]
    terms = chunk_terms(decay, step, pos_ref[...])
    inside, lower, cumulative, cumulative_rows, spread, step_wide, carried, fade, keep = terms
    x = x_ref[...]
    grad = grad_ref[...]
    scaled = x * step_wide
    scaled_low = scaled.astype(BF16)
    grad_low = grad.astype(BF16)
    b_low = b_ref[...].astype(BF16)
    c_low = c_ref[...].astype(BF16)
    inner = times_transposed(c_low, b_low)
    state = enter_ref[0]
    state_low = state.astype(BF16)
    adjoint = adjoint_ref[...]
    adjoint_low = adjoint.astype(BF16)

    lane = lax.broadcasted_iota(jnp.int32, (CHUNK, 2 * HD), 1)
    inner_grad = jnp.zeros((CHUNK, CHUNK), F32)
    sum_grad = jnp.zeros((CHUNK, HEADS), F32)
    spot = lax.broadcasted_iota(jnp.int32, (CHUNK, HEADS), 1)
    near_parts = []
    for pair in range(HEADS // 2):
        lanes = slice(pair * 2 * HD, (pair + 1) * 2 * HD)
        grad_pair = grad_low[:, lanes]
        scaled_pair = scaled_low[:, lanes]
        near = []
        for half in range(2):
            head = 2 * pair + half
            fall = head_decay(inside, cumulative, cumulative_rows, head)
            mixed = fall * inner
            mine = (lane // HD) == half
            mixed_grad = times_transposed(jnp.where(mine, grad_pair, BF16(0.0)), scaled_pair)
            inner_grad = inner_grad + mixed_grad * fall
            weight_low = (mixed_grad * mixed).astype(BF16)
            pick = jnp.where(spot == head, 1.0, 0.0).astype(BF16)
            sum_grad = sum_grad + product(weight_low, pick) - transposed_times(weight_low, pick)
            near.append(transposed_times(mixed.astype(BF16), grad_pair))
        near_parts.append(jnp.where(lane < HD, near[0], near[1]))
    near_grad = jnp.concatenate(near_parts, axis=1)
    inner_grad_low = inner_grad.astype(BF16)

    carried_grad = grad * carried
    carried_low = carried_grad.astype(BF16)
    far_term = carried_grad * product(c_low, state_low)
    faded = scaled * fade
    reached = product(b_low, adjoint_low)
    tail_term = faded * reached
    scaled_grad = near_grad + fade * reached
    keep_term = jnp.sum(adjoint * state, axis=0, keepdims=True) * keep
    final_term = keep_term + jnp.sum(tail_term, axis=0, keepdims=True)
    final_row = lax.broadcasted_iota(jnp.int32, (CHUNK, 1), 0) == CHUNK - 1
    wide_term = far_term - tail_term + jnp.where(final_row, final_term, 0.0)
    sum_grad = sum_grad + exact(wide_term, spread, ((1,), (1,)))
    decay_grad = exact(lower, sum_grad, ((0,), (0,)))
    step_grad = exact(scaled_grad * x, spread, ((1,), (1,)))
    dt_grad = (step_grad - decay_grad * rate_ref[...]) * slope_ref[...]

    gx_ref[...] = scaled_grad * step_wide + skip_ref[...] * grad
    gb_ref[...] = transposed_times(inner_grad_low, c_low) + times_transposed(
        faded.astype(BF16), adjoint_low
    )
    gc_ref[...] = product(inner_grad_low, b_low) + times_transposed(carried_low, state_low)
    gdt_ref[...] = dt_grad
    gsums_ref[0:1, :] += jnp.sum(decay_grad * decay, axis=0, keepdims=True)
    gsums_ref[1:2, :] += jnp.sum(dt_grad, axis=0, keepdims=True)
    gskip_ref[...] += jnp.sum(grad * x, axis=0, keepdims=True)
    adjoint_ref[...] = adjoint * keep + transposed_times(c_low, carried_low)


def scan_backward(
    inputs, b_rows, c_rows, step_sizes, log_decay, positions, slopes, rates, skip, entering, grad,
    grad_end,
):
    tokens = inputs.shape[0]
    blocks = tokens // CHUNK
    rows, whole, enter = scan_specs(blocks, True)

    def fixed(first, second):
        return pl.BlockSpec((first, second), lambda block: (0, 0))

    shapes = [(tokens, CX), (tokens, NST), (tokens, NST), (tokens, HEADS), (2, HEADS), (1, CX)]
    return pl.pallas_call(
        scan_backward_kernel,
        grid=(blocks,),
        in_specs=[rows(CX), rows(NST), rows(NST), rows(HEADS), rows(HEADS), rows(1), rows(HEADS)]
        + [fixed(1, HEADS), fixed(1, CX), enter, rows(CX), whole],
        out_specs=[rows(CX), rows(NST), rows(NST), rows(HEADS), fixed(2, HEADS), fixed(1, CX)],
        out_shape=[jax.ShapeDtypeStruct(shape, F32) for shape in shapes],
        scratch_shapes=[pltpu.VMEM((NST, CX), F32)],
        cost_estimate=pl.CostEstimate(flops=900000000, bytes_accessed=6000000, transcendentals=500000),
    )(
        inputs, b_rows, c_rows, step_sizes, log_decay, positions, slopes, rates, skip, entering,
        grad, grad_end,
    )


def combine_states(own, rate, steps, reach):
    coarse = rate.astype(BF16)
    fine = (rate - coarse.astype(F32)).astype(BF16)
    flat = jnp.concatenate(
        [own.astype(BF16), jnp.broadcast_to(coarse, (8, CX)), jnp.broadcast_to(fine, (8, CX))], axis=0
    )
    total = None
    through = None
    for distance in range(1, reach + 1):
        arrived = shift_teams(flat, steps * distance).astype(F32)
        state = arrived[:NST]
        their_rate = arrived[NST : NST + 1] + arrived[NST + 8 : NST + 9]
        if total is None:
            total, through = state, their_rate
        else:
            total = total + through * state
            through = through * their_rate
    return total


def masked_scores(query_low, key_low, positions):
    row_count = query_low.shape[0]
    span_rows = key_low.shape[0]
    grouped = query_low.reshape(row_count, QH, HD)
    scores = jnp.einsum("sjd,td->jst", grouped, key_low, preferred_element_type=F32) * HD ** (-0.5)
    q_index = span_rows - row_count + jnp.arange(row_count)
    k_index = jnp.arange(span_rows)
    visible = (k_index[None, :] <= q_index[:, None]) & (
        k_index[None, :] >= (q_index - positions)[:, None]
    )
    return jnp.where(visible, scores, -1e30), grouped


def attend_forward(query_low, key_low, value_low, positions):
    scores, _ = masked_scores(query_low, key_low, positions)
    totals = jax.nn.logsumexp(scores, axis=-1, keepdims=True)
    weights_low = jnp.exp(scores - totals).astype(BF16)
    attended = jnp.einsum("jst,td->sjd", weights_low, value_low, preferred_element_type=F32)
    return attended.reshape(query_low.shape[0], CQ), totals


def attend_backward(query_low, key_low, value_low, positions, totals, grad_attended_low):
    scores, grouped = masked_scores(query_low, key_low, positions)
    row_count = query_low.shape[0]
    weights_full = jnp.exp(scores - totals)
    weights_low = weights_full.astype(BF16)
    grad_grouped = grad_attended_low.reshape(row_count, QH, HD)
    grad_weights = jnp.einsum(
        "sjd,td->jst", grad_grouped, value_low, preferred_element_type=F32
    )
    row_sums = jnp.sum(weights_full * grad_weights, axis=-1, keepdims=True)
    grad_scores = (weights_full * (grad_weights - row_sums)).astype(BF16)
    scale = HD ** (-0.5)
    grad_query = jnp.einsum("jst,td->sjd", grad_scores, key_low, preferred_element_type=F32) * scale
    grad_keys = jnp.einsum("jst,sjd->td", grad_scores, grouped, preferred_element_type=F32) * scale
    grad_values = jnp.einsum("jst,sjd->td", weights_low, grad_grouped, preferred_element_type=F32)
    return grad_query.reshape(row_count, CQ), jnp.concatenate([grad_keys, grad_values], axis=1)


def silu_slope(value):
    chance = jax.nn.sigmoid(value)
    return chance * (1.0 + value * (1.0 - chance))


def body(
    layer_in,
    cotangent,
    doc_positions,
    norm_gain,
    in_proj,
    w_query,
    w_key,
    w_value,
    out_proj,
    w_attn_out,
    ffn_gain,
    w_gate,
    w_up,
    w_down,
    conv_weight,
    conv_bias,
    a_log,
    dt_bias,
    d_skip,
):
    me = member()
    kv_mine = me // SHARE
    bc_cols = in_proj[:, 2 * DI : 2 * DI + 2 * NST]
    dt_cols = in_proj[:, DI + CONVCH :]
    first_pieces = jnp.stack(
        [
            jnp.concatenate(
                [
                    columns_of(in_proj[:, :DI], r, CX),
                    columns_of(in_proj[:, DI : 2 * DI], r, CX),
                    bc_cols,
                    columns_of(w_query, r, CQ),
                    columns_of(w_key, r // SHARE, HD),
                    columns_of(w_value, r // SHARE, HD),
                    columns_of(dt_cols, r, HEADS),
                    norm_gain[:, None],
                ],
                axis=1,
            )
            for r in range(TEAM)
        ]
    )
    out_rows = out_proj.T
    attn_rows = w_attn_out.T
    down_rows = w_down.T
    second_pieces = jnp.stack(
        [
            jnp.concatenate(
                [
                    columns_of(out_rows, r, CX),
                    columns_of(attn_rows, r, CQ),
                    columns_of(w_gate, r, CF),
                    columns_of(w_up, r, CF),
                    columns_of(down_rows, r, CF),
                    ffn_gain[:, None],
                ],
                axis=1,
            )
            for r in range(TEAM)
        ]
    )
    rows_one = gather_rows(first_pieces)
    rows_two = gather_rows(second_pieces)
    coarse = (doc_positions // 64).astype(BF16)[:, None]
    fine = (doc_positions % 64).astype(BF16)[:, None]
    spots = jnp.concatenate([coarse, fine, jnp.zeros((layer_in.shape[0], 126), BF16)], axis=1)
    team_start = team_gather(jnp.concatenate([layer_in, spots, cotangent], axis=1))
    team_top = team_start[:, D + 128 :]
    team_start = reorder(team_start[:, : D + 128], True)
    team_in = team_start[:, :D]
    spots = team_start[:, D : D + 2].astype(F32)
    position_column = (spots[:, :1] * 64.0 + spots[:, 1:]).astype(jnp.int32)
    positions = position_column[:, 0]

    z_end = CX
    x_end = 2 * CX
    bc_end = x_end + 2 * NST
    q_end = bc_end + CQ
    kv_end = q_end + 2 * HD
    dt_end = kv_end + HEADS
    main_one = rows_one[:, :dt_end]
    gain_one = rows_one[:, dt_end].astype(F32)
    mix_weights = rows_two[:, : CX + CQ]
    ffn_weights = rows_two[:, CX + CQ : CX + CQ + 2 * CF]
    down_weights = rows_two[:, CX + CQ + 2 * CF : CX + CQ + 3 * CF]
    gain_two = rows_two[:, CX + CQ + 3 * CF].astype(F32)

    tokens = team_in.shape[0]
    row_count = layer_in.shape[0]
    reach = SEQ // tokens - 1
    last = tokens - 1

    wide_in = team_in.astype(F32)
    scaled_in = wide_in * lax.rsqrt(jnp.mean(wide_in * wide_in, axis=-1, keepdims=True) + EPS)
    normed_low = (scaled_in * gain_one).astype(BF16)
    projected = product(normed_low, main_one)

    half_dim = HD // 2
    frequency = ROPE_BASE ** (-jnp.arange(half_dim, dtype=F32) / half_dim)
    angles = positions.astype(F32)[:, None] * frequency[None, :]
    cosine = jnp.cos(angles)
    sine_vals = jnp.sin(angles)

    gate_z = projected[:, :z_end]
    conv_low = projected[:, z_end:bc_end].astype(BF16)
    rim_rows = shift_teams(conv_low[tokens - (KCONV - 1) :], 1)
    query_low = rotate(projected[:, bc_end:q_end], cosine, sine_vals).astype(BF16)
    key_low = rotate(projected[:, q_end : q_end + HD], cosine, sine_vals).astype(BF16)
    value_low = projected[:, q_end + HD : kv_end].astype(BF16)
    dt_raw = projected[:, kv_end:dt_end]
    own_window = jnp.concatenate([key_low, value_low], axis=1)
    window = jnp.concatenate(
        [shift_teams(own_window, steps) for steps in range(reach, 0, -1)] + [own_window], axis=0
    )
    key_window = window[:, :HD]
    value_window = window[:, HD:]

    taps_x = my_slice(conv_weight[:, :DI], CX)
    bias_x = my_slice(conv_bias[:DI], CX)
    taps = jnp.concatenate([taps_x, conv_weight[:, DI:]], axis=1)
    bias = jnp.concatenate([bias_x, conv_bias[DI:]], axis=0)
    my_log_rates = my_slice(a_log, HEADS)
    my_dt_bias = my_slice(dt_bias, HEADS)
    my_skip = my_slice(d_skip, HEADS)
    skip_wide = jnp.repeat(my_skip, HD)

    padded = jnp.concatenate([rim_rows, conv_low], axis=0).astype(F32)
    conv_out = causal_conv(padded, taps, bias, positions)
    inputs = conv_out[:, :CX]
    b_rows = conv_out[:, CX : CX + NST]
    c_rows = conv_out[:, CX + NST :]

    raw_steps = dt_raw + my_dt_bias
    rate_of_head = jnp.exp(my_log_rates)
    step_sizes = jax.nn.softplus(raw_steps)
    log_decay = -step_sizes * rate_of_head
    row_index = jnp.arange(tokens)
    earlier = jnp.where(row_index[None, :] <= row_index[:, None], 1.0, 0.0).astype(F32)
    cumulative = jnp.repeat(exact(earlier, log_decay), HD, axis=1)
    tail_mask = jnp.where(row_index >= last - positions[last], 1.0, 0.0)
    fade_weights = jnp.exp(cumulative[last:] - cumulative) * tail_mask[:, None]
    scaled_inputs = inputs * jnp.repeat(step_sizes, HD, axis=1) * fade_weights
    local_state = transposed_times(b_rows, scaled_inputs)
    through = jnp.where(positions[last] > last, jnp.exp(cumulative[last:]), 0.0)
    state_in = combine_states(local_state, through, 1, reach)

    attended, totals = attend_forward(query_low, key_window, value_window, positions)
    attended_low = attended.astype(BF16)

    scanned, entering = scan_forward(
        inputs, b_rows, c_rows, step_sizes, log_decay, position_column, state_in
    )
    ssm_out = scanned + skip_wide * inputs
    silu_z = jax.nn.silu(gate_z)
    gated_low = (ssm_out * silu_z).astype(BF16)
    mixed_low = jnp.concatenate([gated_low, attended_low], axis=1)
    mixed_low = reorder(mixed_low, False)
    branches = team_scatter(times_transposed(mixed_low, mix_weights))
    middle = layer_in.astype(F32) + branches
    inverse_two = lax.rsqrt(jnp.mean(middle * middle, axis=-1, keepdims=True) + EPS)
    scaled_two = middle * inverse_two
    normed_two = team_gather((scaled_two * gain_two).astype(BF16))
    gate_up = product(normed_two, ffn_weights)
    gate_value = gate_up[:, :CF]
    up_value = gate_up[:, CF:]
    silu_gate = jax.nn.silu(gate_value)
    hidden_low = (silu_gate * up_value).astype(BF16)
    layer_out = (middle + team_scatter(times_transposed(hidden_low, down_weights))).astype(BF16)

    grad_hidden = product(team_top, down_weights)
    grad_gate_up = jnp.concatenate(
        [grad_hidden * up_value * silu_slope(gate_value), grad_hidden * silu_gate], axis=1
    ).astype(BF16)
    grad_normed_two = team_scatter(times_transposed(grad_gate_up, ffn_weights))
    ffn_sums = jnp.concatenate(
        [
            transposed_times(normed_two, grad_gate_up),
            transposed_times(team_top, hidden_low),
        ],
        axis=1,
    ).astype(BF16)
    grad_normed_two, ffn_sums = tied(grad_normed_two, ffn_sums)
    ffn_summed = sum_rows(ffn_sums)
    grad_gain_two = jnp.sum(grad_normed_two * scaled_two, axis=0)
    pulled = grad_normed_two * gain_two
    grad_middle = cotangent.astype(F32) + inverse_two * (
        pulled - scaled_two * jnp.mean(pulled * scaled_two, axis=-1, keepdims=True)
    )
    grad_branch = team_gather(grad_middle.astype(BF16))
    grad_mixed = reorder(product(grad_branch, mix_weights), True)
    grad_gated = grad_mixed[:, :CX]
    grad_attended_low = grad_mixed[:, CX:].astype(BF16)
    grad_ssm = grad_gated * silu_z
    grad_z_low = (grad_gated * ssm_out * silu_slope(gate_z)).astype(BF16)

    entry_weights = jnp.where(position_column > row_index[:, None], jnp.exp(cumulative), 0.0)
    local_adjoint = transposed_times(c_rows, grad_ssm * entry_weights)
    grad_state = combine_states(local_adjoint, through, -1, reach)

    grad_query_rot, grad_window = attend_backward(
        query_low, key_window, value_window, positions, totals, grad_attended_low
    )
    own_grad = grad_window[reach * tokens :]
    for steps in range(1, reach + 1):
        part = grad_window[(reach - steps) * tokens : (reach - steps + 1) * tokens]
        own_grad = own_grad + shift_teams(part.astype(BF16), -steps).astype(F32)
    distance = 1
    while distance < SHARE:
        own_grad = own_grad + peer(own_grad, distance)
        distance *= 2
    grad_query_low = rotate(grad_query_rot, cosine, -sine_vals).astype(BF16)
    grad_key_low = rotate(own_grad[:, :HD], cosine, -sine_vals).astype(BF16)
    grad_value_low = own_grad[:, HD:].astype(BF16)

    early_low = jnp.concatenate([grad_z_low, grad_query_low, grad_key_low, grad_value_low], axis=1)
    mix_sums = jnp.concatenate(
        [
            transposed_times(grad_branch, mixed_low),
            transposed_times(normed_low, early_low),
        ],
        axis=1,
    ).astype(BF16)
    grad_core = scan_backward(
        inputs, b_rows, c_rows, step_sizes, log_decay, position_column,
        jax.nn.sigmoid(raw_steps), rate_of_head[None], skip_wide[None], entering, grad_ssm,
        grad_state,
    )
    grad_core, mix_sums = tied(grad_core, mix_sums)
    mix_summed = sum_rows(mix_sums)
    grad_inputs, grad_b, grad_c, grad_dt_raw, head_sums, skip_sums = grad_core
    grad_skip = jnp.sum(skip_sums.reshape(HEADS, HD), axis=1)
    grad_log_rates, grad_step_bias = head_sums[0], head_sums[1]
    grad_bc = jnp.concatenate([grad_b, grad_c], axis=1)
    for bit in reversed(range(BITS)):
        half = grad_bc.shape[1] // 2
        low_half, high_half = grad_bc[:, :half], grad_bc[:, half:]
        first = member_bit(bit) == 0
        kept = jnp.where(first, low_half, high_half)
        sent = jnp.where(first, high_half, low_half).astype(BF16)
        grad_bc = kept + peer(sent, 1 << bit).astype(F32)

    conv_padded = jnp.concatenate([padded[:, :CX], my_slice(padded[:, CX:], CB)], axis=1)
    conv_taps = jnp.concatenate([taps[:, :CX], my_slice(taps[:, CX:], CB)], axis=1)
    conv_shift = jnp.concatenate([bias[:CX], my_slice(bias[CX:], CB)], axis=0)
    _, conv_back = jax.vjp(
        lambda rows, weights, offset: causal_conv(rows, weights, offset, positions),
        conv_padded, conv_taps, conv_shift,
    )
    grad_padded, grad_taps, grad_shift = conv_back(
        jnp.concatenate([grad_inputs, grad_bc], axis=1)
    )
    returned_rim = shift_teams(grad_padded[: KCONV - 1], -1)
    grad_conv = grad_padded[KCONV - 1 :]
    grad_conv = jnp.concatenate(
        [grad_conv[: tokens - (KCONV - 1)], grad_conv[tokens - (KCONV - 1) :] + returned_rim],
        axis=0,
    )
    grad_conv, ffn_summed = tied(grad_conv, ffn_summed)
    ffn_grads = hand_out(ffn_summed)
    grad_conv_low = grad_conv.astype(BF16)
    grad_dt_low = grad_dt_raw.astype(BF16)

    shared = 1.0 / SHARE
    late_low = jnp.concatenate([grad_conv_low, grad_dt_low], axis=1)
    all_low = jnp.concatenate(
        [
            grad_z_low,
            grad_conv_low,
            grad_query_low,
            grad_key_low * BF16(shared),
            grad_value_low * BF16(shared),
            grad_dt_low,
        ],
        axis=1,
    )
    back_weights = jnp.concatenate(
        [main_one[:, :x_end], my_slice(main_one[:, x_end:bc_end], CB), main_one[:, bc_end:]], axis=1
    )
    grad_normed_part = times_transposed(all_low, back_weights)
    gain_sums = jnp.sum(grad_normed_part * scaled_in, axis=0)
    sent_sums, kept_sums = split_sums(normed_low, late_low)
    arrived_sums = peer(sent_sums, TEAM << first_level())
    late_sums = (kept_sums.astype(F32) + arrived_sums.astype(F32)).astype(BF16)
    for level in later_levels():
        late_sums = scatter_step(late_sums, level)
    late_sums, mix_summed = tied(late_sums, mix_summed)
    late_grads = hand_out(late_sums)
    mix_grads = hand_out(mix_summed)
    grad_normed = team_scatter(reorder(grad_normed_part, False))
    own_in = layer_in.astype(F32)
    inverse_one = lax.rsqrt(jnp.mean(own_in * own_in, axis=-1, keepdims=True) + EPS)
    own_scaled = own_in * inverse_one
    pulled_one = grad_normed * gain_one
    grad_in = grad_middle + inverse_one * (
        pulled_one - own_scaled * jnp.mean(pulled_one * own_scaled, axis=-1, keepdims=True)
    )

    small = jnp.concatenate(
        [
            grad_taps.reshape(-1),
            grad_shift,
            grad_log_rates,
            grad_step_bias,
            grad_skip,
            grad_gain_two,
            gain_sums,
        ]
    )
    small = reorder_rows(team_gather(sum_across_teams(small)[None]))
    gains = jnp.sum(small[:, -2 * D :], axis=0)
    small = small[:, : -2 * D]
    gain_rows = norm_gain.shape[0]
    at_gain = device_index() * gain_rows
    grad_ffn_gain = lax.dynamic_slice_in_dim(gains[:D], at_gain, gain_rows, 0)
    grad_norm_gain = lax.dynamic_slice_in_dim(gains[D:], at_gain, gain_rows, 0)
    width = CX + CB
    taps_all = small[:, : KCONV * width].reshape(TEAM, KCONV, width)
    shift_all = small[:, KCONV * width : (KCONV + 1) * width]
    rest = small[:, (KCONV + 1) * width :].reshape(TEAM, 3, HEADS)
    grad_conv_weight = jnp.concatenate(
        [
            taps_all[:, :, :CX].transpose(1, 0, 2).reshape(KCONV, DI),
            taps_all[:, :, CX:].transpose(1, 0, 2).reshape(KCONV, 2 * NST),
        ],
        axis=1,
    )
    grad_conv_bias = jnp.concatenate([shift_all[:, :CX].reshape(-1), shift_all[:, CX:].reshape(-1)])
    grad_a_log = rest[:, 0].reshape(-1)
    grad_dt_bias = rest[:, 1].reshape(-1)
    grad_d_skip = rest[:, 2].reshape(-1)

    grad_gate, grad_up, grad_down = place(
        [ffn_grads],
        [(0, 0, CF, 0, 0), (0, CF, 2 * CF, 1, 0), (0, 2 * CF, 3 * CF, 2, 0)],
        [FF, FF, FF],
        [1, 1, 1],
    )
    base = CX + CQ
    keys_at = base + CX + CQ
    gain_at = keys_at + 2 * HD
    grad_out_proj, grad_attn_out, grad_in_proj, grad_query, grad_key, grad_value = place(
        [mix_grads, late_grads],
        [
            (0, 0, CX, 0, 0),
            (0, CX, base, 1, 0),
            (0, base, base + CX, 2, 0),
            (1, 0, CX, 2, DI),
            (1, CX, CX + CB, 2, 2 * DI),
            (1, CX + CB, CX + CB + HEADS, 2, 2 * DI + 2 * NST),
            (0, base + CX, keys_at, 3, 0),
            (0, keys_at, keys_at + HD, 4, 0),
            (0, keys_at + HD, gain_at, 5, 0),
        ],
        [DI, AH * HD, in_proj.shape[1], AH * HD, KVH * HD, KVH * HD],
        [1, 1, 1, 1, SHARE, SHARE],
    )
    grad_down = grad_down.T
    grad_out_proj = grad_out_proj.T
    grad_attn_out = grad_attn_out.T
    return (
        layer_out,
        grad_in,
        grad_norm_gain,
        grad_in_proj,
        grad_query,
        grad_key,
        grad_value,
        grad_out_proj,
        grad_attn_out,
        grad_ffn_gain,
        grad_gate,
        grad_up,
        grad_down,
        grad_conv_weight,
        grad_conv_bias,
        grad_a_log,
        grad_dt_bias,
        grad_d_skip,
    )


def solution(mesh):
    rows = P("dp", None)
    columns = P(None, "dp")
    in_specs = (
        (rows, rows, P("dp"), P("dp"), rows, rows, rows, rows, columns, columns)
        + (P("dp"), rows, rows, columns)
        + (P(),) * 5
    )
    out_specs = (
        (rows, rows, P("dp"), rows, rows, rows, rows, columns, columns)
        + (P("dp"), rows, rows, columns)
        + (P(),) * 5
    )
    return jax.shard_map(body, mesh=mesh, in_specs=in_specs, out_specs=out_specs, check_vma=False)
```

```python
import functools

import jax
import jax.numpy as jnp
from jax import lax
from jax.experimental import pallas as pl
from jax.experimental.pallas import tpu as pltpu
from jax.sharding import PartitionSpec as P

D = 1024
MH = 24
HD = 64
NST = 128
KCONV = 4
AH = 8
KVH = 2
FF = 2048
CHUNK = 128
DI = 1536
CONVCH = 1792
SEQ = 2048

EPS = 1e-05
ROPE_BASE = 10000.0

TEAM = 4
BITS = TEAM.bit_length() - 1
HEADS = MH // TEAM
CX = HEADS * HD
QH = AH // TEAM
CQ = QH * HD
CF = FF // TEAM
SHARE = TEAM // KVH
CB = 2 * NST // TEAM

F32 = jnp.float32
BF16 = jnp.bfloat16


def product(first_arg, second_arg):
    return jnp.dot(first_arg, second_arg, preferred_element_type=F32)


def times_transposed(first_arg, second_arg):
    return lax.dot_general(
        first_arg, second_arg, (((1,), (1,)), ((), ())), preferred_element_type=F32
    )


def transposed_times(first_arg, second_arg):
    return lax.dot_general(
        first_arg, second_arg, (((0,), (0,)), ((), ())), preferred_element_type=F32
    )


def device_index():
    return lax.axis_index("dp")


def member():
    return device_index() % TEAM


def member_bit(bit):
    return (device_index() >> bit) & 1


def peer(value, distance):
    count = lax.axis_size("dp")
    return lax.ppermute(value, "dp", [(i, i ^ distance) for i in range(count)])


def shift_teams(value, steps):
    count = lax.axis_size("dp")
    offset = steps * TEAM
    first, last = (max(0, -offset), min(count, count - offset))
    return lax.ppermute(value, "dp", [(i, i + offset) for i in range(first, last)])


def team_gather(value):
    for bit in reversed(range(BITS)):
        value = jnp.concatenate([value, peer(value, 1 << bit)], axis=0)
    return value


def team_scatter(partial):
    for bit in range(BITS):
        half = partial.shape[0] // 2
        arrived = peer(partial[half:].astype(BF16), 1 << bit)
        partial = partial[:half] + arrived.astype(F32)
    return partial


def reversed_bits(value):
    result = 0
    for bit in range(BITS):
        result = result | (((value >> bit) & 1) << (BITS - 1 - bit))
    return result


def reorder_kernel(to_seq, index_ref, from_ref, to_ref):
    rows = from_ref.shape[0] // TEAM
    me = index_ref[0]
    for block in range(TEAM):
        if to_seq:
            source = reversed_bits(me ^ block)
        else:
            source = me ^ reversed_bits(block)
        start = pl.multiple_of(source * rows, rows)
        to_ref[block * rows : (block + 1) * rows, :] = from_ref[pl.ds(start, rows), :]


def reorder(value, to_seq):
    whole = pl.BlockSpec(memory_space=pltpu.VMEM)
    return pl.pallas_call(
        functools.partial(reorder_kernel, to_seq),
        in_specs=[pl.BlockSpec(memory_space=pltpu.SMEM), whole],
        out_specs=whole,
        out_shape=jax.ShapeDtypeStruct(value.shape, value.dtype),
        compiler_params=pltpu.CompilerParams(vmem_limit_bytes=32 << 20),
    )(member()[None].astype(jnp.int32), value)


def member_order(pieces):
    for bit in range(BITS):
        split = pieces.reshape((TEAM >> (bit + 1), 2, 1 << bit) + pieces.shape[1:])
        flipped = jnp.concatenate([split[:, 1:], split[:, :1]], axis=1)
        pieces = jnp.where(member_bit(bit) == 0, split, flipped).reshape(pieces.shape)
    return pieces


def reorder_rows(rows):
    order = [0]
    for bit in reversed(range(BITS)):
        order = order + [k | (1 << bit) for k in order]
    return member_order(jnp.stack([rows[order.index(k)] for k in range(TEAM)]))


def team_exchange(pieces):
    relative = member_order(pieces)
    arrived = [relative[0]] + [peer(relative[k], k) for k in range(1, TEAM)]
    return member_order(jnp.stack(arrived))


def across_groups():
    count = lax.axis_size("dp")
    return [list(range(first, count, TEAM)) for first in range(TEAM)]


def exchanged_rows(pieces):
    rows = team_exchange(pieces)
    return rows.reshape((-1, rows.shape[-1]))


def gather_rows(rows):
    return lax.all_gather(rows, "dp", axis=0, tiled=True, axis_index_groups=across_groups())


def first_level():
    rows = D // (lax.axis_size("dp") // TEAM)
    return max(0, (CHUNK // rows).bit_length() - 1)


def later_levels():
    levels = (lax.axis_size("dp") // TEAM).bit_length() - 1
    first = first_level()
    return list(range(levels - 1, first, -1)) + list(range(first - 1, -1, -1))


def split_order(columns):
    blocks = (lax.axis_size("dp") // TEAM) >> first_level()
    width = columns.shape[1] // blocks
    parts = [columns[:, b * width : (b + 1) * width] for b in range(blocks)]
    return jnp.concatenate(parts[::2] + parts[1::2], axis=1)


def sum_rows(matrix):
    return lax.psum_scatter(
        matrix, "dp", scatter_dimension=0, tiled=True, axis_index_groups=across_groups()
    )


def scatter_step(blocks, level):
    half = blocks.shape[0] // 2
    mine = member_bit(BITS + level)
    kept = lax.dynamic_slice_in_dim(blocks, mine * half, half, 0)
    sent = lax.dynamic_slice_in_dim(blocks, (1 - mine) * half, half, 0)
    arrived = peer(sent, TEAM << level)
    return (kept.astype(F32) + arrived.astype(F32)).astype(BF16)


def tied(first, second):
    return lax.optimization_barrier((first, second))


def hand_out(summed):
    rows = summed.shape[0] // TEAM
    arrived = []
    for k in range(TEAM):
        piece = lax.dynamic_slice_in_dim(summed, (member() ^ k) * rows, rows, 0)
        arrived.append(piece if k == 0 else peer(piece, k))
    return arrived


def place_kernel(plan, index_ref, *refs):
    outs = refs[len(refs) - plan["outs"] :]
    me = index_ref[0]
    for k in range(TEAM):
        for source in range(TEAM):

            @pl.when((me ^ k) == source)
            def _():
                for group, first, stop, out, column in plan["moves"]:
                    piece = refs[group * TEAM + k]
                    share = plan["share"][out]
                    if source % share == 0:
                        at = column + (source // share) * (stop - first)
                        outs[out][:, at : at + stop - first] = piece[:, first:stop].astype(F32)


def place(groups, moves, widths, share):
    plan = {"moves": moves, "outs": len(widths), "share": share}
    rows = groups[0][0].shape[0]
    operands = [piece for group in groups for piece in group]
    return pl.pallas_call(
        functools.partial(place_kernel, plan),
        out_shape=[jax.ShapeDtypeStruct((rows, width), F32) for width in widths],
        in_specs=[pl.BlockSpec(memory_space=pltpu.SMEM)]
        + [pl.BlockSpec(memory_space=pltpu.VMEM)] * len(operands),
        out_specs=[pl.BlockSpec(memory_space=pltpu.VMEM)] * len(widths),
    )(member()[None].astype(jnp.int32), *operands)


def sum_across_teams(vector):
    count = lax.axis_size("dp")
    distance = TEAM
    while distance < count:
        vector = vector + peer(vector, distance)
        distance *= 2
    return vector


def columns_of(matrix, index, width):
    return lax.slice_in_dim(matrix, index * width, (index + 1) * width, axis=1)


def my_slice(array, width, axis=-1):
    axis = axis % array.ndim
    return lax.dynamic_slice_in_dim(array, member() * width, width, axis)


def rotate(values, cosine, sine_vals):
    half_dim = HD // 2
    rows = values.shape[0]
    heads = values.reshape(rows, -1, HD)
    first_half = heads[..., :half_dim]
    second_half = heads[..., half_dim:]
    cosine = cosine[:, None, :]
    sine_vals = sine_vals[:, None, :]
    return jnp.concatenate(
        [
            first_half * cosine - second_half * sine_vals,
            second_half * cosine + first_half * sine_vals,
        ],
        axis=-1,
    ).reshape(values.shape)


def causal_conv(padded, conv_weight, conv_bias, positions):
    token_count = padded.shape[0] - (KCONV - 1)
    conv_sum = jnp.zeros((token_count, padded.shape[1]), F32) + conv_bias[None, :]
    for tap_index in range(KCONV):
        lag_rows = KCONV - 1 - tap_index
        shifted = padded[tap_index : tap_index + token_count] * conv_weight[tap_index][None, :]
        conv_sum = conv_sum + jnp.where((positions >= lag_rows)[:, None], shifted, 0.0)
    return jax.nn.silu(conv_sum)


def head_spread():
    head = lax.broadcasted_iota(jnp.int32, (HEADS, CX), 0)
    channel = lax.broadcasted_iota(jnp.int32, (HEADS, CX), 1)
    return jnp.where(channel // HD == head, 1.0, 0.0).astype(F32)


def exact(first_arg, second_arg, dims=((1,), (0,))):
    return lax.dot_general(
        first_arg,
        second_arg,
        (dims, ((), ())),
        precision=lax.Precision.HIGHEST,
        preferred_element_type=F32,
    )


def chunk_terms(decay, step, positions):
    row = lax.broadcasted_iota(jnp.int32, (CHUNK, CHUNK), 0)
    col = lax.broadcasted_iota(jnp.int32, (CHUNK, CHUNK), 1)
    inside = (col <= row) & (col >= row - positions)
    lower = jnp.where(col <= row, 1.0, 0.0).astype(F32)
    cumulative = exact(lower, decay)
    cumulative_rows = exact(decay, lower, ((0,), (1,)))
    spread = head_spread()
    wide = exact(cumulative, spread)
    step_wide = exact(step, spread)
    index = lax.broadcasted_iota(jnp.int32, (CHUNK, 1), 0)
    final = CHUNK - 1
    final_position = positions[final:, :]
    final_sum = wide[final:, :]
    carried = jnp.where(positions > index, jnp.exp(wide), 0.0)
    fade = jnp.where(index >= final - final_position, jnp.exp(final_sum - wide), 0.0)
    keep = jnp.where(final_position > final, jnp.exp(final_sum), 0.0)
    return inside, lower, cumulative, cumulative_rows, spread, step_wide, carried, fade, keep


def head_decay(inside, cumulative, cumulative_rows, head):
    gap = cumulative[:, head : head + 1] - cumulative_rows[head : head + 1, :]
    return jnp.exp(jnp.where(inside, gap, -1e30))


def scan_forward_kernel(
    x_ref, b_ref, c_ref, step_ref, decay_ref, pos_ref, start_ref, y_ref, enter_ref, state_ref
):
    @pl.when(pl.program_id(0) == 0)
    def _():
        state_ref[...] = start_ref[...]

    terms = chunk_terms(decay_ref[...], step_ref[...], pos_ref[...])
    inside, _, cumulative, cumulative_rows, _, step_wide, carried, fade, keep = terms
    scaled = x_ref[...] * step_wide
    scaled_low = scaled.astype(BF16)
    b_low = b_ref[...].astype(BF16)
    c_low = c_ref[...].astype(BF16)
    inner = times_transposed(c_low, b_low)
    state = state_ref[...]
    enter_ref[0] = state
    far = product(c_low, state.astype(BF16)) * carried
    first_half = lax.broadcasted_iota(jnp.int32, (CHUNK, 2 * HD), 1) < HD
    for pair in range(HEADS // 2):
        lanes = slice(pair * 2 * HD, (pair + 1) * 2 * HD)
        near = [
            product(
                (head_decay(inside, cumulative, cumulative_rows, head) * inner).astype(BF16),
                scaled_low[:, lanes],
            )
            for head in (2 * pair, 2 * pair + 1)
        ]
        y_ref[:, lanes] = jnp.where(first_half, near[0], near[1]) + far[:, lanes]
    state_ref[...] = state * keep + transposed_times(b_low, (scaled * fade).astype(BF16))


def scan_specs(blocks, reverse):
    def at(block):
        return blocks - 1 - block if reverse else block

    def rows(width):
        return pl.BlockSpec((CHUNK, width), lambda block: (at(block), 0))

    whole = pl.BlockSpec((NST, CX), lambda block: (0, 0))
    entering = pl.BlockSpec((1, NST, CX), lambda block: (at(block), 0, 0))
    return rows, whole, entering


def scan_forward(inputs, b_rows, c_rows, step_sizes, log_decay, positions, state_in):
    tokens = inputs.shape[0]
    blocks = tokens // CHUNK
    rows, whole, entering = scan_specs(blocks, False)
    return pl.pallas_call(
        scan_forward_kernel,
        grid=(blocks,),
        in_specs=[rows(CX), rows(NST), rows(NST), rows(HEADS), rows(HEADS), rows(1), whole],
        out_specs=[rows(CX), entering],
        out_shape=[
            jax.ShapeDtypeStruct((tokens, CX), F32),
            jax.ShapeDtypeStruct((blocks, NST, CX), F32),
        ],
        scratch_shapes=[pltpu.VMEM((NST, CX), F32)],
        cost_estimate=pl.CostEstimate(flops=300000000, bytes_accessed=4000000, transcendentals=500000),
    )(inputs, b_rows, c_rows, step_sizes, log_decay, positions, state_in)


def scan_backward_kernel(
    x_ref, b_ref, c_ref, step_ref, decay_ref, pos_ref, slope_ref, rate_ref, skip_ref, enter_ref,
    grad_ref, end_ref, gx_ref, gb_ref, gc_ref, gdt_ref, gsums_ref, gskip_ref, adjoint_ref,
):
    @pl.when(pl.program_id(0) == 0)
    def _():
        adjoint_ref[...] = end_ref[...]
        gsums_ref[...] = jnp.zeros_like(gsums_ref)
        gskip_ref[...] = jnp.zeros_like(gskip_ref)

    step = step_ref[...]
    decay = decay_ref[...]
    terms = chunk_terms(decay, step, pos_ref[...])
    inside, lower, cumulative, cumulative_rows, spread, step_wide, carried, fade, keep = terms
    x = x_ref[...]
    grad = grad_ref[...]
    scaled = x * step_wide
    scaled_low = scaled.astype(BF16)
    grad_low = grad.astype(BF16)
    b_low = b_ref[...].astype(BF16)
    c_low = c_ref[...].astype(BF16)
    inner = times_transposed(c_low, b_low)
    state = enter_ref[0]
    state_low = state.astype(BF16)
    adjoint = adjoint_ref[...]
    adjoint_low = adjoint.astype(BF16)

    lane = lax.broadcasted_iota(jnp.int32, (CHUNK, 2 * HD), 1)
    inner_grad = jnp.zeros((CHUNK, CHUNK), F32)
    sum_grad = jnp.zeros((CHUNK, HEADS), F32)
    spot = lax.broadcasted_iota(jnp.int32, (CHUNK, HEADS), 1)
    near_parts = []
    for pair in range(HEADS // 2):
        lanes = slice(pair * 2 * HD, (pair + 1) * 2 * HD)
        grad_pair = grad_low[:, lanes]
        scaled_pair = scaled_low[:, lanes]
        near = []
        for half in range(2):
            head = 2 * pair + half
            fall = head_decay(inside, cumulative, cumulative_rows, head)
            mixed = fall * inner
            mine = (lane // HD) == half
            mixed_grad = times_transposed(jnp.where(mine, grad_pair, BF16(0.0)), scaled_pair)
            inner_grad = inner_grad + mixed_grad * fall
            weight_low = (mixed_grad * mixed).astype(BF16)
            pick = jnp.where(spot == head, 1.0, 0.0).astype(BF16)
            sum_grad = sum_grad + product(weight_low, pick) - transposed_times(weight_low, pick)
            near.append(transposed_times(mixed.astype(BF16), grad_pair))
        near_parts.append(jnp.where(lane < HD, near[0], near[1]))
    near_grad = jnp.concatenate(near_parts, axis=1)
    inner_grad_low = inner_grad.astype(BF16)

    carried_grad = grad * carried
    carried_low = carried_grad.astype(BF16)
    far_term = carried_grad * product(c_low, state_low)
    faded = scaled * fade
    reached = product(b_low, adjoint_low)
    tail_term = faded * reached
    scaled_grad = near_grad + fade * reached
    keep_term = jnp.sum(adjoint * state, axis=0, keepdims=True) * keep
    final_term = keep_term + jnp.sum(tail_term, axis=0, keepdims=True)
    final_row = lax.broadcasted_iota(jnp.int32, (CHUNK, 1), 0) == CHUNK - 1
    wide_term = far_term - tail_term + jnp.where(final_row, final_term, 0.0)
    sum_grad = sum_grad + exact(wide_term, spread, ((1,), (1,)))
    decay_grad = exact(lower, sum_grad, ((0,), (0,)))
    step_grad = exact(scaled_grad * x, spread, ((1,), (1,)))
    dt_grad = (step_grad - decay_grad * rate_ref[...]) * slope_ref[...]

    gx_ref[...] = scaled_grad * step_wide + skip_ref[...] * grad
    gb_ref[...] = transposed_times(inner_grad_low, c_low) + times_transposed(
        faded.astype(BF16), adjoint_low
    )
    gc_ref[...] = product(inner_grad_low, b_low) + times_transposed(carried_low, state_low)
    gdt_ref[...] = dt_grad
    gsums_ref[0:1, :] += jnp.sum(decay_grad * decay, axis=0, keepdims=True)
    gsums_ref[1:2, :] += jnp.sum(dt_grad, axis=0, keepdims=True)
    gskip_ref[...] += jnp.sum(grad * x, axis=0, keepdims=True)
    adjoint_ref[...] = adjoint * keep + transposed_times(c_low, carried_low)


def scan_backward(
    inputs, b_rows, c_rows, step_sizes, log_decay, positions, slopes, rates, skip, entering, grad,
    grad_end,
):
    tokens = inputs.shape[0]
    blocks = tokens // CHUNK
    rows, whole, enter = scan_specs(blocks, True)

    def fixed(first, second):
        return pl.BlockSpec((first, second), lambda block: (0, 0))

    shapes = [(tokens, CX), (tokens, NST), (tokens, NST), (tokens, HEADS), (2, HEADS), (1, CX)]
    return pl.pallas_call(
        scan_backward_kernel,
        grid=(blocks,),
        in_specs=[rows(CX), rows(NST), rows(NST), rows(HEADS), rows(HEADS), rows(1), rows(HEADS)]
        + [fixed(1, HEADS), fixed(1, CX), enter, rows(CX), whole],
        out_specs=[rows(CX), rows(NST), rows(NST), rows(HEADS), fixed(2, HEADS), fixed(1, CX)],
        out_shape=[jax.ShapeDtypeStruct(shape, F32) for shape in shapes],
        scratch_shapes=[pltpu.VMEM((NST, CX), F32)],
        cost_estimate=pl.CostEstimate(flops=1000000, bytes_accessed=100000, transcendentals=0),
    )(
        inputs, b_rows, c_rows, step_sizes, log_decay, positions, slopes, rates, skip, entering,
        grad, grad_end,
    )


def combine_states(own, rate, steps, reach):
    coarse = rate.astype(BF16)
    fine = (rate - coarse.astype(F32)).astype(BF16)
    flat = jnp.concatenate(
        [own.astype(BF16), jnp.broadcast_to(coarse, (8, CX)), jnp.broadcast_to(fine, (8, CX))], axis=0
    )
    total = None
    through = None
    for distance in range(1, reach + 1):
        arrived = shift_teams(flat, steps * distance).astype(F32)
        state = arrived[:NST]
        their_rate = arrived[NST : NST + 1] + arrived[NST + 8 : NST + 9]
        if total is None:
            total, through = state, their_rate
        else:
            total = total + through * state
            through = through * their_rate
    return total


def masked_scores(query_low, key_low, positions):
    row_count = query_low.shape[0]
    span_rows = key_low.shape[0]
    grouped = query_low.reshape(row_count, QH, HD)
    scores = jnp.einsum("sjd,td->jst", grouped, key_low, preferred_element_type=F32) * HD ** (-0.5)
    q_index = span_rows - row_count + jnp.arange(row_count)
    k_index = jnp.arange(span_rows)
    visible = (k_index[None, :] <= q_index[:, None]) & (
        k_index[None, :] >= (q_index - positions)[:, None]
    )
    return jnp.where(visible, scores, -1e30), grouped


def attend_forward(query_low, key_low, value_low, positions):
    scores, _ = masked_scores(query_low, key_low, positions)
    totals = jax.nn.logsumexp(scores, axis=-1, keepdims=True)
    weights_low = jnp.exp(scores - totals).astype(BF16)
    attended = jnp.einsum("jst,td->sjd", weights_low, value_low, preferred_element_type=F32)
    return attended.reshape(query_low.shape[0], CQ), totals


def attend_backward(query_low, key_low, value_low, positions, totals, grad_attended_low):
    scores, grouped = masked_scores(query_low, key_low, positions)
    row_count = query_low.shape[0]
    weights_full = jnp.exp(scores - totals)
    weights_low = weights_full.astype(BF16)
    grad_grouped = grad_attended_low.reshape(row_count, QH, HD)
    grad_weights = jnp.einsum(
        "sjd,td->jst", grad_grouped, value_low, preferred_element_type=F32
    )
    row_sums = jnp.sum(weights_full * grad_weights, axis=-1, keepdims=True)
    grad_scores = (weights_full * (grad_weights - row_sums)).astype(BF16)
    scale = HD ** (-0.5)
    grad_query = jnp.einsum("jst,td->sjd", grad_scores, key_low, preferred_element_type=F32) * scale
    grad_keys = jnp.einsum("jst,sjd->td", grad_scores, grouped, preferred_element_type=F32) * scale
    grad_values = jnp.einsum("jst,sjd->td", weights_low, grad_grouped, preferred_element_type=F32)
    return grad_query.reshape(row_count, CQ), jnp.concatenate([grad_keys, grad_values], axis=1)


def silu_slope(value):
    chance = jax.nn.sigmoid(value)
    return chance * (1.0 + value * (1.0 - chance))


def body(
    layer_in,
    cotangent,
    doc_positions,
    norm_gain,
    in_proj,
    w_query,
    w_key,
    w_value,
    out_proj,
    w_attn_out,
    ffn_gain,
    w_gate,
    w_up,
    w_down,
    conv_weight,
    conv_bias,
    a_log,
    dt_bias,
    d_skip,
):
    me = member()
    kv_mine = me // SHARE
    bc_cols = in_proj[:, 2 * DI : 2 * DI + 2 * NST]
    dt_cols = in_proj[:, DI + CONVCH :]
    first_pieces = jnp.stack(
        [
            jnp.concatenate(
                [
                    columns_of(in_proj[:, :DI], r, CX),
                    columns_of(in_proj[:, DI : 2 * DI], r, CX),
                    bc_cols,
                    columns_of(w_query, r, CQ),
                    columns_of(w_key, r // SHARE, HD),
                    columns_of(w_value, r // SHARE, HD),
                    columns_of(dt_cols, r, HEADS),
                    norm_gain[:, None],
                ],
                axis=1,
            )
            for r in range(TEAM)
        ]
    )
    out_rows = out_proj.T
    attn_rows = w_attn_out.T
    down_rows = w_down.T
    second_pieces = jnp.stack(
        [
            jnp.concatenate(
                [
                    columns_of(out_rows, r, CX),
                    columns_of(attn_rows, r, CQ),
                    columns_of(w_gate, r, CF),
                    columns_of(w_up, r, CF),
                    columns_of(down_rows, r, CF),
                    ffn_gain[:, None],
                ],
                axis=1,
            )
            for r in range(TEAM)
        ]
    )
    rows_one = gather_rows(exchanged_rows(first_pieces))
    rows_two = gather_rows(exchanged_rows(second_pieces))
    coarse = (doc_positions // 64).astype(BF16)[:, None]
    fine = (doc_positions % 64).astype(BF16)[:, None]
    spots = jnp.concatenate([coarse, fine, jnp.zeros((layer_in.shape[0], 126), BF16)], axis=1)
    team_start = team_gather(jnp.concatenate([layer_in, spots, cotangent], axis=1))
    team_top = team_start[:, D + 128 :]
    team_start = reorder(team_start[:, : D + 128], True)
    team_in = team_start[:, :D]
    spots = team_start[:, D : D + 2].astype(F32)
    position_column = (spots[:, :1] * 64.0 + spots[:, 1:]).astype(jnp.int32)
    positions = position_column[:, 0]

    z_end = CX
    x_end = 2 * CX
    bc_end = x_end + 2 * NST
    q_end = bc_end + CQ
    kv_end = q_end + 2 * HD
    dt_end = kv_end + HEADS
    main_one = rows_one[:, :dt_end]
    gain_one = rows_one[:, dt_end].astype(F32)
    mix_weights = rows_two[:, : CX + CQ]
    ffn_weights = rows_two[:, CX + CQ : CX + CQ + 2 * CF]
    down_weights = rows_two[:, CX + CQ + 2 * CF : CX + CQ + 3 * CF]
    gain_two = rows_two[:, CX + CQ + 3 * CF].astype(F32)

    tokens = team_in.shape[0]
    row_count = layer_in.shape[0]
    reach = SEQ // tokens - 1
    last = tokens - 1

    wide_in = team_in.astype(F32)
    scaled_in = wide_in * lax.rsqrt(jnp.mean(wide_in * wide_in, axis=-1, keepdims=True) + EPS)
    normed_low = (scaled_in * gain_one).astype(BF16)
    ordered_normed = split_order(normed_low)
    projected = product(normed_low, main_one)

    half_dim = HD // 2
    frequency = ROPE_BASE ** (-jnp.arange(half_dim, dtype=F32) / half_dim)
    angles = positions.astype(F32)[:, None] * frequency[None, :]
    cosine = jnp.cos(angles)
    sine_vals = jnp.sin(angles)

    gate_z = projected[:, :z_end]
    conv_low = projected[:, z_end:bc_end].astype(BF16)
    rim_rows = shift_teams(conv_low[tokens - (KCONV - 1) :], 1)
    query_low = rotate(projected[:, bc_end:q_end], cosine, sine_vals).astype(BF16)
    key_low = rotate(projected[:, q_end : q_end + HD], cosine, sine_vals).astype(BF16)
    value_low = projected[:, q_end + HD : kv_end].astype(BF16)
    dt_raw = projected[:, kv_end:dt_end]
    own_window = jnp.concatenate([key_low, value_low], axis=1)
    window = jnp.concatenate(
        [shift_teams(own_window, steps) for steps in range(reach, 0, -1)] + [own_window], axis=0
    )
    key_window = window[:, :HD]
    value_window = window[:, HD:]

    taps_x = my_slice(conv_weight[:, :DI], CX)
    bias_x = my_slice(conv_bias[:DI], CX)
    taps = jnp.concatenate([taps_x, conv_weight[:, DI:]], axis=1)
    bias = jnp.concatenate([bias_x, conv_bias[DI:]], axis=0)
    my_log_rates = my_slice(a_log, HEADS)
    my_dt_bias = my_slice(dt_bias, HEADS)
    my_skip = my_slice(d_skip, HEADS)
    skip_wide = jnp.repeat(my_skip, HD)

    padded = jnp.concatenate([rim_rows, conv_low], axis=0).astype(F32)
    conv_out = causal_conv(padded, taps, bias, positions)
    inputs = conv_out[:, :CX]
    b_rows = conv_out[:, CX : CX + NST]
    c_rows = conv_out[:, CX + NST :]

    raw_steps = dt_raw + my_dt_bias
    rate_of_head = jnp.exp(my_log_rates)
    step_sizes = jax.nn.softplus(raw_steps)
    log_decay = -step_sizes * rate_of_head
    row_index = jnp.arange(tokens)
    earlier = jnp.where(row_index[None, :] <= row_index[:, None], 1.0, 0.0).astype(F32)
    cumulative = jnp.repeat(exact(earlier, log_decay), HD, axis=1)
    tail_mask = jnp.where(row_index >= last - positions[last], 1.0, 0.0)
    fade_weights = jnp.exp(cumulative[last:] - cumulative) * tail_mask[:, None]
    scaled_inputs = inputs * jnp.repeat(step_sizes, HD, axis=1) * fade_weights
    local_state = transposed_times(b_rows, scaled_inputs)
    through = jnp.where(positions[last] > last, jnp.exp(cumulative[last:]), 0.0)
    state_in = combine_states(local_state, through, 1, reach)

    attended, totals = attend_forward(query_low, key_window, value_window, positions)
    attended_low = attended.astype(BF16)

    scanned, entering = scan_forward(
        inputs, b_rows, c_rows, step_sizes, log_decay, position_column, state_in
    )
    ssm_out = scanned + skip_wide * inputs
    silu_z = jax.nn.silu(gate_z)
    gated_low = (ssm_out * silu_z).astype(BF16)
    mixed_low = jnp.concatenate([gated_low, attended_low], axis=1)
    mixed_low = reorder(mixed_low, False)
    branches = team_scatter(times_transposed(mixed_low, mix_weights))
    middle = layer_in.astype(F32) + branches
    inverse_two = lax.rsqrt(jnp.mean(middle * middle, axis=-1, keepdims=True) + EPS)
    scaled_two = middle * inverse_two
    normed_two = team_gather((scaled_two * gain_two).astype(BF16))
    gate_up = product(normed_two, ffn_weights)
    gate_value = gate_up[:, :CF]
    up_value = gate_up[:, CF:]
    silu_gate = jax.nn.silu(gate_value)
    hidden_low = (silu_gate * up_value).astype(BF16)
    layer_out = (middle + team_scatter(times_transposed(hidden_low, down_weights))).astype(BF16)

    grad_hidden = product(team_top, down_weights)
    grad_gate_up = jnp.concatenate(
        [grad_hidden * up_value * silu_slope(gate_value), grad_hidden * silu_gate], axis=1
    ).astype(BF16)
    grad_normed_two = team_scatter(times_transposed(grad_gate_up, ffn_weights))
    ffn_sums = (transposed_times(normed_two, grad_gate_up), transposed_times(team_top, hidden_low))
    ffn_sums = tuple(part.astype(BF16) for part in ffn_sums)
    grad_normed_two, ffn_sums = tied(grad_normed_two, ffn_sums)
    grad_gain_two = jnp.sum(grad_normed_two * scaled_two, axis=0)
    pulled = grad_normed_two * gain_two
    grad_middle = cotangent.astype(F32) + inverse_two * (
        pulled - scaled_two * jnp.mean(pulled * scaled_two, axis=-1, keepdims=True)
    )
    grad_branch = team_gather(grad_middle.astype(BF16))
    grad_mixed = reorder(product(grad_branch, mix_weights), True)
    branch_sums = transposed_times(grad_branch, mixed_low).astype(BF16)
    first_sums = jnp.concatenate([ffn_sums[0], ffn_sums[1], branch_sums], axis=1)
    grad_mixed, first_sums = tied(grad_mixed, first_sums)
    first_summed = sum_rows(first_sums)
    grad_gated = grad_mixed[:, :CX]
    grad_attended_low = grad_mixed[:, CX:].astype(BF16)
    grad_ssm = grad_gated * silu_z
    grad_z_low = (grad_gated * ssm_out * silu_slope(gate_z)).astype(BF16)

    entry_weights = jnp.where(position_column > row_index[:, None], jnp.exp(cumulative), 0.0)
    local_adjoint = transposed_times(c_rows, grad_ssm * entry_weights)
    grad_state = combine_states(local_adjoint, through, -1, reach)

    grad_query_rot, grad_window = attend_backward(
        query_low, key_window, value_window, positions, totals, grad_attended_low
    )
    own_grad = grad_window[reach * tokens :]
    for steps in range(1, reach + 1):
        part = grad_window[(reach - steps) * tokens : (reach - steps + 1) * tokens]
        own_grad = own_grad + shift_teams(part.astype(BF16), -steps).astype(F32)
    distance = 1
    while distance < SHARE:
        own_grad = own_grad + peer(own_grad, distance)
        distance *= 2
    grad_query_low = rotate(grad_query_rot, cosine, -sine_vals).astype(BF16)
    grad_key_low = rotate(own_grad[:, :HD], cosine, -sine_vals).astype(BF16)
    grad_value_low = own_grad[:, HD:].astype(BF16)

    early_low = jnp.concatenate([grad_z_low, grad_query_low, grad_key_low, grad_value_low], axis=1)
    early_sums = transposed_times(ordered_normed, early_low).astype(BF16)
    early_sums = scatter_step(early_sums, first_level())
    grad_core = scan_backward(
        inputs, b_rows, c_rows, step_sizes, log_decay, position_column,
        jax.nn.sigmoid(raw_steps), rate_of_head[None], skip_wide[None], entering, grad_ssm,
        grad_state,
    )
    grad_inputs, grad_b, grad_c, grad_dt_raw, head_sums, skip_sums = grad_core
    grad_skip = jnp.sum(skip_sums.reshape(HEADS, HD), axis=1)
    grad_log_rates, grad_step_bias = head_sums[0], head_sums[1]
    grad_bc = jnp.concatenate([grad_b, grad_c], axis=1)
    for bit in reversed(range(BITS)):
        half = grad_bc.shape[1] // 2
        low_half, high_half = grad_bc[:, :half], grad_bc[:, half:]
        first = member_bit(bit) == 0
        kept = jnp.where(first, low_half, high_half)
        sent = jnp.where(first, high_half, low_half).astype(BF16)
        grad_bc = kept + peer(sent, 1 << bit).astype(F32)

    conv_padded = jnp.concatenate([padded[:, :CX], my_slice(padded[:, CX:], CB)], axis=1)
    conv_taps = jnp.concatenate([taps[:, :CX], my_slice(taps[:, CX:], CB)], axis=1)
    conv_shift = jnp.concatenate([bias[:CX], my_slice(bias[CX:], CB)], axis=0)
    _, conv_back = jax.vjp(
        lambda rows, weights, offset: causal_conv(rows, weights, offset, positions),
        conv_padded, conv_taps, conv_shift,
    )
    grad_padded, grad_taps, grad_shift = conv_back(
        jnp.concatenate([grad_inputs, grad_bc], axis=1)
    )
    returned_rim = shift_teams(grad_padded[: KCONV - 1], -1)
    grad_conv = grad_padded[KCONV - 1 :]
    grad_conv = jnp.concatenate(
        [grad_conv[: tokens - (KCONV - 1)], grad_conv[tokens - (KCONV - 1) :] + returned_rim],
        axis=0,
    )
    grad_conv, early_sums = tied(grad_conv, early_sums)
    if later_levels()[:-1]:
        early_sums = scatter_step(early_sums, later_levels()[0])
    grad_conv_low = grad_conv.astype(BF16)
    grad_dt_low = grad_dt_raw.astype(BF16)

    shared = 1.0 / SHARE
    late_low = jnp.concatenate([grad_conv_low, grad_dt_low], axis=1)
    late_sums = transposed_times(ordered_normed, late_low).astype(BF16)
    late_sums, main_one = tied(late_sums, main_one)
    late_sums = scatter_step(late_sums, first_level())
    grad_bc_low = grad_conv_low[:, CX:]
    owner = jnp.arange(2 * NST) // CB
    wide_bc = jnp.where(owner == me, jnp.concatenate([grad_bc_low] * TEAM, axis=1), BF16(0.0))
    all_low = jnp.concatenate(
        [
            grad_z_low,
            grad_conv_low[:, :CX],
            wide_bc,
            grad_query_low,
            grad_key_low * BF16(shared),
            grad_value_low * BF16(shared),
            grad_dt_low,
        ],
        axis=1,
    )
    back_weights = main_one
    grad_normed_part = times_transposed(all_low, back_weights)
    grad_normed_part, late_sums, first_summed = lax.optimization_barrier(
        (grad_normed_part, late_sums, first_summed)
    )
    first_grads = hand_out(first_summed)
    if later_levels()[:-1]:
        late_sums = scatter_step(late_sums, later_levels()[0])
    gain_sums = jnp.sum(grad_normed_part * scaled_in, axis=0)
    grad_normed = team_scatter(reorder(grad_normed_part, False))
    grad_normed, late_sums = tied(grad_normed, late_sums)
    last_sums = jnp.concatenate([early_sums, late_sums], axis=1)
    for level in later_levels()[:-1][1:] + later_levels()[-1:]:
        last_sums = scatter_step(last_sums, level)
    last_grads = hand_out(last_sums)
    own_in = layer_in.astype(F32)
    inverse_one = lax.rsqrt(jnp.mean(own_in * own_in, axis=-1, keepdims=True) + EPS)
    own_scaled = own_in * inverse_one
    pulled_one = grad_normed * gain_one
    grad_in = grad_middle + inverse_one * (
        pulled_one - own_scaled * jnp.mean(pulled_one * own_scaled, axis=-1, keepdims=True)
    )

    small = jnp.concatenate(
        [
            grad_taps.reshape(-1),
            grad_shift,
            grad_log_rates,
            grad_step_bias,
            grad_skip,
            grad_gain_two,
            gain_sums,
        ]
    )
    small = reorder_rows(team_gather(sum_across_teams(small)[None]))
    gains = jnp.sum(small[:, -2 * D :], axis=0)
    small = small[:, : -2 * D]
    gain_rows = norm_gain.shape[0]
    at_gain = device_index() * gain_rows
    grad_ffn_gain = lax.dynamic_slice_in_dim(gains[:D], at_gain, gain_rows, 0)
    grad_norm_gain = lax.dynamic_slice_in_dim(gains[D:], at_gain, gain_rows, 0)
    width = CX + CB
    taps_all = small[:, : KCONV * width].reshape(TEAM, KCONV, width)
    shift_all = small[:, KCONV * width : (KCONV + 1) * width]
    rest = small[:, (KCONV + 1) * width :].reshape(TEAM, 3, HEADS)
    grad_conv_weight = jnp.concatenate(
        [
            taps_all[:, :, :CX].transpose(1, 0, 2).reshape(KCONV, DI),
            taps_all[:, :, CX:].transpose(1, 0, 2).reshape(KCONV, 2 * NST),
        ],
        axis=1,
    )
    grad_conv_bias = jnp.concatenate([shift_all[:, :CX].reshape(-1), shift_all[:, CX:].reshape(-1)])
    grad_a_log = rest[:, 0].reshape(-1)
    grad_dt_bias = rest[:, 1].reshape(-1)
    grad_d_skip = rest[:, 2].reshape(-1)

    base = 3 * CF + CX
    grad_gate, grad_up, grad_down, grad_out_proj, grad_attn_out = place(
        [first_grads],
        [
            (0, 0, CF, 0, 0),
            (0, CF, 2 * CF, 1, 0),
            (0, 2 * CF, 3 * CF, 2, 0),
            (0, 3 * CF, base, 3, 0),
            (0, base, base + CQ, 4, 0),
        ],
        [FF, FF, FF, DI, AH * HD],
        [1, 1, 1, 1, 1],
    )
    keys_at = CX + CQ
    late_at = keys_at + 2 * HD
    grad_in_proj, grad_query, grad_key, grad_value = place(
        [last_grads],
        [
            (0, 0, CX, 0, 0),
            (0, late_at, late_at + CX, 0, DI),
            (0, late_at + CX, late_at + CX + CB, 0, 2 * DI),
            (0, late_at + CX + CB, late_at + CX + CB + HEADS, 0, 2 * DI + 2 * NST),
            (0, CX, keys_at, 1, 0),
            (0, keys_at, keys_at + HD, 2, 0),
            (0, keys_at + HD, late_at, 3, 0),
        ],
        [in_proj.shape[1], AH * HD, KVH * HD, KVH * HD],
        [1, 1, SHARE, SHARE],
    )
    grad_down = grad_down.T
    grad_out_proj = grad_out_proj.T
    grad_attn_out = grad_attn_out.T
    return (
        layer_out,
        grad_in,
        grad_norm_gain,
        grad_in_proj,
        grad_query,
        grad_key,
        grad_value,
        grad_out_proj,
        grad_attn_out,
        grad_ffn_gain,
        grad_gate,
        grad_up,
        grad_down,
        grad_conv_weight,
        grad_conv_bias,
        grad_a_log,
        grad_dt_bias,
        grad_d_skip,
    )


def solution(mesh):
    rows = P("dp", None)
    columns = P(None, "dp")
    in_specs = (
        (rows, rows, P("dp"), P("dp"), rows, rows, rows, rows, columns, columns)
        + (P("dp"), rows, rows, columns)
        + (P(),) * 5
    )
    out_specs = (
        (rows, rows, P("dp"), rows, rows, rows, rows, columns, columns)
        + (P("dp"), rows, rows, columns)
        + (P(),) * 5
    )
    return jax.shard_map(body, mesh=mesh, in_specs=in_specs, out_specs=out_specs, check_vma=False)
```

```python
import functools

import jax
import jax.numpy as jnp
from jax import lax
from jax.experimental import pallas as pl
from jax.experimental.pallas import tpu as pltpu
from jax.sharding import PartitionSpec as P

D = 1024
MH = 24
HD = 64
NST = 128
KCONV = 4
AH = 8
KVH = 2
FF = 2048
CHUNK = 128
DI = 1536
CONVCH = 1792
SEQ = 2048

EPS = 1e-05
ROPE_BASE = 10000.0

TEAM = 4
BITS = TEAM.bit_length() - 1
HEADS = MH // TEAM
CX = HEADS * HD
QH = AH // TEAM
CQ = QH * HD
CF = FF // TEAM
SHARE = TEAM // KVH
CB = 2 * NST // TEAM

F32 = jnp.float32
BF16 = jnp.bfloat16


def product(first_arg, second_arg):
    return jnp.dot(first_arg, second_arg, preferred_element_type=F32)


def times_transposed(first_arg, second_arg):
    return lax.dot_general(
        first_arg, second_arg, (((1,), (1,)), ((), ())), preferred_element_type=F32
    )


def transposed_times(first_arg, second_arg):
    return lax.dot_general(
        first_arg, second_arg, (((0,), (0,)), ((), ())), preferred_element_type=F32
    )


def device_index():
    return lax.axis_index("dp")


def member():
    return device_index() % TEAM


def member_bit(bit):
    return (device_index() >> bit) & 1


def peer(value, distance):
    count = lax.axis_size("dp")
    return lax.ppermute(value, "dp", [(i, i ^ distance) for i in range(count)])


def shift_teams(value, steps):
    count = lax.axis_size("dp")
    offset = steps * TEAM
    first, last = (max(0, -offset), min(count, count - offset))
    return lax.ppermute(value, "dp", [(i, i + offset) for i in range(first, last)])


def team_gather(value):
    for bit in reversed(range(BITS)):
        value = jnp.concatenate([value, peer(value, 1 << bit)], axis=0)
    return value


def team_scatter(partial):
    for bit in range(BITS):
        half = partial.shape[0] // 2
        arrived = peer(partial[half:].astype(BF16), 1 << bit)
        partial = partial[:half] + arrived.astype(F32)
    return partial


def reversed_bits(value):
    result = 0
    for bit in range(BITS):
        result = result | (((value >> bit) & 1) << (BITS - 1 - bit))
    return result


def reorder_kernel(to_seq, index_ref, from_ref, to_ref):
    rows = from_ref.shape[0] // TEAM
    me = index_ref[0]
    for block in range(TEAM):
        if to_seq:
            source = reversed_bits(me ^ block)
        else:
            source = me ^ reversed_bits(block)
        start = pl.multiple_of(source * rows, rows)
        to_ref[block * rows : (block + 1) * rows, :] = from_ref[pl.ds(start, rows), :]


def reorder(value, to_seq):
    whole = pl.BlockSpec(memory_space=pltpu.VMEM)
    return pl.pallas_call(
        functools.partial(reorder_kernel, to_seq),
        in_specs=[pl.BlockSpec(memory_space=pltpu.SMEM), whole],
        out_specs=whole,
        out_shape=jax.ShapeDtypeStruct(value.shape, value.dtype),
        compiler_params=pltpu.CompilerParams(vmem_limit_bytes=32 << 20),
    )(member()[None].astype(jnp.int32), value)


def member_order(pieces):
    for bit in range(BITS):
        split = pieces.reshape((TEAM >> (bit + 1), 2, 1 << bit) + pieces.shape[1:])
        flipped = jnp.concatenate([split[:, 1:], split[:, :1]], axis=1)
        pieces = jnp.where(member_bit(bit) == 0, split, flipped).reshape(pieces.shape)
    return pieces


def reorder_rows(rows):
    order = [0]
    for bit in reversed(range(BITS)):
        order = order + [k | (1 << bit) for k in order]
    return member_order(jnp.stack([rows[order.index(k)] for k in range(TEAM)]))


def team_exchange(pieces):
    relative = member_order(pieces)
    arrived = [relative[0]] + [peer(relative[k], k) for k in range(1, TEAM)]
    return member_order(jnp.stack(arrived))


def across_groups():
    count = lax.axis_size("dp")
    return [list(range(first, count, TEAM)) for first in range(TEAM)]


def exchanged_rows(pieces):
    rows = team_exchange(pieces)
    return rows.reshape((-1, rows.shape[-1]))


def gather_rows(rows):
    return lax.all_gather(rows, "dp", axis=0, tiled=True, axis_index_groups=across_groups())


def first_level():
    rows = D // (lax.axis_size("dp") // TEAM)
    return max(0, (CHUNK // rows).bit_length() - 1)


def later_levels():
    levels = (lax.axis_size("dp") // TEAM).bit_length() - 1
    first = first_level()
    return list(range(levels - 1, first, -1)) + list(range(first - 1, -1, -1))


def split_order(columns):
    blocks = (lax.axis_size("dp") // TEAM) >> first_level()
    width = columns.shape[1] // blocks
    parts = [columns[:, b * width : (b + 1) * width] for b in range(blocks)]
    return jnp.concatenate(parts[::2] + parts[1::2], axis=1)


def sum_rows(matrix):
    return lax.psum_scatter(
        matrix, "dp", scatter_dimension=0, tiled=True, axis_index_groups=across_groups()
    )


def scatter_step(blocks, level):
    half = blocks.shape[0] // 2
    mine = member_bit(BITS + level)
    kept = lax.dynamic_slice_in_dim(blocks, mine * half, half, 0)
    sent = lax.dynamic_slice_in_dim(blocks, (1 - mine) * half, half, 0)
    arrived = peer(sent, TEAM << level)
    return (kept.astype(F32) + arrived.astype(F32)).astype(BF16)


def tied(first, second):
    return lax.optimization_barrier((first, second))


def hand_out(summed):
    rows = summed.shape[0] // TEAM
    arrived = []
    for k in range(TEAM):
        piece = lax.dynamic_slice_in_dim(summed, (member() ^ k) * rows, rows, 0)
        arrived.append(piece if k == 0 else peer(piece, k))
    return arrived


def place_kernel(plan, index_ref, *refs):
    outs = refs[len(refs) - plan["outs"] :]
    me = index_ref[0]
    for k in range(TEAM):
        for source in range(TEAM):

            @pl.when((me ^ k) == source)
            def _():
                for group, first, stop, out, column in plan["moves"]:
                    piece = refs[group * TEAM + k]
                    share = plan["share"][out]
                    if source % share == 0:
                        at = column + (source // share) * (stop - first)
                        outs[out][:, at : at + stop - first] = piece[:, first:stop].astype(F32)


def place(groups, moves, widths, share):
    plan = {"moves": moves, "outs": len(widths), "share": share}
    rows = groups[0][0].shape[0]
    operands = [piece for group in groups for piece in group]
    return pl.pallas_call(
        functools.partial(place_kernel, plan),
        out_shape=[jax.ShapeDtypeStruct((rows, width), F32) for width in widths],
        in_specs=[pl.BlockSpec(memory_space=pltpu.SMEM)]
        + [pl.BlockSpec(memory_space=pltpu.VMEM)] * len(operands),
        out_specs=[pl.BlockSpec(memory_space=pltpu.VMEM)] * len(widths),
    )(member()[None].astype(jnp.int32), *operands)


def sum_across_teams(vector):
    count = lax.axis_size("dp")
    distance = TEAM
    while distance < count:
        vector = vector + peer(vector, distance)
        distance *= 2
    return vector


def columns_of(matrix, index, width):
    return lax.slice_in_dim(matrix, index * width, (index + 1) * width, axis=1)


def my_slice(array, width, axis=-1):
    axis = axis % array.ndim
    return lax.dynamic_slice_in_dim(array, member() * width, width, axis)


def rotate(values, cosine, sine_vals):
    half_dim = HD // 2
    rows = values.shape[0]
    heads = values.reshape(rows, -1, HD)
    first_half = heads[..., :half_dim]
    second_half = heads[..., half_dim:]
    cosine = cosine[:, None, :]
    sine_vals = sine_vals[:, None, :]
    return jnp.concatenate(
        [
            first_half * cosine - second_half * sine_vals,
            second_half * cosine + first_half * sine_vals,
        ],
        axis=-1,
    ).reshape(values.shape)


def causal_conv(padded, conv_weight, conv_bias, positions):
    token_count = padded.shape[0] - (KCONV - 1)
    conv_sum = jnp.zeros((token_count, padded.shape[1]), F32) + conv_bias[None, :]
    for tap_index in range(KCONV):
        lag_rows = KCONV - 1 - tap_index
        shifted = padded[tap_index : tap_index + token_count] * conv_weight[tap_index][None, :]
        conv_sum = conv_sum + jnp.where((positions >= lag_rows)[:, None], shifted, 0.0)
    return jax.nn.silu(conv_sum)


def head_spread():
    head = lax.broadcasted_iota(jnp.int32, (HEADS, CX), 0)
    channel = lax.broadcasted_iota(jnp.int32, (HEADS, CX), 1)
    return jnp.where(channel // HD == head, 1.0, 0.0).astype(F32)


def exact(first_arg, second_arg, dims=((1,), (0,))):
    return lax.dot_general(
        first_arg,
        second_arg,
        (dims, ((), ())),
        precision=lax.Precision.HIGHEST,
        preferred_element_type=F32,
    )


def chunk_terms(decay, step, positions):
    row = lax.broadcasted_iota(jnp.int32, (CHUNK, CHUNK), 0)
    col = lax.broadcasted_iota(jnp.int32, (CHUNK, CHUNK), 1)
    inside = (col <= row) & (col >= row - positions)
    lower = jnp.where(col <= row, 1.0, 0.0).astype(F32)
    cumulative = exact(lower, decay)
    cumulative_rows = exact(decay, lower, ((0,), (1,)))
    spread = head_spread()
    wide = exact(cumulative, spread)
    step_wide = exact(step, spread)
    index = lax.broadcasted_iota(jnp.int32, (CHUNK, 1), 0)
    final = CHUNK - 1
    final_position = positions[final:, :]
    final_sum = wide[final:, :]
    carried = jnp.where(positions > index, jnp.exp(wide), 0.0)
    fade = jnp.where(index >= final - final_position, jnp.exp(final_sum - wide), 0.0)
    keep = jnp.where(final_position > final, jnp.exp(final_sum), 0.0)
    return inside, lower, cumulative, cumulative_rows, spread, step_wide, carried, fade, keep


def head_decay(inside, cumulative, cumulative_rows, head):
    gap = cumulative[:, head : head + 1] - cumulative_rows[head : head + 1, :]
    return jnp.exp(jnp.where(inside, gap, -1e30))


def scan_forward_kernel(
    x_ref, b_ref, c_ref, step_ref, decay_ref, pos_ref, start_ref, y_ref, enter_ref, state_ref
):
    @pl.when(pl.program_id(0) == 0)
    def _():
        state_ref[...] = start_ref[...]

    terms = chunk_terms(decay_ref[...], step_ref[...], pos_ref[...])
    inside, _, cumulative, cumulative_rows, _, step_wide, carried, fade, keep = terms
    scaled = x_ref[...] * step_wide
    scaled_low = scaled.astype(BF16)
    b_low = b_ref[...].astype(BF16)
    c_low = c_ref[...].astype(BF16)
    inner = times_transposed(c_low, b_low)
    state = state_ref[...]
    enter_ref[0] = state
    far = product(c_low, state.astype(BF16)) * carried
    first_half = lax.broadcasted_iota(jnp.int32, (CHUNK, 2 * HD), 1) < HD
    for pair in range(HEADS // 2):
        lanes = slice(pair * 2 * HD, (pair + 1) * 2 * HD)
        near = [
            product(
                (head_decay(inside, cumulative, cumulative_rows, head) * inner).astype(BF16),
                scaled_low[:, lanes],
            )
            for head in (2 * pair, 2 * pair + 1)
        ]
        y_ref[:, lanes] = jnp.where(first_half, near[0], near[1]) + far[:, lanes]
    state_ref[...] = state * keep + transposed_times(b_low, (scaled * fade).astype(BF16))


def scan_specs(blocks, reverse):
    def at(block):
        return blocks - 1 - block if reverse else block

    def rows(width):
        return pl.BlockSpec((CHUNK, width), lambda block: (at(block), 0))

    whole = pl.BlockSpec((NST, CX), lambda block: (0, 0))
    entering = pl.BlockSpec((1, NST, CX), lambda block: (at(block), 0, 0))
    return rows, whole, entering


def scan_forward(inputs, b_rows, c_rows, step_sizes, log_decay, positions, state_in):
    tokens = inputs.shape[0]
    blocks = tokens // CHUNK
    rows, whole, entering = scan_specs(blocks, False)
    return pl.pallas_call(
        scan_forward_kernel,
        grid=(blocks,),
        in_specs=[rows(CX), rows(NST), rows(NST), rows(HEADS), rows(HEADS), rows(1), whole],
        out_specs=[rows(CX), entering],
        out_shape=[
            jax.ShapeDtypeStruct((tokens, CX), F32),
            jax.ShapeDtypeStruct((blocks, NST, CX), F32),
        ],
        scratch_shapes=[pltpu.VMEM((NST, CX), F32)],
        cost_estimate=pl.CostEstimate(flops=300000000, bytes_accessed=4000000, transcendentals=500000),
    )(inputs, b_rows, c_rows, step_sizes, log_decay, positions, state_in)


def scan_backward_kernel(
    x_ref, b_ref, c_ref, step_ref, decay_ref, pos_ref, slope_ref, rate_ref, skip_ref, enter_ref,
    grad_ref, end_ref, gx_ref, gb_ref, gc_ref, gdt_ref, gsums_ref, gskip_ref, adjoint_ref,
):
    @pl.when(pl.program_id(0) == 0)
    def _():
        adjoint_ref[...] = end_ref[...]
        gsums_ref[...] = jnp.zeros_like(gsums_ref)
        gskip_ref[...] = jnp.zeros_like(gskip_ref)

    step = step_ref[...]
    decay = decay_ref[...]
    terms = chunk_terms(decay, step, pos_ref[...])
    inside, lower, cumulative, cumulative_rows, spread, step_wide, carried, fade, keep = terms
    x = x_ref[...]
    grad = grad_ref[...]
    scaled = x * step_wide
    scaled_low = scaled.astype(BF16)
    grad_low = grad.astype(BF16)
    b_low = b_ref[...].astype(BF16)
    c_low = c_ref[...].astype(BF16)
    inner = times_transposed(c_low, b_low)
    state = enter_ref[0]
    state_low = state.astype(BF16)
    adjoint = adjoint_ref[...]
    adjoint_low = adjoint.astype(BF16)

    lane = lax.broadcasted_iota(jnp.int32, (CHUNK, 2 * HD), 1)
    inner_grad = jnp.zeros((CHUNK, CHUNK), F32)
    sum_grad = jnp.zeros((CHUNK, HEADS), F32)
    spot = lax.broadcasted_iota(jnp.int32, (CHUNK, HEADS), 1)
    near_parts = []
    for pair in range(HEADS // 2):
        lanes = slice(pair * 2 * HD, (pair + 1) * 2 * HD)
        grad_pair = grad_low[:, lanes]
        scaled_pair = scaled_low[:, lanes]
        near = []
        for half in range(2):
            head = 2 * pair + half
            fall = head_decay(inside, cumulative, cumulative_rows, head)
            mixed = fall * inner
            mine = (lane // HD) == half
            mixed_grad = times_transposed(jnp.where(mine, grad_pair, BF16(0.0)), scaled_pair)
            inner_grad = inner_grad + mixed_grad * fall
            weight_low = (mixed_grad * mixed).astype(BF16)
            pick = jnp.where(spot == head, 1.0, 0.0).astype(BF16)
            sum_grad = sum_grad + product(weight_low, pick) - transposed_times(weight_low, pick)
            near.append(transposed_times(mixed.astype(BF16), grad_pair))
        near_parts.append(jnp.where(lane < HD, near[0], near[1]))
    near_grad = jnp.concatenate(near_parts, axis=1)
    inner_grad_low = inner_grad.astype(BF16)

    carried_grad = grad * carried
    carried_low = carried_grad.astype(BF16)
    far_term = carried_grad * product(c_low, state_low)
    faded = scaled * fade
    reached = product(b_low, adjoint_low)
    tail_term = faded * reached
    scaled_grad = near_grad + fade * reached
    keep_term = jnp.sum(adjoint * state, axis=0, keepdims=True) * keep
    final_term = keep_term + jnp.sum(tail_term, axis=0, keepdims=True)
    final_row = lax.broadcasted_iota(jnp.int32, (CHUNK, 1), 0) == CHUNK - 1
    wide_term = far_term - tail_term + jnp.where(final_row, final_term, 0.0)
    sum_grad = sum_grad + exact(wide_term, spread, ((1,), (1,)))
    decay_grad = exact(lower, sum_grad, ((0,), (0,)))
    step_grad = exact(scaled_grad * x, spread, ((1,), (1,)))
    dt_grad = (step_grad - decay_grad * rate_ref[...]) * slope_ref[...]

    gx_ref[...] = scaled_grad * step_wide + skip_ref[...] * grad
    gb_ref[...] = transposed_times(inner_grad_low, c_low) + times_transposed(
        faded.astype(BF16), adjoint_low
    )
    gc_ref[...] = product(inner_grad_low, b_low) + times_transposed(carried_low, state_low)
    gdt_ref[...] = dt_grad
    gsums_ref[0:1, :] += jnp.sum(decay_grad * decay, axis=0, keepdims=True)
    gsums_ref[1:2, :] += jnp.sum(dt_grad, axis=0, keepdims=True)
    gskip_ref[...] += jnp.sum(grad * x, axis=0, keepdims=True)
    adjoint_ref[...] = adjoint * keep + transposed_times(c_low, carried_low)


def scan_backward(
    inputs, b_rows, c_rows, step_sizes, log_decay, positions, slopes, rates, skip, entering, grad,
    grad_end,
):
    tokens = inputs.shape[0]
    blocks = tokens // CHUNK
    rows, whole, enter = scan_specs(blocks, True)

    def fixed(first, second):
        return pl.BlockSpec((first, second), lambda block: (0, 0))

    shapes = [(tokens, CX), (tokens, NST), (tokens, NST), (tokens, HEADS), (2, HEADS), (1, CX)]
    return pl.pallas_call(
        scan_backward_kernel,
        grid=(blocks,),
        in_specs=[rows(CX), rows(NST), rows(NST), rows(HEADS), rows(HEADS), rows(1), rows(HEADS)]
        + [fixed(1, HEADS), fixed(1, CX), enter, rows(CX), whole],
        out_specs=[rows(CX), rows(NST), rows(NST), rows(HEADS), fixed(2, HEADS), fixed(1, CX)],
        out_shape=[jax.ShapeDtypeStruct(shape, F32) for shape in shapes],
        scratch_shapes=[pltpu.VMEM((NST, CX), F32)],
        cost_estimate=pl.CostEstimate(flops=1000000, bytes_accessed=100000, transcendentals=0),
    )(
        inputs, b_rows, c_rows, step_sizes, log_decay, positions, slopes, rates, skip, entering,
        grad, grad_end,
    )


def combine_states(own, rate, steps, reach):
    coarse = rate.astype(BF16)
    fine = (rate - coarse.astype(F32)).astype(BF16)
    flat = jnp.concatenate(
        [own.astype(BF16), jnp.broadcast_to(coarse, (8, CX)), jnp.broadcast_to(fine, (8, CX))], axis=0
    )
    total = None
    through = None
    for distance in range(1, reach + 1):
        arrived = shift_teams(flat, steps * distance).astype(F32)
        state = arrived[:NST]
        their_rate = arrived[NST : NST + 1] + arrived[NST + 8 : NST + 9]
        if total is None:
            total, through = state, their_rate
        else:
            total = total + through * state
            through = through * their_rate
    return total


def masked_scores(query_low, key_low, positions):
    row_count = query_low.shape[0]
    span_rows = key_low.shape[0]
    grouped = query_low.reshape(row_count, QH, HD)
    scores = jnp.einsum("sjd,td->jst", grouped, key_low, preferred_element_type=F32) * HD ** (-0.5)
    q_index = span_rows - row_count + jnp.arange(row_count)
    k_index = jnp.arange(span_rows)
    visible = (k_index[None, :] <= q_index[:, None]) & (
        k_index[None, :] >= (q_index - positions)[:, None]
    )
    return jnp.where(visible, scores, -1e30), grouped


def attend_forward(query_low, key_low, value_low, positions):
    scores, _ = masked_scores(query_low, key_low, positions)
    totals = jax.nn.logsumexp(scores, axis=-1, keepdims=True)
    weights_low = jnp.exp(scores - totals).astype(BF16)
    attended = jnp.einsum("jst,td->sjd", weights_low, value_low, preferred_element_type=F32)
    return attended.reshape(query_low.shape[0], CQ), totals


def attend_backward(query_low, key_low, value_low, positions, totals, grad_attended_low):
    scores, grouped = masked_scores(query_low, key_low, positions)
    row_count = query_low.shape[0]
    weights_full = jnp.exp(scores - totals)
    weights_low = weights_full.astype(BF16)
    grad_grouped = grad_attended_low.reshape(row_count, QH, HD)
    grad_weights = jnp.einsum(
        "sjd,td->jst", grad_grouped, value_low, preferred_element_type=F32
    )
    row_sums = jnp.sum(weights_full * grad_weights, axis=-1, keepdims=True)
    grad_scores = (weights_full * (grad_weights - row_sums)).astype(BF16)
    scale = HD ** (-0.5)
    grad_query = jnp.einsum("jst,td->sjd", grad_scores, key_low, preferred_element_type=F32) * scale
    grad_keys = jnp.einsum("jst,sjd->td", grad_scores, grouped, preferred_element_type=F32) * scale
    grad_values = jnp.einsum("jst,sjd->td", weights_low, grad_grouped, preferred_element_type=F32)
    return grad_query.reshape(row_count, CQ), jnp.concatenate([grad_keys, grad_values], axis=1)


def silu_slope(value):
    chance = jax.nn.sigmoid(value)
    return chance * (1.0 + value * (1.0 - chance))


def body(
    layer_in,
    cotangent,
    doc_positions,
    norm_gain,
    in_proj,
    w_query,
    w_key,
    w_value,
    out_proj,
    w_attn_out,
    ffn_gain,
    w_gate,
    w_up,
    w_down,
    conv_weight,
    conv_bias,
    a_log,
    dt_bias,
    d_skip,
):
    me = member()
    kv_mine = me // SHARE
    bc_cols = in_proj[:, 2 * DI : 2 * DI + 2 * NST]
    dt_cols = in_proj[:, DI + CONVCH :]
    first_pieces = jnp.stack(
        [
            jnp.concatenate(
                [
                    columns_of(in_proj[:, :DI], r, CX),
                    columns_of(in_proj[:, DI : 2 * DI], r, CX),
                    bc_cols,
                    columns_of(w_query, r, CQ),
                    columns_of(w_key, r // SHARE, HD),
                    columns_of(w_value, r // SHARE, HD),
                    columns_of(dt_cols, r, HEADS),
                    norm_gain[:, None],
                    ffn_gain[:, None],
                ],
                axis=1,
            )
            for r in range(TEAM)
        ]
    )
    out_rows = out_proj.T
    attn_rows = w_attn_out.T
    down_rows = w_down.T
    second_pieces = jnp.stack(
        [
            jnp.concatenate(
                [
                    columns_of(out_rows, r, CX),
                    columns_of(attn_rows, r, CQ),
                    columns_of(w_gate, r, CF),
                    columns_of(w_up, r, CF),
                    columns_of(down_rows, r, CF),
                ],
                axis=1,
            )
            for r in range(TEAM)
        ]
    )
    rows_one = gather_rows(exchanged_rows(first_pieces))
    rows_two = gather_rows(exchanged_rows(second_pieces))
    coarse = (doc_positions // 64).astype(BF16)[:, None]
    fine = (doc_positions % 64).astype(BF16)[:, None]
    spots = jnp.concatenate([coarse, fine, jnp.zeros((layer_in.shape[0], 126), BF16)], axis=1)
    team_start = team_gather(jnp.concatenate([layer_in, spots, cotangent], axis=1))
    team_top = team_start[:, D + 128 :]
    team_start = reorder(team_start[:, : D + 128], True)
    team_in = team_start[:, :D]
    spots = team_start[:, D : D + 2].astype(F32)
    position_column = (spots[:, :1] * 64.0 + spots[:, 1:]).astype(jnp.int32)
    positions = position_column[:, 0]

    z_end = CX
    x_end = 2 * CX
    bc_end = x_end + 2 * NST
    q_end = bc_end + CQ
    kv_end = q_end + 2 * HD
    dt_end = kv_end + HEADS
    main_one = rows_one[:, :dt_end]
    gain_one = rows_one[:, dt_end].astype(F32)
    mix_weights = rows_two[:, : CX + CQ]
    ffn_weights = rows_two[:, CX + CQ : CX + CQ + 2 * CF]
    down_weights = rows_two[:, CX + CQ + 2 * CF : CX + CQ + 3 * CF]
    gain_two = rows_one[:, dt_end + 1].astype(F32)

    tokens = team_in.shape[0]
    row_count = layer_in.shape[0]
    reach = SEQ // tokens - 1
    last = tokens - 1

    wide_in = team_in.astype(F32)
    scaled_in = wide_in * lax.rsqrt(jnp.mean(wide_in * wide_in, axis=-1, keepdims=True) + EPS)
    normed_low = (scaled_in * gain_one).astype(BF16)
    ordered_normed = split_order(normed_low)
    projected = product(normed_low, main_one)

    half_dim = HD // 2
    frequency = ROPE_BASE ** (-jnp.arange(half_dim, dtype=F32) / half_dim)
    angles = positions.astype(F32)[:, None] * frequency[None, :]
    cosine = jnp.cos(angles)
    sine_vals = jnp.sin(angles)

    gate_z = projected[:, :z_end]
    conv_low = projected[:, z_end:bc_end].astype(BF16)
    rim_rows = shift_teams(conv_low[tokens - (KCONV - 1) :], 1)
    query_low = rotate(projected[:, bc_end:q_end], cosine, sine_vals).astype(BF16)
    key_low = rotate(projected[:, q_end : q_end + HD], cosine, sine_vals).astype(BF16)
    value_low = projected[:, q_end + HD : kv_end].astype(BF16)
    dt_raw = projected[:, kv_end:dt_end]
    own_window = jnp.concatenate([key_low, value_low], axis=1)
    window = jnp.concatenate(
        [shift_teams(own_window, steps) for steps in range(reach, 0, -1)] + [own_window], axis=0
    )
    key_window = window[:, :HD]
    value_window = window[:, HD:]

    taps_x = my_slice(conv_weight[:, :DI], CX)
    bias_x = my_slice(conv_bias[:DI], CX)
    taps = jnp.concatenate([taps_x, conv_weight[:, DI:]], axis=1)
    bias = jnp.concatenate([bias_x, conv_bias[DI:]], axis=0)
    my_log_rates = my_slice(a_log, HEADS)
    my_dt_bias = my_slice(dt_bias, HEADS)
    my_skip = my_slice(d_skip, HEADS)
    skip_wide = jnp.repeat(my_skip, HD)

    padded = jnp.concatenate([rim_rows, conv_low], axis=0).astype(F32)
    conv_out = causal_conv(padded, taps, bias, positions)
    inputs = conv_out[:, :CX]
    b_rows = conv_out[:, CX : CX + NST]
    c_rows = conv_out[:, CX + NST :]

    raw_steps = dt_raw + my_dt_bias
    rate_of_head = jnp.exp(my_log_rates)
    step_sizes = jax.nn.softplus(raw_steps)
    log_decay = -step_sizes * rate_of_head
    row_index = jnp.arange(tokens)
    earlier = jnp.where(row_index[None, :] <= row_index[:, None], 1.0, 0.0).astype(F32)
    cumulative = jnp.repeat(exact(earlier, log_decay), HD, axis=1)
    tail_mask = jnp.where(row_index >= last - positions[last], 1.0, 0.0)
    fade_weights = jnp.exp(cumulative[last:] - cumulative) * tail_mask[:, None]
    scaled_inputs = inputs * jnp.repeat(step_sizes, HD, axis=1) * fade_weights
    local_state = transposed_times(b_rows, scaled_inputs)
    through = jnp.where(positions[last] > last, jnp.exp(cumulative[last:]), 0.0)
    state_in = combine_states(local_state, through, 1, reach)

    attended, totals = attend_forward(query_low, key_window, value_window, positions)
    attended_low = attended.astype(BF16)

    scanned, entering = scan_forward(
        inputs, b_rows, c_rows, step_sizes, log_decay, position_column, state_in
    )
    ssm_out = scanned + skip_wide * inputs
    silu_z = jax.nn.silu(gate_z)
    gated_low = (ssm_out * silu_z).astype(BF16)
    mixed_low = jnp.concatenate([gated_low, attended_low], axis=1)
    mixed_low = reorder(mixed_low, False)
    branches = team_scatter(times_transposed(mixed_low, mix_weights))
    middle = layer_in.astype(F32) + branches
    inverse_two = lax.rsqrt(jnp.mean(middle * middle, axis=-1, keepdims=True) + EPS)
    scaled_two = middle * inverse_two
    normed_two = team_gather((scaled_two * gain_two).astype(BF16))
    gate_up = product(normed_two, ffn_weights)
    gate_value = gate_up[:, :CF]
    up_value = gate_up[:, CF:]
    silu_gate = jax.nn.silu(gate_value)
    hidden_low = (silu_gate * up_value).astype(BF16)
    layer_out = (middle + team_scatter(times_transposed(hidden_low, down_weights))).astype(BF16)

    grad_hidden = product(team_top, down_weights)
    grad_gate_up = jnp.concatenate(
        [grad_hidden * up_value * silu_slope(gate_value), grad_hidden * silu_gate], axis=1
    ).astype(BF16)
    grad_normed_two = team_scatter(times_transposed(grad_gate_up, ffn_weights))
    ffn_sums = (transposed_times(normed_two, grad_gate_up), transposed_times(team_top, hidden_low))
    ffn_sums = tuple(part.astype(BF16) for part in ffn_sums)
    grad_normed_two, ffn_sums = tied(grad_normed_two, ffn_sums)
    grad_gain_two = jnp.sum(grad_normed_two * scaled_two, axis=0)
    pulled = grad_normed_two * gain_two
    grad_middle = cotangent.astype(F32) + inverse_two * (
        pulled - scaled_two * jnp.mean(pulled * scaled_two, axis=-1, keepdims=True)
    )
    grad_branch = team_gather(grad_middle.astype(BF16))
    grad_mixed = reorder(product(grad_branch, mix_weights), True)
    branch_sums = transposed_times(grad_branch, mixed_low).astype(BF16)
    first_sums = jnp.concatenate([ffn_sums[0], ffn_sums[1], branch_sums], axis=1)
    grad_mixed, first_sums = tied(grad_mixed, first_sums)
    first_summed = sum_rows(first_sums)
    grad_gated = grad_mixed[:, :CX]
    grad_attended_low = grad_mixed[:, CX:].astype(BF16)
    grad_ssm = grad_gated * silu_z
    grad_z_low = (grad_gated * ssm_out * silu_slope(gate_z)).astype(BF16)

    entry_weights = jnp.where(position_column > row_index[:, None], jnp.exp(cumulative), 0.0)
    local_adjoint = transposed_times(c_rows, grad_ssm * entry_weights)
    grad_state = combine_states(local_adjoint, through, -1, reach)

    grad_query_rot, grad_window = attend_backward(
        query_low, key_window, value_window, positions, totals, grad_attended_low
    )
    own_grad = grad_window[reach * tokens :]
    for steps in range(1, reach + 1):
        part = grad_window[(reach - steps) * tokens : (reach - steps + 1) * tokens]
        own_grad = own_grad + shift_teams(part.astype(BF16), -steps).astype(F32)
    distance = 1
    while distance < SHARE:
        own_grad = own_grad + peer(own_grad, distance)
        distance *= 2
    grad_query_low = rotate(grad_query_rot, cosine, -sine_vals).astype(BF16)
    grad_key_low = rotate(own_grad[:, :HD], cosine, -sine_vals).astype(BF16)
    grad_value_low = own_grad[:, HD:].astype(BF16)

    early_low = jnp.concatenate([grad_z_low, grad_query_low, grad_key_low, grad_value_low], axis=1)
    early_sums = transposed_times(ordered_normed, early_low).astype(BF16)
    early_sums = scatter_step(early_sums, first_level())
    grad_core = scan_backward(
        inputs, b_rows, c_rows, step_sizes, log_decay, position_column,
        jax.nn.sigmoid(raw_steps), rate_of_head[None], skip_wide[None], entering, grad_ssm,
        grad_state,
    )
    grad_inputs, grad_b, grad_c, grad_dt_raw, head_sums, skip_sums = grad_core
    grad_skip = jnp.sum(skip_sums.reshape(HEADS, HD), axis=1)
    grad_log_rates, grad_step_bias = head_sums[0], head_sums[1]
    grad_bc = jnp.concatenate([grad_b, grad_c], axis=1)
    for bit in reversed(range(BITS)):
        half = grad_bc.shape[1] // 2
        low_half, high_half = grad_bc[:, :half], grad_bc[:, half:]
        first = member_bit(bit) == 0
        kept = jnp.where(first, low_half, high_half)
        sent = jnp.where(first, high_half, low_half).astype(BF16)
        grad_bc = kept + peer(sent, 1 << bit).astype(F32)

    conv_padded = jnp.concatenate([padded[:, :CX], my_slice(padded[:, CX:], CB)], axis=1)
    conv_taps = jnp.concatenate([taps[:, :CX], my_slice(taps[:, CX:], CB)], axis=1)
    conv_shift = jnp.concatenate([bias[:CX], my_slice(bias[CX:], CB)], axis=0)
    _, conv_back = jax.vjp(
        lambda rows, weights, offset: causal_conv(rows, weights, offset, positions),
        conv_padded, conv_taps, conv_shift,
    )
    grad_padded, grad_taps, grad_shift = conv_back(
        jnp.concatenate([grad_inputs, grad_bc], axis=1)
    )
    returned_rim = shift_teams(grad_padded[: KCONV - 1], -1)
    grad_conv = grad_padded[KCONV - 1 :]
    grad_conv = jnp.concatenate(
        [grad_conv[: tokens - (KCONV - 1)], grad_conv[tokens - (KCONV - 1) :] + returned_rim],
        axis=0,
    )
    grad_conv, early_sums = tied(grad_conv, early_sums)
    if later_levels()[:-1]:
        early_sums = scatter_step(early_sums, later_levels()[0])
    grad_conv_low = grad_conv.astype(BF16)
    grad_dt_low = grad_dt_raw.astype(BF16)

    shared = 1.0 / SHARE
    late_low = jnp.concatenate([grad_conv_low, grad_dt_low], axis=1)
    late_sums = transposed_times(ordered_normed, late_low).astype(BF16)
    late_sums, main_one = tied(late_sums, main_one)
    late_sums = scatter_step(late_sums, first_level())
    grad_bc_low = grad_conv_low[:, CX:]
    owner = jnp.arange(2 * NST) // CB
    wide_bc = jnp.where(owner == me, jnp.concatenate([grad_bc_low] * TEAM, axis=1), BF16(0.0))
    all_low = jnp.concatenate(
        [
            grad_z_low,
            grad_conv_low[:, :CX],
            wide_bc,
            grad_query_low,
            grad_key_low * BF16(shared),
            grad_value_low * BF16(shared),
            grad_dt_low,
        ],
        axis=1,
    )
    back_weights = main_one
    grad_normed_part = times_transposed(all_low, back_weights)
    grad_normed_part, late_sums, first_summed = lax.optimization_barrier(
        (grad_normed_part, late_sums, first_summed)
    )
    first_grads = hand_out(first_summed)
    if later_levels()[:-1]:
        late_sums = scatter_step(late_sums, later_levels()[0])
    gain_sums = jnp.sum(grad_normed_part * scaled_in, axis=0)
    grad_normed = team_scatter(reorder(grad_normed_part, False))
    grad_normed, late_sums = tied(grad_normed, late_sums)
    last_sums = jnp.concatenate([early_sums, late_sums], axis=1)
    for level in later_levels()[:-1][1:] + later_levels()[-1:]:
        last_sums = scatter_step(last_sums, level)
    last_grads = hand_out(last_sums)
    own_in = layer_in.astype(F32)
    inverse_one = lax.rsqrt(jnp.mean(own_in * own_in, axis=-1, keepdims=True) + EPS)
    own_scaled = own_in * inverse_one
    pulled_one = grad_normed * gain_one
    grad_in = grad_middle + inverse_one * (
        pulled_one - own_scaled * jnp.mean(pulled_one * own_scaled, axis=-1, keepdims=True)
    )

    small = jnp.concatenate(
        [
            grad_taps.reshape(-1),
            grad_shift,
            grad_log_rates,
            grad_step_bias,
            grad_skip,
            grad_gain_two,
            gain_sums,
        ]
    )
    small = reorder_rows(team_gather(sum_across_teams(small)[None]))
    gains = jnp.sum(small[:, -2 * D :], axis=0)
    small = small[:, : -2 * D]
    gain_rows = norm_gain.shape[0]
    at_gain = device_index() * gain_rows
    grad_ffn_gain = lax.dynamic_slice_in_dim(gains[:D], at_gain, gain_rows, 0)
    grad_norm_gain = lax.dynamic_slice_in_dim(gains[D:], at_gain, gain_rows, 0)
    width = CX + CB
    taps_all = small[:, : KCONV * width].reshape(TEAM, KCONV, width)
    shift_all = small[:, KCONV * width : (KCONV + 1) * width]
    rest = small[:, (KCONV + 1) * width :].reshape(TEAM, 3, HEADS)
    grad_conv_weight = jnp.concatenate(
        [
            taps_all[:, :, :CX].transpose(1, 0, 2).reshape(KCONV, DI),
            taps_all[:, :, CX:].transpose(1, 0, 2).reshape(KCONV, 2 * NST),
        ],
        axis=1,
    )
    grad_conv_bias = jnp.concatenate([shift_all[:, :CX].reshape(-1), shift_all[:, CX:].reshape(-1)])
    grad_a_log = rest[:, 0].reshape(-1)
    grad_dt_bias = rest[:, 1].reshape(-1)
    grad_d_skip = rest[:, 2].reshape(-1)

    base = 3 * CF + CX
    grad_gate, grad_up, grad_down, grad_out_proj, grad_attn_out = place(
        [first_grads],
        [
            (0, 0, CF, 0, 0),
            (0, CF, 2 * CF, 1, 0),
            (0, 2 * CF, 3 * CF, 2, 0),
            (0, 3 * CF, base, 3, 0),
            (0, base, base + CQ, 4, 0),
        ],
        [FF, FF, FF, DI, AH * HD],
        [1, 1, 1, 1, 1],
    )
    keys_at = CX + CQ
    late_at = keys_at + 2 * HD
    grad_in_proj, grad_query, grad_key, grad_value = place(
        [last_grads],
        [
            (0, 0, CX, 0, 0),
            (0, late_at, late_at + CX, 0, DI),
            (0, late_at + CX, late_at + CX + CB, 0, 2 * DI),
            (0, late_at + CX + CB, late_at + CX + CB + HEADS, 0, 2 * DI + 2 * NST),
            (0, CX, keys_at, 1, 0),
            (0, keys_at, keys_at + HD, 2, 0),
            (0, keys_at + HD, late_at, 3, 0),
        ],
        [in_proj.shape[1], AH * HD, KVH * HD, KVH * HD],
        [1, 1, SHARE, SHARE],
    )
    grad_down = grad_down.T
    grad_out_proj = grad_out_proj.T
    grad_attn_out = grad_attn_out.T
    return (
        layer_out,
        grad_in,
        grad_norm_gain,
        grad_in_proj,
        grad_query,
        grad_key,
        grad_value,
        grad_out_proj,
        grad_attn_out,
        grad_ffn_gain,
        grad_gate,
        grad_up,
        grad_down,
        grad_conv_weight,
        grad_conv_bias,
        grad_a_log,
        grad_dt_bias,
        grad_d_skip,
    )


def solution(mesh):
    rows = P("dp", None)
    columns = P(None, "dp")
    in_specs = (
        (rows, rows, P("dp"), P("dp"), rows, rows, rows, rows, columns, columns)
        + (P("dp"), rows, rows, columns)
        + (P(),) * 5
    )
    out_specs = (
        (rows, rows, P("dp"), rows, rows, rows, rows, columns, columns)
        + (P("dp"), rows, rows, columns)
        + (P(),) * 5
    )
    return jax.shard_map(body, mesh=mesh, in_specs=in_specs, out_specs=out_specs, check_vma=False)
```

```python
import functools

import jax
import jax.numpy as jnp
from jax import lax
from jax.experimental import pallas as pl
from jax.experimental.pallas import tpu as pltpu
from jax.sharding import PartitionSpec as P

D = 1024
MH = 24
HD = 64
NST = 128
KCONV = 4
AH = 8
KVH = 2
FF = 2048
CHUNK = 128
DI = 1536
CONVCH = 1792
SEQ = 2048

EPS = 1e-05
ROPE_BASE = 10000.0

TEAM = 4
BITS = TEAM.bit_length() - 1
HEADS = MH // TEAM
CX = HEADS * HD
QH = AH // TEAM
CQ = QH * HD
CF = FF // TEAM
SHARE = TEAM // KVH
CB = 2 * NST // TEAM

F32 = jnp.float32
BF16 = jnp.bfloat16


def product(first_arg, second_arg):
    return jnp.dot(first_arg, second_arg, preferred_element_type=F32)


def times_transposed(first_arg, second_arg):
    return lax.dot_general(
        first_arg, second_arg, (((1,), (1,)), ((), ())), preferred_element_type=F32
    )


def transposed_times(first_arg, second_arg):
    return lax.dot_general(
        first_arg, second_arg, (((0,), (0,)), ((), ())), preferred_element_type=F32
    )


def device_index():
    return lax.axis_index("dp")


def member():
    return device_index() % TEAM


def member_bit(bit):
    return (device_index() >> bit) & 1


def peer(value, distance):
    count = lax.axis_size("dp")
    return lax.ppermute(value, "dp", [(i, i ^ distance) for i in range(count)])


def shift_teams(value, steps):
    count = lax.axis_size("dp")
    offset = steps * TEAM
    first, last = (max(0, -offset), min(count, count - offset))
    return lax.ppermute(value, "dp", [(i, i + offset) for i in range(first, last)])


def team_gather(value):
    for bit in reversed(range(BITS)):
        value = jnp.concatenate([value, peer(value, 1 << bit)], axis=0)
    return value


def team_scatter(partial):
    for bit in range(BITS):
        half = partial.shape[0] // 2
        arrived = peer(partial[half:].astype(BF16), 1 << bit)
        partial = partial[:half] + arrived.astype(F32)
    return partial


def reversed_bits(value):
    result = 0
    for bit in range(BITS):
        result = result | (((value >> bit) & 1) << (BITS - 1 - bit))
    return result


def reorder_kernel(to_seq, index_ref, from_ref, to_ref):
    rows = from_ref.shape[0] // TEAM
    me = index_ref[0]
    for block in range(TEAM):
        if to_seq:
            source = reversed_bits(me ^ block)
        else:
            source = me ^ reversed_bits(block)
        start = pl.multiple_of(source * rows, rows)
        to_ref[block * rows : (block + 1) * rows, :] = from_ref[pl.ds(start, rows), :]


def reorder(value, to_seq):
    whole = pl.BlockSpec(memory_space=pltpu.VMEM)
    return pl.pallas_call(
        functools.partial(reorder_kernel, to_seq),
        in_specs=[pl.BlockSpec(memory_space=pltpu.SMEM), whole],
        out_specs=whole,
        out_shape=jax.ShapeDtypeStruct(value.shape, value.dtype),
        compiler_params=pltpu.CompilerParams(vmem_limit_bytes=32 << 20),
    )(member()[None].astype(jnp.int32), value)


def member_order(pieces):
    for bit in range(BITS):
        split = pieces.reshape((TEAM >> (bit + 1), 2, 1 << bit) + pieces.shape[1:])
        flipped = jnp.concatenate([split[:, 1:], split[:, :1]], axis=1)
        pieces = jnp.where(member_bit(bit) == 0, split, flipped).reshape(pieces.shape)
    return pieces


def reorder_rows(rows):
    order = [0]
    for bit in reversed(range(BITS)):
        order = order + [k | (1 << bit) for k in order]
    return member_order(jnp.stack([rows[order.index(k)] for k in range(TEAM)]))


def team_exchange(pieces):
    relative = member_order(pieces)
    arrived = [relative[0]] + [peer(relative[k], k) for k in range(1, TEAM)]
    return member_order(jnp.stack(arrived))


def across_groups():
    count = lax.axis_size("dp")
    return [list(range(first, count, TEAM)) for first in range(TEAM)]


def exchanged_rows(pieces):
    rows = team_exchange(pieces)
    return rows.reshape((-1, rows.shape[-1]))


def gather_rows(rows):
    return lax.all_gather(rows, "dp", axis=0, tiled=True, axis_index_groups=across_groups())


def first_level():
    rows = D // (lax.axis_size("dp") // TEAM)
    return max(0, (CHUNK // rows).bit_length() - 1)


def later_levels():
    levels = (lax.axis_size("dp") // TEAM).bit_length() - 1
    first = first_level()
    return list(range(levels - 1, first, -1)) + list(range(first - 1, -1, -1))


def split_order(columns):
    blocks = (lax.axis_size("dp") // TEAM) >> first_level()
    width = columns.shape[1] // blocks
    parts = [columns[:, b * width : (b + 1) * width] for b in range(blocks)]
    return jnp.concatenate(parts[::2] + parts[1::2], axis=1)


def sum_rows(matrix):
    return lax.psum_scatter(
        matrix, "dp", scatter_dimension=0, tiled=True, axis_index_groups=across_groups()
    )


def scatter_step(blocks, level):
    half = blocks.shape[0] // 2
    mine = member_bit(BITS + level)
    kept = lax.dynamic_slice_in_dim(blocks, mine * half, half, 0)
    sent = lax.dynamic_slice_in_dim(blocks, (1 - mine) * half, half, 0)
    arrived = peer(sent, TEAM << level)
    return (kept.astype(F32) + arrived.astype(F32)).astype(BF16)


def tied(first, second):
    return lax.optimization_barrier((first, second))


def hand_out(summed):
    rows = summed.shape[0] // TEAM
    arrived = []
    for k in range(TEAM):
        piece = lax.dynamic_slice_in_dim(summed, (member() ^ k) * rows, rows, 0)
        arrived.append(piece if k == 0 else peer(piece, k))
    return arrived


def place_kernel(plan, index_ref, *refs):
    outs = refs[len(refs) - plan["outs"] :]
    me = index_ref[0]
    for k in range(TEAM):
        for source in range(TEAM):

            @pl.when((me ^ k) == source)
            def _():
                for group, first, stop, out, column in plan["moves"]:
                    piece = refs[group * TEAM + k]
                    share = plan["share"][out]
                    if source % share == 0:
                        at = column + (source // share) * (stop - first)
                        outs[out][:, at : at + stop - first] = piece[:, first:stop].astype(F32)


def place(groups, moves, widths, share):
    plan = {"moves": moves, "outs": len(widths), "share": share}
    rows = groups[0][0].shape[0]
    operands = [piece for group in groups for piece in group]
    return pl.pallas_call(
        functools.partial(place_kernel, plan),
        out_shape=[jax.ShapeDtypeStruct((rows, width), F32) for width in widths],
        in_specs=[pl.BlockSpec(memory_space=pltpu.SMEM)]
        + [pl.BlockSpec(memory_space=pltpu.VMEM)] * len(operands),
        out_specs=[pl.BlockSpec(memory_space=pltpu.VMEM)] * len(widths),
    )(member()[None].astype(jnp.int32), *operands)


def sum_across_teams(vector):
    count = lax.axis_size("dp")
    distance = TEAM
    while distance < count:
        vector = vector + peer(vector, distance)
        distance *= 2
    return vector


def columns_of(matrix, index, width):
    return lax.slice_in_dim(matrix, index * width, (index + 1) * width, axis=1)


def my_slice(array, width, axis=-1):
    axis = axis % array.ndim
    return lax.dynamic_slice_in_dim(array, member() * width, width, axis)


def rotate(values, cosine, sine_vals):
    half_dim = HD // 2
    rows = values.shape[0]
    heads = values.reshape(rows, -1, HD)
    first_half = heads[..., :half_dim]
    second_half = heads[..., half_dim:]
    cosine = cosine[:, None, :]
    sine_vals = sine_vals[:, None, :]
    return jnp.concatenate(
        [
            first_half * cosine - second_half * sine_vals,
            second_half * cosine + first_half * sine_vals,
        ],
        axis=-1,
    ).reshape(values.shape)


def causal_conv(padded, conv_weight, conv_bias, positions):
    token_count = padded.shape[0] - (KCONV - 1)
    conv_sum = jnp.zeros((token_count, padded.shape[1]), F32) + conv_bias[None, :]
    for tap_index in range(KCONV):
        lag_rows = KCONV - 1 - tap_index
        shifted = padded[tap_index : tap_index + token_count] * conv_weight[tap_index][None, :]
        conv_sum = conv_sum + jnp.where((positions >= lag_rows)[:, None], shifted, 0.0)
    return jax.nn.silu(conv_sum)


def head_spread():
    head = lax.broadcasted_iota(jnp.int32, (HEADS, CX), 0)
    channel = lax.broadcasted_iota(jnp.int32, (HEADS, CX), 1)
    return jnp.where(channel // HD == head, 1.0, 0.0).astype(F32)


def exact(first_arg, second_arg, dims=((1,), (0,))):
    return lax.dot_general(
        first_arg,
        second_arg,
        (dims, ((), ())),
        precision=lax.Precision.HIGHEST,
        preferred_element_type=F32,
    )


def chunk_terms(decay, step, positions):
    row = lax.broadcasted_iota(jnp.int32, (CHUNK, CHUNK), 0)
    col = lax.broadcasted_iota(jnp.int32, (CHUNK, CHUNK), 1)
    inside = (col <= row) & (col >= row - positions)
    lower = jnp.where(col <= row, 1.0, 0.0).astype(F32)
    cumulative = exact(lower, decay)
    cumulative_rows = exact(decay, lower, ((0,), (1,)))
    spread = head_spread()
    wide = exact(cumulative, spread)
    step_wide = exact(step, spread)
    index = lax.broadcasted_iota(jnp.int32, (CHUNK, 1), 0)
    final = CHUNK - 1
    final_position = positions[final:, :]
    final_sum = wide[final:, :]
    carried = jnp.where(positions > index, jnp.exp(wide), 0.0)
    fade = jnp.where(index >= final - final_position, jnp.exp(final_sum - wide), 0.0)
    keep = jnp.where(final_position > final, jnp.exp(final_sum), 0.0)
    return inside, lower, cumulative, cumulative_rows, spread, step_wide, carried, fade, keep


def head_decay(inside, cumulative, cumulative_rows, head):
    gap = cumulative[:, head : head + 1] - cumulative_rows[head : head + 1, :]
    return jnp.exp(jnp.where(inside, gap, -1e30))


def scan_forward_kernel(
    x_ref, b_ref, c_ref, step_ref, decay_ref, pos_ref, start_ref, y_ref, enter_ref, state_ref
):
    @pl.when(pl.program_id(0) == 0)
    def _():
        state_ref[...] = start_ref[...]

    terms = chunk_terms(decay_ref[...], step_ref[...], pos_ref[...])
    inside, _, cumulative, cumulative_rows, _, step_wide, carried, fade, keep = terms
    scaled = x_ref[...] * step_wide
    scaled_low = scaled.astype(BF16)
    b_low = b_ref[...].astype(BF16)
    c_low = c_ref[...].astype(BF16)
    inner = times_transposed(c_low, b_low)
    state = state_ref[...]
    enter_ref[0] = state
    far = product(c_low, state.astype(BF16)) * carried
    first_half = lax.broadcasted_iota(jnp.int32, (CHUNK, 2 * HD), 1) < HD
    for pair in range(HEADS // 2):
        lanes = slice(pair * 2 * HD, (pair + 1) * 2 * HD)
        near = [
            product(
                (head_decay(inside, cumulative, cumulative_rows, head) * inner).astype(BF16),
                scaled_low[:, lanes],
            )
            for head in (2 * pair, 2 * pair + 1)
        ]
        y_ref[:, lanes] = jnp.where(first_half, near[0], near[1]) + far[:, lanes]
    state_ref[...] = state * keep + transposed_times(b_low, (scaled * fade).astype(BF16))


def scan_specs(blocks, reverse):
    def at(block):
        return blocks - 1 - block if reverse else block

    def rows(width):
        return pl.BlockSpec((CHUNK, width), lambda block: (at(block), 0))

    whole = pl.BlockSpec((NST, CX), lambda block: (0, 0))
    entering = pl.BlockSpec((1, NST, CX), lambda block: (at(block), 0, 0))
    return rows, whole, entering


def scan_forward(inputs, b_rows, c_rows, step_sizes, log_decay, positions, state_in):
    tokens = inputs.shape[0]
    blocks = tokens // CHUNK
    rows, whole, entering = scan_specs(blocks, False)
    return pl.pallas_call(
        scan_forward_kernel,
        grid=(blocks,),
        in_specs=[rows(CX), rows(NST), rows(NST), rows(HEADS), rows(HEADS), rows(1), whole],
        out_specs=[rows(CX), entering],
        out_shape=[
            jax.ShapeDtypeStruct((tokens, CX), F32),
            jax.ShapeDtypeStruct((blocks, NST, CX), F32),
        ],
        scratch_shapes=[pltpu.VMEM((NST, CX), F32)],
        cost_estimate=pl.CostEstimate(flops=300000000, bytes_accessed=4000000, transcendentals=500000),
    )(inputs, b_rows, c_rows, step_sizes, log_decay, positions, state_in)


def scan_backward_kernel(
    x_ref, b_ref, c_ref, step_ref, decay_ref, pos_ref, slope_ref, rate_ref, skip_ref, enter_ref,
    grad_ref, end_ref, gx_ref, gb_ref, gc_ref, gdt_ref, gsums_ref, gskip_ref, adjoint_ref,
):
    @pl.when(pl.program_id(0) == 0)
    def _():
        adjoint_ref[...] = end_ref[...]
        gsums_ref[...] = jnp.zeros_like(gsums_ref)
        gskip_ref[...] = jnp.zeros_like(gskip_ref)

    step = step_ref[...]
    decay = decay_ref[...]
    terms = chunk_terms(decay, step, pos_ref[...])
    inside, lower, cumulative, cumulative_rows, spread, step_wide, carried, fade, keep = terms
    x = x_ref[...]
    grad = grad_ref[...]
    scaled = x * step_wide
    scaled_low = scaled.astype(BF16)
    grad_low = grad.astype(BF16)
    b_low = b_ref[...].astype(BF16)
    c_low = c_ref[...].astype(BF16)
    inner = times_transposed(c_low, b_low)
    state = enter_ref[0]
    state_low = state.astype(BF16)
    adjoint = adjoint_ref[...]
    adjoint_low = adjoint.astype(BF16)

    lane = lax.broadcasted_iota(jnp.int32, (CHUNK, 2 * HD), 1)
    inner_grad = jnp.zeros((CHUNK, CHUNK), F32)
    sum_grad = jnp.zeros((CHUNK, HEADS), F32)
    spot = lax.broadcasted_iota(jnp.int32, (CHUNK, HEADS), 1)
    near_parts = []
    for pair in range(HEADS // 2):
        lanes = slice(pair * 2 * HD, (pair + 1) * 2 * HD)
        grad_pair = grad_low[:, lanes]
        scaled_pair = scaled_low[:, lanes]
        near = []
        for half in range(2):
            head = 2 * pair + half
            fall = head_decay(inside, cumulative, cumulative_rows, head)
            mixed = fall * inner
            mine = (lane // HD) == half
            mixed_grad = times_transposed(jnp.where(mine, grad_pair, BF16(0.0)), scaled_pair)
            inner_grad = inner_grad + mixed_grad * fall
            weight_low = (mixed_grad * mixed).astype(BF16)
            pick = jnp.where(spot == head, 1.0, 0.0).astype(BF16)
            sum_grad = sum_grad + product(weight_low, pick) - transposed_times(weight_low, pick)
            near.append(transposed_times(mixed.astype(BF16), grad_pair))
        near_parts.append(jnp.where(lane < HD, near[0], near[1]))
    near_grad = jnp.concatenate(near_parts, axis=1)
    inner_grad_low = inner_grad.astype(BF16)

    carried_grad = grad * carried
    carried_low = carried_grad.astype(BF16)
    far_term = carried_grad * product(c_low, state_low)
    faded = scaled * fade
    reached = product(b_low, adjoint_low)
    tail_term = faded * reached
    scaled_grad = near_grad + fade * reached
    keep_term = jnp.sum(adjoint * state, axis=0, keepdims=True) * keep
    final_term = keep_term + jnp.sum(tail_term, axis=0, keepdims=True)
    final_row = lax.broadcasted_iota(jnp.int32, (CHUNK, 1), 0) == CHUNK - 1
    wide_term = far_term - tail_term + jnp.where(final_row, final_term, 0.0)
    sum_grad = sum_grad + exact(wide_term, spread, ((1,), (1,)))
    decay_grad = exact(lower, sum_grad, ((0,), (0,)))
    step_grad = exact(scaled_grad * x, spread, ((1,), (1,)))
    dt_grad = (step_grad - decay_grad * rate_ref[...]) * slope_ref[...]

    gx_ref[...] = scaled_grad * step_wide + skip_ref[...] * grad
    gb_ref[...] = transposed_times(inner_grad_low, c_low) + times_transposed(
        faded.astype(BF16), adjoint_low
    )
    gc_ref[...] = product(inner_grad_low, b_low) + times_transposed(carried_low, state_low)
    gdt_ref[...] = dt_grad
    gsums_ref[0:1, :] += jnp.sum(decay_grad * decay, axis=0, keepdims=True)
    gsums_ref[1:2, :] += jnp.sum(dt_grad, axis=0, keepdims=True)
    gskip_ref[...] += jnp.sum(grad * x, axis=0, keepdims=True)
    adjoint_ref[...] = adjoint * keep + transposed_times(c_low, carried_low)


def scan_backward(
    inputs, b_rows, c_rows, step_sizes, log_decay, positions, slopes, rates, skip, entering, grad,
    grad_end,
):
    tokens = inputs.shape[0]
    blocks = tokens // CHUNK
    rows, whole, enter = scan_specs(blocks, True)

    def fixed(first, second):
        return pl.BlockSpec((first, second), lambda block: (0, 0))

    shapes = [(tokens, CX), (tokens, NST), (tokens, NST), (tokens, HEADS), (2, HEADS), (1, CX)]
    return pl.pallas_call(
        scan_backward_kernel,
        grid=(blocks,),
        in_specs=[rows(CX), rows(NST), rows(NST), rows(HEADS), rows(HEADS), rows(1), rows(HEADS)]
        + [fixed(1, HEADS), fixed(1, CX), enter, rows(CX), whole],
        out_specs=[rows(CX), rows(NST), rows(NST), rows(HEADS), fixed(2, HEADS), fixed(1, CX)],
        out_shape=[jax.ShapeDtypeStruct(shape, F32) for shape in shapes],
        scratch_shapes=[pltpu.VMEM((NST, CX), F32)],
        cost_estimate=pl.CostEstimate(flops=1000000, bytes_accessed=100000, transcendentals=0),
    )(
        inputs, b_rows, c_rows, step_sizes, log_decay, positions, slopes, rates, skip, entering,
        grad, grad_end,
    )


def combine_states(own, rate, steps, reach):
    coarse = rate.astype(BF16)
    fine = (rate - coarse.astype(F32)).astype(BF16)
    flat = jnp.concatenate(
        [own.astype(BF16), jnp.broadcast_to(coarse, (8, CX)), jnp.broadcast_to(fine, (8, CX))], axis=0
    )
    total = None
    through = None
    for distance in range(1, reach + 1):
        arrived = shift_teams(flat, steps * distance).astype(F32)
        state = arrived[:NST]
        their_rate = arrived[NST : NST + 1] + arrived[NST + 8 : NST + 9]
        if total is None:
            total, through = state, their_rate
        else:
            total = total + through * state
            through = through * their_rate
    return total


def masked_scores(query_low, key_low, positions):
    row_count = query_low.shape[0]
    span_rows = key_low.shape[0]
    grouped = query_low.reshape(row_count, QH, HD)
    scores = jnp.einsum("sjd,td->jst", grouped, key_low, preferred_element_type=F32) * HD ** (-0.5)
    q_index = span_rows - row_count + jnp.arange(row_count)
    k_index = jnp.arange(span_rows)
    visible = (k_index[None, :] <= q_index[:, None]) & (
        k_index[None, :] >= (q_index - positions)[:, None]
    )
    return jnp.where(visible, scores, -1e30), grouped


def attend_forward(query_low, key_low, value_low, positions):
    scores, _ = masked_scores(query_low, key_low, positions)
    totals = jax.nn.logsumexp(scores, axis=-1, keepdims=True)
    weights_low = jnp.exp(scores - totals).astype(BF16)
    attended = jnp.einsum("jst,td->sjd", weights_low, value_low, preferred_element_type=F32)
    return attended.reshape(query_low.shape[0], CQ), totals


def attend_backward(query_low, key_low, value_low, positions, totals, grad_attended_low):
    scores, grouped = masked_scores(query_low, key_low, positions)
    row_count = query_low.shape[0]
    weights_full = jnp.exp(scores - totals)
    weights_low = weights_full.astype(BF16)
    grad_grouped = grad_attended_low.reshape(row_count, QH, HD)
    grad_weights = jnp.einsum(
        "sjd,td->jst", grad_grouped, value_low, preferred_element_type=F32
    )
    row_sums = jnp.sum(weights_full * grad_weights, axis=-1, keepdims=True)
    grad_scores = (weights_full * (grad_weights - row_sums)).astype(BF16)
    scale = HD ** (-0.5)
    grad_query = jnp.einsum("jst,td->sjd", grad_scores, key_low, preferred_element_type=F32) * scale
    grad_keys = jnp.einsum("jst,sjd->td", grad_scores, grouped, preferred_element_type=F32) * scale
    grad_values = jnp.einsum("jst,sjd->td", weights_low, grad_grouped, preferred_element_type=F32)
    return grad_query.reshape(row_count, CQ), jnp.concatenate([grad_keys, grad_values], axis=1)


def silu_slope(value):
    chance = jax.nn.sigmoid(value)
    return chance * (1.0 + value * (1.0 - chance))


def body(
    layer_in,
    cotangent,
    doc_positions,
    norm_gain,
    in_proj,
    w_query,
    w_key,
    w_value,
    out_proj,
    w_attn_out,
    ffn_gain,
    w_gate,
    w_up,
    w_down,
    conv_weight,
    conv_bias,
    a_log,
    dt_bias,
    d_skip,
):
    me = member()
    kv_mine = me // SHARE
    bc_cols = in_proj[:, 2 * DI : 2 * DI + 2 * NST]
    dt_cols = in_proj[:, DI + CONVCH :]
    first_pieces = jnp.stack(
        [
            jnp.concatenate(
                [
                    columns_of(in_proj[:, :DI], r, CX),
                    columns_of(in_proj[:, DI : 2 * DI], r, CX),
                    bc_cols,
                    columns_of(w_query, r, CQ),
                    columns_of(w_key, r // SHARE, HD),
                    columns_of(w_value, r // SHARE, HD),
                    columns_of(dt_cols, r, HEADS),
                    norm_gain[:, None],
                    ffn_gain[:, None],
                ],
                axis=1,
            )
            for r in range(TEAM)
        ]
    )
    out_rows = out_proj.T
    attn_rows = w_attn_out.T
    down_rows = w_down.T
    second_pieces = jnp.stack(
        [
            jnp.concatenate(
                [
                    columns_of(out_rows, r, CX),
                    columns_of(attn_rows, r, CQ),
                    columns_of(w_gate, r, CF),
                    columns_of(w_up, r, CF),
                    columns_of(down_rows, r, CF),
                ],
                axis=1,
            )
            for r in range(TEAM)
        ]
    )
    rows_one = gather_rows(exchanged_rows(first_pieces))
    rows_two = gather_rows(exchanged_rows(second_pieces))
    coarse = (doc_positions // 64).astype(BF16)[:, None]
    fine = (doc_positions % 64).astype(BF16)[:, None]
    spots = jnp.concatenate([coarse, fine, jnp.zeros((layer_in.shape[0], 126), BF16)], axis=1)
    team_start = team_gather(jnp.concatenate([layer_in, spots, cotangent], axis=1))
    team_top = team_start[:, D + 128 :]
    team_start = reorder(team_start[:, : D + 128], True)
    team_in = team_start[:, :D]
    spots = team_start[:, D : D + 2].astype(F32)
    position_column = (spots[:, :1] * 64.0 + spots[:, 1:]).astype(jnp.int32)
    positions = position_column[:, 0]

    z_end = CX
    x_end = 2 * CX
    bc_end = x_end + 2 * NST
    q_end = bc_end + CQ
    kv_end = q_end + 2 * HD
    dt_end = kv_end + HEADS
    main_one = rows_one[:, :dt_end]
    gain_one = rows_one[:, dt_end].astype(F32)
    mix_weights = rows_two[:, : CX + CQ]
    ffn_weights = rows_two[:, CX + CQ : CX + CQ + 2 * CF]
    down_weights = rows_two[:, CX + CQ + 2 * CF : CX + CQ + 3 * CF]
    gain_two = rows_one[:, dt_end + 1].astype(F32)

    tokens = team_in.shape[0]
    row_count = layer_in.shape[0]
    reach = SEQ // tokens - 1
    last = tokens - 1

    wide_in = team_in.astype(F32)
    scaled_in = wide_in * lax.rsqrt(jnp.mean(wide_in * wide_in, axis=-1, keepdims=True) + EPS)
    normed_low = (scaled_in * gain_one).astype(BF16)
    ordered_normed = split_order(normed_low)
    gate_z = product(normed_low, main_one[:, :z_end])
    conv_low = product(normed_low, main_one[:, z_end:bc_end]).astype(BF16)
    projected = product(normed_low, main_one[:, bc_end:])

    half_dim = HD // 2
    frequency = ROPE_BASE ** (-jnp.arange(half_dim, dtype=F32) / half_dim)
    angles = positions.astype(F32)[:, None] * frequency[None, :]
    cosine = jnp.cos(angles)
    sine_vals = jnp.sin(angles)

    rim_rows = shift_teams(conv_low[tokens - (KCONV - 1) :], 1)
    query_low = rotate(projected[:, :CQ], cosine, sine_vals).astype(BF16)
    key_low = rotate(projected[:, CQ : CQ + HD], cosine, sine_vals).astype(BF16)
    value_low = projected[:, CQ + HD : CQ + 2 * HD].astype(BF16)
    dt_raw = projected[:, CQ + 2 * HD :]
    own_window = jnp.concatenate([key_low, value_low], axis=1)
    window = jnp.concatenate(
        [shift_teams(own_window, steps) for steps in range(reach, 0, -1)] + [own_window], axis=0
    )
    key_window = window[:, :HD]
    value_window = window[:, HD:]

    taps_x = my_slice(conv_weight[:, :DI], CX)
    bias_x = my_slice(conv_bias[:DI], CX)
    taps = jnp.concatenate([taps_x, conv_weight[:, DI:]], axis=1)
    bias = jnp.concatenate([bias_x, conv_bias[DI:]], axis=0)
    my_log_rates = my_slice(a_log, HEADS)
    my_dt_bias = my_slice(dt_bias, HEADS)
    my_skip = my_slice(d_skip, HEADS)
    skip_wide = jnp.repeat(my_skip, HD)

    padded = jnp.concatenate([rim_rows, conv_low], axis=0).astype(F32)
    conv_out = causal_conv(padded, taps, bias, positions)
    inputs = conv_out[:, :CX]
    b_rows = conv_out[:, CX : CX + NST]
    c_rows = conv_out[:, CX + NST :]

    raw_steps = dt_raw + my_dt_bias
    rate_of_head = jnp.exp(my_log_rates)
    step_sizes = jax.nn.softplus(raw_steps)
    log_decay = -step_sizes * rate_of_head
    row_index = jnp.arange(tokens)
    earlier = jnp.where(row_index[None, :] <= row_index[:, None], 1.0, 0.0).astype(F32)
    cumulative = jnp.repeat(exact(earlier, log_decay), HD, axis=1)
    tail_mask = jnp.where(row_index >= last - positions[last], 1.0, 0.0)
    fade_weights = jnp.exp(cumulative[last:] - cumulative) * tail_mask[:, None]
    scaled_inputs = inputs * jnp.repeat(step_sizes, HD, axis=1) * fade_weights
    local_state = transposed_times(b_rows, scaled_inputs)
    through = jnp.where(positions[last] > last, jnp.exp(cumulative[last:]), 0.0)
    state_in = combine_states(local_state, through, 1, reach)

    attended, totals = attend_forward(query_low, key_window, value_window, positions)
    attended_low = attended.astype(BF16)

    scanned, entering = scan_forward(
        inputs, b_rows, c_rows, step_sizes, log_decay, position_column, state_in
    )
    ssm_out = scanned + skip_wide * inputs
    silu_z = jax.nn.silu(gate_z)
    gated_low = (ssm_out * silu_z).astype(BF16)
    mixed_low = jnp.concatenate([gated_low, attended_low], axis=1)
    mixed_low = reorder(mixed_low, False)
    branches = team_scatter(times_transposed(mixed_low, mix_weights))
    middle = layer_in.astype(F32) + branches
    inverse_two = lax.rsqrt(jnp.mean(middle * middle, axis=-1, keepdims=True) + EPS)
    scaled_two = middle * inverse_two
    normed_two = team_gather((scaled_two * gain_two).astype(BF16))
    gate_up = product(normed_two, ffn_weights)
    gate_value = gate_up[:, :CF]
    up_value = gate_up[:, CF:]
    silu_gate = jax.nn.silu(gate_value)
    hidden_low = (silu_gate * up_value).astype(BF16)
    layer_out = (middle + team_scatter(times_transposed(hidden_low, down_weights))).astype(BF16)

    grad_hidden = product(team_top, down_weights)
    grad_gate_up = jnp.concatenate(
        [grad_hidden * up_value * silu_slope(gate_value), grad_hidden * silu_gate], axis=1
    ).astype(BF16)
    grad_normed_two = team_scatter(times_transposed(grad_gate_up, ffn_weights))
    ffn_sums = (transposed_times(normed_two, grad_gate_up), transposed_times(team_top, hidden_low))
    ffn_sums = tuple(part.astype(BF16) for part in ffn_sums)
    grad_normed_two, ffn_sums = tied(grad_normed_two, ffn_sums)
    grad_gain_two = jnp.sum(grad_normed_two * scaled_two, axis=0)
    pulled = grad_normed_two * gain_two
    grad_middle = cotangent.astype(F32) + inverse_two * (
        pulled - scaled_two * jnp.mean(pulled * scaled_two, axis=-1, keepdims=True)
    )
    grad_branch = team_gather(grad_middle.astype(BF16))
    grad_mixed = reorder(product(grad_branch, mix_weights), True)
    branch_sums = transposed_times(grad_branch, mixed_low).astype(BF16)
    first_sums = jnp.concatenate([ffn_sums[0], ffn_sums[1], branch_sums], axis=1)
    grad_mixed, first_sums = tied(grad_mixed, first_sums)
    first_summed = sum_rows(first_sums)
    grad_gated = grad_mixed[:, :CX]
    grad_attended_low = grad_mixed[:, CX:].astype(BF16)
    grad_ssm = grad_gated * silu_z
    grad_z_low = (grad_gated * ssm_out * silu_slope(gate_z)).astype(BF16)

    entry_weights = jnp.where(position_column > row_index[:, None], jnp.exp(cumulative), 0.0)
    local_adjoint = transposed_times(c_rows, grad_ssm * entry_weights)
    grad_state = combine_states(local_adjoint, through, -1, reach)

    grad_query_rot, grad_window = attend_backward(
        query_low, key_window, value_window, positions, totals, grad_attended_low
    )
    own_grad = grad_window[reach * tokens :]
    for steps in range(1, reach + 1):
        part = grad_window[(reach - steps) * tokens : (reach - steps + 1) * tokens]
        own_grad = own_grad + shift_teams(part.astype(BF16), -steps).astype(F32)
    distance = 1
    while distance < SHARE:
        own_grad = own_grad + peer(own_grad, distance)
        distance *= 2
    grad_query_low = rotate(grad_query_rot, cosine, -sine_vals).astype(BF16)
    grad_key_low = rotate(own_grad[:, :HD], cosine, -sine_vals).astype(BF16)
    grad_value_low = own_grad[:, HD:].astype(BF16)

    early_low = jnp.concatenate([grad_z_low, grad_query_low, grad_key_low, grad_value_low], axis=1)
    early_sums = transposed_times(ordered_normed, early_low).astype(BF16)
    early_sums = scatter_step(early_sums, first_level())
    grad_core = scan_backward(
        inputs, b_rows, c_rows, step_sizes, log_decay, position_column,
        jax.nn.sigmoid(raw_steps), rate_of_head[None], skip_wide[None], entering, grad_ssm,
        grad_state,
    )
    grad_inputs, grad_b, grad_c, grad_dt_raw, head_sums, skip_sums = grad_core
    grad_skip = jnp.sum(skip_sums.reshape(HEADS, HD), axis=1)
    grad_log_rates, grad_step_bias = head_sums[0], head_sums[1]
    grad_bc = jnp.concatenate([grad_b, grad_c], axis=1)
    for bit in reversed(range(BITS)):
        half = grad_bc.shape[1] // 2
        low_half, high_half = grad_bc[:, :half], grad_bc[:, half:]
        first = member_bit(bit) == 0
        kept = jnp.where(first, low_half, high_half)
        sent = jnp.where(first, high_half, low_half).astype(BF16)
        grad_bc = kept + peer(sent, 1 << bit).astype(F32)

    conv_padded = jnp.concatenate([padded[:, :CX], my_slice(padded[:, CX:], CB)], axis=1)
    conv_taps = jnp.concatenate([taps[:, :CX], my_slice(taps[:, CX:], CB)], axis=1)
    conv_shift = jnp.concatenate([bias[:CX], my_slice(bias[CX:], CB)], axis=0)
    _, conv_back = jax.vjp(
        lambda rows, weights, offset: causal_conv(rows, weights, offset, positions),
        conv_padded, conv_taps, conv_shift,
    )
    grad_padded, grad_taps, grad_shift = conv_back(
        jnp.concatenate([grad_inputs, grad_bc], axis=1)
    )
    returned_rim = shift_teams(grad_padded[: KCONV - 1], -1)
    grad_conv = grad_padded[KCONV - 1 :]
    grad_conv = jnp.concatenate(
        [grad_conv[: tokens - (KCONV - 1)], grad_conv[tokens - (KCONV - 1) :] + returned_rim],
        axis=0,
    )
    grad_conv, early_sums = tied(grad_conv, early_sums)
    if later_levels()[:-1]:
        early_sums = scatter_step(early_sums, later_levels()[0])
    grad_conv_low = grad_conv.astype(BF16)
    grad_dt_low = grad_dt_raw.astype(BF16)

    shared = 1.0 / SHARE
    late_low = jnp.concatenate([grad_conv_low, grad_dt_low], axis=1)
    late_sums = transposed_times(ordered_normed, late_low).astype(BF16)
    late_sums, main_one = tied(late_sums, main_one)
    late_sums = scatter_step(late_sums, first_level())
    grad_bc_low = grad_conv_low[:, CX:]
    owner = jnp.arange(2 * NST) // CB
    wide_bc = jnp.where(owner == me, jnp.concatenate([grad_bc_low] * TEAM, axis=1), BF16(0.0))
    all_low = jnp.concatenate(
        [
            grad_z_low,
            grad_conv_low[:, :CX],
            wide_bc,
            grad_query_low,
            grad_key_low * BF16(shared),
            grad_value_low * BF16(shared),
            grad_dt_low,
        ],
        axis=1,
    )
    back_weights = main_one
    grad_normed_part = times_transposed(all_low, back_weights)
    grad_normed_part, late_sums, first_summed = lax.optimization_barrier(
        (grad_normed_part, late_sums, first_summed)
    )
    first_grads = hand_out(first_summed)
    if later_levels()[:-1]:
        late_sums = scatter_step(late_sums, later_levels()[0])
    gain_sums = jnp.sum(grad_normed_part * scaled_in, axis=0)
    grad_normed = team_scatter(reorder(grad_normed_part, False))
    grad_normed, late_sums = tied(grad_normed, late_sums)
    last_sums = jnp.concatenate([early_sums, late_sums], axis=1)
    for level in later_levels()[:-1][1:] + later_levels()[-1:]:
        last_sums = scatter_step(last_sums, level)
    last_grads = hand_out(last_sums)
    own_in = layer_in.astype(F32)
    inverse_one = lax.rsqrt(jnp.mean(own_in * own_in, axis=-1, keepdims=True) + EPS)
    own_scaled = own_in * inverse_one
    pulled_one = grad_normed * gain_one
    grad_in = grad_middle + inverse_one * (
        pulled_one - own_scaled * jnp.mean(pulled_one * own_scaled, axis=-1, keepdims=True)
    )

    small = jnp.concatenate(
        [
            grad_taps.reshape(-1),
            grad_shift,
            grad_log_rates,
            grad_step_bias,
            grad_skip,
            grad_gain_two,
            gain_sums,
        ]
    )
    small = reorder_rows(team_gather(sum_across_teams(small)[None]))
    gains = jnp.sum(small[:, -2 * D :], axis=0)
    small = small[:, : -2 * D]
    gain_rows = norm_gain.shape[0]
    at_gain = device_index() * gain_rows
    grad_ffn_gain = lax.dynamic_slice_in_dim(gains[:D], at_gain, gain_rows, 0)
    grad_norm_gain = lax.dynamic_slice_in_dim(gains[D:], at_gain, gain_rows, 0)
    width = CX + CB
    taps_all = small[:, : KCONV * width].reshape(TEAM, KCONV, width)
    shift_all = small[:, KCONV * width : (KCONV + 1) * width]
    rest = small[:, (KCONV + 1) * width :].reshape(TEAM, 3, HEADS)
    grad_conv_weight = jnp.concatenate(
        [
            taps_all[:, :, :CX].transpose(1, 0, 2).reshape(KCONV, DI),
            taps_all[:, :, CX:].transpose(1, 0, 2).reshape(KCONV, 2 * NST),
        ],
        axis=1,
    )
    grad_conv_bias = jnp.concatenate([shift_all[:, :CX].reshape(-1), shift_all[:, CX:].reshape(-1)])
    grad_a_log = rest[:, 0].reshape(-1)
    grad_dt_bias = rest[:, 1].reshape(-1)
    grad_d_skip = rest[:, 2].reshape(-1)

    base = 3 * CF + CX
    grad_gate, grad_up, grad_down, grad_out_proj, grad_attn_out = place(
        [first_grads],
        [
            (0, 0, CF, 0, 0),
            (0, CF, 2 * CF, 1, 0),
            (0, 2 * CF, 3 * CF, 2, 0),
            (0, 3 * CF, base, 3, 0),
            (0, base, base + CQ, 4, 0),
        ],
        [FF, FF, FF, DI, AH * HD],
        [1, 1, 1, 1, 1],
    )
    keys_at = CX + CQ
    late_at = keys_at + 2 * HD
    grad_in_proj, grad_query, grad_key, grad_value = place(
        [last_grads],
        [
            (0, 0, CX, 0, 0),
            (0, late_at, late_at + CX, 0, DI),
            (0, late_at + CX, late_at + CX + CB, 0, 2 * DI),
            (0, late_at + CX + CB, late_at + CX + CB + HEADS, 0, 2 * DI + 2 * NST),
            (0, CX, keys_at, 1, 0),
            (0, keys_at, keys_at + HD, 2, 0),
            (0, keys_at + HD, late_at, 3, 0),
        ],
        [in_proj.shape[1], AH * HD, KVH * HD, KVH * HD],
        [1, 1, SHARE, SHARE],
    )
    grad_down = grad_down.T
    grad_out_proj = grad_out_proj.T
    grad_attn_out = grad_attn_out.T
    return (
        layer_out,
        grad_in,
        grad_norm_gain,
        grad_in_proj,
        grad_query,
        grad_key,
        grad_value,
        grad_out_proj,
        grad_attn_out,
        grad_ffn_gain,
        grad_gate,
        grad_up,
        grad_down,
        grad_conv_weight,
        grad_conv_bias,
        grad_a_log,
        grad_dt_bias,
        grad_d_skip,
    )


def solution(mesh):
    rows = P("dp", None)
    columns = P(None, "dp")
    in_specs = (
        (rows, rows, P("dp"), P("dp"), rows, rows, rows, rows, columns, columns)
        + (P("dp"), rows, rows, columns)
        + (P(),) * 5
    )
    out_specs = (
        (rows, rows, P("dp"), rows, rows, rows, rows, columns, columns)
        + (P("dp"), rows, rows, columns)
        + (P(),) * 5
    )
    return jax.shard_map(body, mesh=mesh, in_specs=in_specs, out_specs=out_specs, check_vma=False)
```
